32 devices in a mesh: rep: 2 (over core), shard: 16 (over z, y, x).
Axes of the slice: x: 2, y: 2, z: 4, core: 2. Of those that a mesh axis runs over, the one named last changes fastest.
Arguments:
- content_in: bfloat16 [4, 2048, 768], P('rep', 'shard'), may hold values from -6 to 6
- query_in: bfloat16 [4, 2048, 768], P('rep', 'shard'), may hold values from -6 to 6
- segment_ids: int32 [4, 2048], P('rep', 'shard'), may hold values from 0 to 12, never falling along the last dimension, each value on 1 to 512 neighbouring positions
- parent_ids: int32 [4, 13], P('rep'), may hold values from 0 to 11, as said below
- rank_order: int32 [4, 2048], P('rep', 'shard'), may hold values from 0 to 2047, as said below
- query_flags: int32 [4, 2048], P('rep', 'shard'), may hold values from 0 to 1, as said below
- query_weight: bfloat16 [768, 768], P('shard'), may hold values from -0.21875 to 0.21875
- key_weight: bfloat16 [768, 768], P('shard'), may hold values from -0.21875 to 0.21875
- value_weight: bfloat16 [768, 768], P('shard'), may hold values from -0.21875 to 0.21875
- relative_weight: bfloat16 [768, 768], P('shard'), may hold values from -0.21875 to 0.21875
- output_weight: bfloat16 [768, 768], P('shard'), may hold values from -3 to 3
- inner_weight: bfloat16 [768, 3072], P('shard'), may hold values from -0.21875 to 0.21875
- outer_weight: bfloat16 [3072, 768], P('shard'), may hold values from -0.109375 to 0.109375
- inner_bias: bfloat16 [3072], P('shard'), may hold values from -3 to 3
- outer_bias: bfloat16 [768], P('shard'), may hold values from -2 to 2
- attend_gain: bfloat16 [768], P('shard'), may hold values from 0.5 to 1.5
- attend_shift: bfloat16 [768], P('shard'), may hold values from -2 to 2
- feed_gain: bfloat16 [768], P('shard'), may hold values from 0.5 to 1.5
- feed_shift: bfloat16 [768], P('shard'), may hold values from -2 to 2
- content_bias: bfloat16 [768], P('shard'), may hold values from -3 to 3
- position_bias: bfloat16 [768], P('shard'), may hold values from -3 to 3
- segment_bias: bfloat16 [768], P('shard'), may hold values from -3 to 3
- segment_table: bfloat16 [2, 768], P(None, 'shard'), may hold values from -3 to 3
- content_cot: bfloat16 [4, 2048, 768], P('rep', 'shard'), may hold values from -6 to 6
- query_cot: bfloat16 [4, 2048, 768], P('rep', 'shard'), may hold values from -6 to 6
Outputs:
- content_out: bfloat16 [4, 2048, 768], P('rep', 'shard')
- query_out: bfloat16 [4, 2048, 768], P('rep', 'shard')
- content_grad: bfloat16 [4, 2048, 768], P('rep', 'shard')
- query_grad: bfloat16 [4, 2048, 768], P('rep', 'shard')
- query_weight_grad: float32 [768, 768], P('shard')
- key_weight_grad: float32 [768, 768], P('shard')
- value_weight_grad: float32 [768, 768], P('shard')
- relative_weight_grad: float32 [768, 768], P('shard')
- output_weight_grad: float32 [768, 768], P('shard')
- inner_weight_grad: float32 [768, 3072], P('shard')
- outer_weight_grad: float32 [3072, 768], P('shard')
- inner_bias_grad: float32 [3072], P('shard')
- outer_bias_grad: float32 [768], P('shard')
- attend_gain_grad: float32 [768], P('shard')
- attend_shift_grad: float32 [768], P('shard')
- feed_gain_grad: float32 [768], P('shard')
- feed_shift_grad: float32 [768], P('shard')
- content_bias_grad: float32 [768], P('shard')
- position_bias_grad: float32 [768], P('shard')
- segment_bias_grad: float32 [768], P('shard')
- segment_table_grad: float32 [2, 768], P(None, 'shard')
The draws below stay inside these ranges and needn't reach their ends.
Inputs may be any that keep to these rules, and one draw needn't show every extreme that they name: `parent_ids`: segment 0 of a tree is its own parent; every other segment's parent is a segment of smaller number; the last segment's parent is the segment before it. `rank_order`: the ranks of one tree are a permutation of 0 to 2047, with rank 0 at position 0. `query_flags`: position 0 of each tree has flag 0.
All inputs are finite; a program needn't handle non-finite values.
Results may differ from the reference program's by a relative error of at most 0.03.
Values may be sent and summed in bfloat16 or wider, within the bound.
No kernel may reach another device: no remote copies, remote signals or barrier semaphores. Data moves between devices by JAX's collectives and lax.ppermute only.
A program may use at most 320 MiB of HBM per device.

```python
import math
import jax
import jax.numpy as jnp
import numpy as np
from jax import lax

D = 768
H = 12
DH = 64
FF = 3072
NS = 13
L = 2048
TREES = 4


def draw_parent_ids(key, part):
    key = jax.random.fold_in(key, 11)
    limits = jnp.arange(NS, dtype=jnp.int32)
    random_ints = jax.random.randint(key, (TREES, NS), 0, 1 << 20)
    parents = random_ints % jnp.maximum(limits, 1)[None, :]
    parents = parents.at[:, NS - 1].set(NS - 2)
    return parents.astype(jnp.int32)


def draw_rank_order(key, part):
    key = jax.random.fold_in(key, 12)
    tree_keys = jax.random.split(key, TREES)

    def one_tree(subkey):
        ranking = jax.random.permutation(subkey, L).astype(jnp.int32)
        zero_place = jnp.argmin(ranking)
        first_rank = ranking[0]
        ranking = jnp.where(jnp.arange(L, dtype=jnp.int32) == zero_place, first_rank, ranking)
        return ranking.at[0].set(0)
    return jax.vmap(one_tree)(tree_keys).astype(jnp.int32)


def draw_query_flags(key, part):
    key = jax.random.fold_in(key, 13)
    random_ints = jax.random.randint(key, (TREES, L), 0, 3)
    flag_bits = (random_ints == 0).astype(jnp.int32)
    return flag_bits.at[:, 0].set(0)


def block_scale(rng, shape, shards, smallest, top_value):
    factor_of = 1.0
    for dim, parts in shards:
        steps = jax.random.uniform(jax.random.fold_in(jax.random.fold_in(rng, 6), dim), (parts,), jnp.float32, smallest / len(shards), top_value / len(shards))
        factor_of = factor_of * jnp.repeat(jnp.exp(steps), shape[dim] // parts).reshape((-1,) + (1,) * (len(shape) - 1 - dim))
    return factor_of


def profile(number_of, total, bound, lean):
    weights = [(1 << 20) // math.isqrt(grade ** lean) + 1 for grade in range(2, number_of + 1)]
    surplus, given = total - bound - (number_of - 1), [1] * (number_of - 1)
    while surplus > 0:
        movable = [i for i in range(number_of - 1) if given[i] < bound]
        pool, remaining = sum([weights[i] for i in movable]), surplus
        for i in movable:
            addition = min(bound - given[i], max(1, remaining * weights[i] // pool), surplus)
            given[i] = given[i] + addition
            surplus = surplus - addition
    return np.array([bound] + given)


def uneven_parts(stream_key, amount, total, most, lean):
    if amount == 2:
        one = jax.random.randint(stream_key, (), max(1, total - most), min(most, total - 1) + 1)
        return jnp.stack([one, total - one])
    lengths = jnp.asarray(profile(amount, total, most, lean), jnp.int32)
    twos = (amount - 1) // 2
    source_of, receiver = lengths[1:1 + 2 * twos:2], lengths[2:2 + 2 * twos:2]
    room = jnp.minimum(source_of - 1, most - receiver)
    moved = jax.random.randint(jax.random.fold_in(stream_key, 1), (twos,), 0, 1 << 20) % (room + 1)
    lengths = lengths.at[1:1 + 2 * twos:2].set(source_of - moved).at[2:2 + 2 * twos:2].set(receiver + moved)
    return lengths[jax.random.permutation(jax.random.fold_in(stream_key, 2), amount)]


def bell_draw(key, dims, scale, limit, shards=(), kind=jnp.bfloat16):
    values = scale * jax.random.normal(key, dims, jnp.float32)
    if shards:
        values = values * block_scale(key, dims, shards, -0.22, 0.18)
    return jnp.clip(values, -limit, limit).astype(kind)


def setup_inputs(seed: int = 0) -> dict:
    seeds = jax.random.split(jax.random.key(seed), 26)
    content_in = bell_draw(seeds[0], (TREES, L, D), 1.0, 6.0, ((0, 2), (1, 16)))
    query_in = bell_draw(seeds[1], (TREES, L, D), 1.0, 6.0, ((0, 2), (1, 16)))
    segment_ids = jax.vmap(lambda own: jnp.searchsorted(jnp.cumsum(uneven_parts(own, NS, L, L // 4, 0)), jnp.arange(L), side="right"))(jax.random.split(seeds[2], TREES)).reshape((TREES, L)).astype(jnp.int32)
    parent_ids = draw_parent_ids(jax.random.fold_in(seeds[25], 71), 0)
    rank_order = draw_rank_order(jax.random.fold_in(seeds[25], 71), 0)
    query_flags = draw_query_flags(jax.random.fold_in(seeds[25], 71), 0)
    query_weight = bell_draw(seeds[6], (D, D), D ** -0.5, 0.21875, ((0, 16),))
    key_weight = bell_draw(seeds[7], (D, D), D ** -0.5, 0.21875, ((0, 16),))
    value_weight = bell_draw(seeds[8], (D, D), D ** -0.5, 0.21875, ((0, 16),))
    relative_weight = bell_draw(seeds[9], (D, D), D ** -0.5, 0.21875, ((0, 16),))
    output_weight = bell_draw(seeds[10], (D, D), 4 ** -0.5, 3.0, ((0, 16),))
    inner_weight = bell_draw(seeds[11], (D, FF), D ** -0.5, 0.21875, ((0, 16),))
    outer_weight = bell_draw(seeds[12], (FF, D), FF ** -0.5, 0.109375, ((0, 16),))
    inner_bias = bell_draw(seeds[13], (FF,), 0.5, 3.0, ((0, 16),))
    outer_bias = bell_draw(seeds[14], (D,), 0.3, 2.0, ((0, 16),))
    attend_gain = jnp.clip(1.0 + 0.1 * jax.random.normal(seeds[15], (D,), jnp.float32), 0.5, 1.5).astype(jnp.bfloat16)
    attend_shift = bell_draw(seeds[16], (D,), 0.3, 2.0, ((0, 16),))
    feed_gain = jnp.clip(1.0 + 0.1 * jax.random.normal(seeds[17], (D,), jnp.float32), 0.5, 1.5).astype(jnp.bfloat16)
    feed_shift = bell_draw(seeds[18], (D,), 0.3, 2.0, ((0, 16),))
    content_bias = bell_draw(seeds[19], (D,), 0.5, 3.0, ((0, 16),))
    position_bias = bell_draw(seeds[20], (D,), 0.5, 3.0, ((0, 16),))
    segment_bias = bell_draw(seeds[21], (D,), 0.5, 3.0, ((0, 16),))
    segment_table = bell_draw(seeds[22], (2, D), 0.5, 3.0, ((1, 16),))
    content_cot = bell_draw(seeds[23], (TREES, L, D), 1.0, 6.0, ((0, 2), (1, 16)))
    query_cot = bell_draw(seeds[24], (TREES, L, D), 1.0, 6.0, ((0, 2), (1, 16)))
    return {"content_in": content_in, "query_in": query_in, "segment_ids": segment_ids, "parent_ids": parent_ids, "rank_order": rank_order, "query_flags": query_flags, "query_weight": query_weight, "key_weight": key_weight, "value_weight": value_weight, "relative_weight": relative_weight, "output_weight": output_weight, "inner_weight": inner_weight, "outer_weight": outer_weight, "inner_bias": inner_bias, "outer_bias": outer_bias, "attend_gain": attend_gain, "attend_shift": attend_shift, "feed_gain": feed_gain, "feed_shift": feed_shift, "content_bias": content_bias, "position_bias": position_bias, "segment_bias": segment_bias, "segment_table": segment_table, "content_cot": content_cot, "query_cot": query_cot}


EPSILON = 1e-05
MASKED = -1e+30

@jax.custom_vjp
def low(v):
    return lax.optimization_barrier(v.astype(jnp.bfloat16)).astype(jnp.float32)

@jax.custom_vjp
def low_back(v):
    return v

def low_keep(v):
    return (low(v), None)

def low_pass(kept, grad):
    return (grad,)

def back_keep(v):
    return (v, None)

def back_low(kept, grad):
    return (low(grad),)
low.defvjp(low_keep, low_pass)
low_back.defvjp(back_keep, back_low)

def round_both(tensor):
    return low(low_back(tensor))

def exact_dot(former, latter):
    return jnp.dot(former, latter, precision=lax.Precision.HIGHEST)

def layer_norm(vector, gain_row, shift_row):
    average = lax.optimization_barrier(jnp.mean(vector, axis=-1, keepdims=True))
    centred = vector - average
    variance = lax.optimization_barrier(jnp.mean(centred * centred, axis=-1, keepdims=True))
    return centred * lax.rsqrt(variance + EPSILON) * gain_row + shift_row

def position_rows(offsets, model_width):
    half_width = model_width // 2
    powers = jnp.arange(half_width, dtype=jnp.float32) * (2.0 / model_width)
    inverse_freq = 1.0 / 10000.0 ** powers
    angles = offsets[:, None] * inverse_freq[None, :]
    return jnp.concatenate([jnp.sin(angles), jnp.cos(angles)], axis=1)

def skew_rows(full_table, row_count, key_count):
    leading = full_table.shape[0]
    window = row_count + key_count - 1
    flattened = full_table.reshape(leading, row_count * window)
    flattened = lax.slice_in_dim(flattened, row_count - 1, row_count - 1 + row_count * (window - 1), axis=1)
    return flattened.reshape(leading, row_count, window - 1)[:, :, :key_count]

def ancestry(parents):
    segment_count = parents.shape[0]
    labels = jnp.arange(segment_count, dtype=jnp.int32)
    parent_step = (parents[:, None] == labels[None, :]).astype(jnp.float32)
    reached = jnp.eye(segment_count, dtype=jnp.float32)
    current = reached
    for repeat in range(segment_count - 1):
        current = exact_dot(current, parent_step)
        reached = jnp.maximum(reached, current)
    return reached

def tree_forward(params, content, query, segments, ranks, flag_bits, parents):
    query_weight, key_weight, value_weight, relative_weight, output_weight, inner_weight, outer_weight, inner_bias, outer_bias, attend_gain, attend_shift, feed_gain, feed_shift, content_bias, position_bias, segment_bias, segment_table = params
    length = content.shape[0]
    model_width = content.shape[1]
    query_block = math.gcd(length, 512)
    block_count = length // query_block
    score_scale = DH ** (-0.5)
    stacked = jnp.stack([content, query]).reshape(2 * length, model_width)
    queries = low_back(exact_dot(stacked, query_weight)).reshape(2, length, H, DH)
    keys = round_both(exact_dot(content, key_weight)).reshape(length, H, DH)
    values = round_both(exact_dot(content, value_weight)).reshape(length, H, DH)
    offsets = (length - 1 - jnp.arange(2 * length, dtype=jnp.int32)).astype(jnp.float32)
    rel_keys = low(exact_dot(low(position_rows(offsets, model_width)), relative_weight))
    query_plain = low(queries + content_bias.reshape(H, DH))
    query_place = low(queries + position_bias.reshape(H, DH))
    query_label = queries + segment_bias.reshape(H, DH)
    label_terms = jnp.einsum('sqhd,thd->sthq', query_label, segment_table.reshape(2, H, DH), precision=lax.Precision.HIGHEST)
    reached = ancestry(parents)
    label_hot = (segments[:, None] == jnp.arange(NS, dtype=jnp.int32)[None, :]).astype(jnp.float32)
    path_rows = exact_dot(label_hot, reached)
    limits = jnp.stack([ranks, ranks - flag_bits])

    def one_block(block_index):
        start = (block_index * query_block).astype(jnp.int32)
        plain_rows = lax.dynamic_slice_in_dim(query_plain, start, query_block, 1)
        place_rows = lax.dynamic_slice_in_dim(query_place, start, query_block, 1)
        label_rows = lax.dynamic_slice_in_dim(label_terms, start, query_block, 3)
        path_part = lax.dynamic_slice_in_dim(path_rows, start, query_block, 0)
        segment_rows = lax.dynamic_slice_in_dim(segments, start, query_block, 0)
        limit_rows = lax.dynamic_slice_in_dim(limits, start, query_block, 1)
        content_part = jnp.einsum('sqhd,khd->shqk', plain_rows, keys, precision=lax.Precision.HIGHEST)
        place_window = lax.dynamic_slice_in_dim(rel_keys, length - start - query_block, query_block + length - 1, 0).reshape(-1, H, DH)
        full_part = jnp.einsum('sqhd,chd->shqc', place_rows, place_window, precision=lax.Precision.HIGHEST)
        shifted = skew_rows(full_part.reshape(2 * H, query_block, query_block + length - 1), query_block, length).reshape(2, H, query_block, length)
        same_label = segment_rows[:, None] == segments[None, :]
        label_part = jnp.where(same_label[None, None], label_rows[:, 0][..., None], label_rows[:, 1][..., None])
        scores = low_back((content_part + shifted + label_part) * score_scale)
        on_path = exact_dot(path_part, label_hot.T) > 0.5
        allowed = on_path[None] & (ranks[None, None, :] <= limit_rows[:, :, None])
        scores = jnp.where(allowed[:, None], scores, MASKED)
        maxima = lax.optimization_barrier(jnp.max(scores, axis=-1, keepdims=True))
        scaled_exp = jnp.exp(scores - maxima)
        attention = scaled_exp / lax.optimization_barrier(jnp.sum(scaled_exp, axis=-1, keepdims=True))
        return jnp.einsum('shqk,khd->sqhd', low(attention), values, precision=lax.Precision.HIGHEST)
    blocks = lax.map(jax.checkpoint(one_block), jnp.arange(block_count, dtype=jnp.int32))
    mixed = round_both(blocks.transpose(1, 0, 2, 3, 4).reshape(2 * length, model_width))
    attended = low_back(exact_dot(mixed, output_weight))
    residual = attended + stacked
    normed = layer_norm(residual, attend_gain, attend_shift)
    inner_pre = low_back(exact_dot(low(normed), inner_weight)) + inner_bias
    hidden = low(jax.nn.gelu(inner_pre, approximate=True))
    summed = low_back(exact_dot(hidden, outer_weight)) + outer_bias + normed
    return layer_norm(summed, feed_gain, feed_shift).reshape(2, length, model_width)

def reference(content_in, query_in, segment_ids, parent_ids, rank_order, query_flags, query_weight, key_weight, value_weight, relative_weight, output_weight, inner_weight, outer_weight, inner_bias, outer_bias, attend_gain, attend_shift, feed_gain, feed_shift, content_bias, position_bias, segment_bias, segment_table, content_cot, query_cot):
    params = tuple((weight.astype(jnp.float32) for weight in (query_weight, key_weight, value_weight, relative_weight, output_weight, inner_weight, outer_weight, inner_bias, outer_bias, attend_gain, attend_shift, feed_gain, feed_shift, content_bias, position_bias, segment_bias, segment_table)))

    def forward(params, content, query):
        results = [tree_forward(params, content[tree_index], query[tree_index], segment_ids[tree_index], rank_order[tree_index], query_flags[tree_index], parent_ids[tree_index]) for tree_index in range(content.shape[0])]
        stacked = jnp.stack(results)
        return (stacked[:, 0], stacked[:, 1])
    outputs, backward = jax.vjp(forward, params, content_in.astype(jnp.float32), query_in.astype(jnp.float32))
    gradients, content_grad, query_grad = backward((content_cot.astype(jnp.float32), query_cot.astype(jnp.float32)))
    return (outputs[0].astype(jnp.bfloat16), outputs[1].astype(jnp.bfloat16), content_grad.astype(jnp.bfloat16), query_grad.astype(jnp.bfloat16), gradients[0], gradients[1], gradients[2], gradients[3], gradients[4], gradients[5], gradients[6], gradients[7], gradients[8], gradients[9], gradients[10], gradients[11], gradients[12], gradients[13], gradients[14], gradients[15], gradients[16])
```

```python
import functools

import jax
import jax.numpy as jnp
from jax import lax
from jax.experimental import pallas as pl
from jax.experimental.pallas import tpu as pltpu
from jax.sharding import PartitionSpec as P

DH = 64
NS = 13
EPSILON = 1e-05
NEG = -1e30
F32 = jnp.float32
BF = jnp.bfloat16
HIGHEST = lax.Precision.HIGHEST

R = 128
KB = 256
W = R + KB
SCALE = DH**-0.5
LOG2E = 1.4426950408889634
LN2 = 0.6931471805599453
ONES = 32


def mm(a, b, ca=1, cb=0, precision=None):
    return lax.dot_general(
        a, b, (((ca,), (cb,)), ((), ())), preferred_element_type=F32, precision=precision
    )


def row_features(seg_col):
    lane = lax.broadcasted_iota(jnp.int32, (2 * R, 128), 1)
    folded = jnp.where(lane < NS, lane, lane - NS).astype(F32)
    return jnp.where((lane < 2 * NS) & (folded == seg_col), 1.0, 0.0)


def live_list(live_ref, list_ref, block, nkb):
    def step(kb, count):
        list_ref[count] = kb
        return count + live_ref[block * nkb + kb]

    return lax.fori_loop(0, nkb, step, 0)


def forward_kernel(
    nkb,
    base_ref,
    live_ref,
    q_ref,
    vec_ref,
    table_ref,
    info_ref,
    reach_ref,
    kv_ref,
    hot_ref,
    rel_ref,
    rank_ref,
    p_ref,
    o_ref,
    inv_ref,
    qq_scr,
    qr_scr,
    s_scr,
    m_scr,
    acc_scr,
    list_scr,
):
    block = pl.program_id(0)
    base = base_ref[block]
    count = live_list(live_ref, list_scr, block, nkb)
    seg_col = info_ref[:, 0:1]
    limit = info_ref[:, 1:2]
    hot_row = row_features(seg_col)
    lane = lax.broadcasted_iota(jnp.int32, (2 * R, 128), 1)
    reach = mm(jnp.where(lane < NS, hot_row, 0.0).astype(BF), reach_ref[...])
    outside = jnp.where((lane < 2 * NS) & (reach < 0.5), NEG, 0.0)
    zero = jnp.zeros((2 * R, DH), BF)
    for h in range(2):
        half = slice(DH * h, DH * h + DH)
        q = q_ref[:, half]
        plain = ((q + vec_ref[0:1, half]) * (SCALE * LOG2E)).astype(BF)
        place = ((q + vec_ref[1:2, half]) * (SCALE * LOG2E)).astype(BF)
        label = q + vec_ref[2:3, half]
        same = mm(label, table_ref[h, 0], precision=HIGHEST)
        other = mm(label, table_ref[h, 1], precision=HIGHEST)
        term = jnp.where(hot_row > 0.5, same, other) * (SCALE * LOG2E) + outside
        high = term.astype(BF).astype(F32)
        extra = jnp.where(lane < NS, high, jnp.where(lane < 2 * NS, term - high, 0.0))
        qq_scr[h] = jnp.concatenate([plain, zero, extra.astype(BF)], axis=1)
        qr_scr[h] = jnp.concatenate([place, zero] if h == 0 else [zero, place], axis=1)
    m_scr[...] = jnp.full(m_scr.shape, -jnp.inf, F32)
    acc_scr[...] = jnp.zeros(acc_scr.shape, F32)

    def score(n, carry):
        k0 = pl.multiple_of(list_scr[n] * KB, KB)
        ok = rank_ref[:, pl.ds(k0, KB)] <= limit
        window = rel_ref[pl.ds(pl.multiple_of(base + k0, 128), W), :]
        hot = hot_ref[pl.ds(k0, KB), :]
        for h in range(2):
            keys = jnp.concatenate([kv_ref[pl.ds(k0, KB), 128 * h : 128 * h + 128], hot], axis=1)
            s = mm(qq_scr[h], keys, 1, 1)
            full = mm(qr_scr[h], window, 1, 1)
            shifted = [
                pltpu.roll(full[i * R : i * R + R], W - (R - 1), 1, stride=1, stride_axis=0)[
                    :, :KB
                ]
                for i in range(2)
            ]
            s = jnp.where(ok, s + jnp.concatenate(shifted, axis=0), NEG)
            s_scr[h, n] = s
            m_scr[h] = jnp.maximum(m_scr[h], jnp.maximum(s[:, :128], s[:, 128:]))
        return carry

    lax.fori_loop(0, count, score, 0)
    top = [jnp.max(m_scr[h], axis=1, keepdims=True) for h in range(2)]

    def mix(n, carry):
        k0 = pl.multiple_of(list_scr[n] * KB, KB)
        hot = hot_ref[pl.ds(k0, KB), :]
        for h in range(2):
            p = jnp.exp2(s_scr[h, n] - top[h]).astype(BF)
            p_ref[0, 0, h, n] = p
            keys = jnp.concatenate([kv_ref[pl.ds(k0, KB), 128 * h : 128 * h + 128], hot], axis=1)
            acc_scr[h] += mm(p, keys)
        return carry

    lax.fori_loop(0, count, mix, 0)
    for h in range(2):
        half = slice(DH * h, DH * h + DH)
        acc = acc_scr[h]
        inverse = 1.0 / acc[:, 128 + ONES : 129 + ONES]
        o_ref[:, half] = acc[:, DH : 2 * DH] * inverse
        inv_ref[:, half] = jnp.broadcast_to(inverse, (2 * R, DH))


def attend_forward(base, live, q, vec, table, info, reach, kv, hot, rel, rank):
    nb = q.shape[0] // (2 * R)
    pairs = q.shape[1] // 128
    length = kv.shape[0]
    nkb = length // KB
    rows = lambda width: pl.BlockSpec((2 * R, width), lambda b, p, *_: (b, p))
    whole = lambda *shape: pl.BlockSpec(shape, lambda b, p, *_: (0,) * len(shape))
    return pl.pallas_call(
        functools.partial(forward_kernel, nkb),
        grid_spec=pltpu.PrefetchScalarGridSpec(
            num_scalar_prefetch=2,
            grid=(nb, pairs),
            in_specs=[
                rows(128),
                pl.BlockSpec((8, 128), lambda b, p, *_: (0, p)),
                pl.BlockSpec((2, 2, DH, 128), lambda b, p, *_: (p, 0, 0, 0)),
                pl.BlockSpec((2 * R, 2), lambda b, p, *_: (b, 0)),
                whole(128, 128),
                pl.BlockSpec((length, 256), lambda b, p, *_: (0, p)),
                whole(length, 128),
                pl.BlockSpec((2 * length, 128), lambda b, p, *_: (0, p)),
                whole(1, length),
            ],
            out_specs=[
                pl.BlockSpec((1, 1, 2, nkb, 2 * R, KB), lambda b, p, *_: (b, p, 0, 0, 0, 0)),
                rows(128),
                rows(128),
            ],
            scratch_shapes=[
                pltpu.VMEM((2, 2 * R, 256), BF),
                pltpu.VMEM((2, 2 * R, 128), BF),
                pltpu.VMEM((2, nkb, 2 * R, KB), F32),
                pltpu.VMEM((2, 2 * R, 128), F32),
                pltpu.VMEM((2, 2 * R, 256), F32),
                pltpu.SMEM((nkb + 1,), jnp.int32),
            ],
        ),
        out_shape=[
            jax.ShapeDtypeStruct((nb, pairs, 2, nkb, 2 * R, KB), BF),
            jax.ShapeDtypeStruct(q.shape, F32),
            jax.ShapeDtypeStruct(q.shape, F32),
        ],
        compiler_params=pltpu.CompilerParams(
            dimension_semantics=("arbitrary", "arbitrary"), vmem_limit_bytes=58 * 2**20
        ),
        cost_estimate=pl.CostEstimate(
            flops=nb * pairs * nkb * 2 * 2 * 2 * R * KB * 700,
            bytes_accessed=nb * pairs * nkb * 2 * 2 * 2 * R * KB,
            transcendentals=nb * pairs * nkb * 2 * 2 * R * KB,
        ),
        name="attend_forward",
    )(base, live, q, vec, table, info, reach, kv, hot, rel, rank)


def backward_kernel(
    nkb,
    nb,
    base_ref,
    live_ref,
    p_ref,
    q_ref,
    g_ref,
    o_ref,
    inv_ref,
    vec_ref,
    info_ref,
    kv_ref,
    hot_ref,
    rel_ref,
    dq_ref,
    dkv_ref,
    drel_ref,
    small_ref,
    qq_scr,
    qr_scr,
    dd_scr,
    acc_scr,
    accr_scr,
    dkv_scr,
    drel_scr,
    flip_scr,
    list_scr,
):
    block = pl.program_id(1)
    length = nkb * KB
    base = base_ref[block]
    count = live_list(live_ref, list_scr, block, nkb)

    @pl.when(block == 0)
    def start():
        dkv_scr[...] = jnp.zeros(dkv_scr.shape, F32)
        drel_scr[...] = jnp.zeros(drel_scr.shape, F32)
        small_ref[...] = jnp.zeros(small_ref.shape, F32)
        down = lax.broadcasted_iota(jnp.int32, (KB, KB), 0)
        across = lax.broadcasted_iota(jnp.int32, (KB, KB), 1)
        flip_scr[...] = jnp.where(down + across == KB - 1, 1.0, 0.0).astype(BF)

    lane = lax.broadcasted_iota(jnp.int32, (2 * R, 128), 1)
    zero = jnp.zeros((2 * R, DH), BF)
    for h in range(2):
        half = slice(DH * h, DH * h + DH)
        q = q_ref[:, half]
        plain = ((q + vec_ref[0:1, half]) * (SCALE * LOG2E)).astype(BF)
        place = ((q + vec_ref[1:2, half]) * (SCALE * LOG2E)).astype(BF)
        g = g_ref[:, half].astype(F32)
        inverse = inv_ref[:, DH * h : DH * h + 1]
        delta = -jnp.sum(g * o_ref[:, half], axis=1, keepdims=True) * inverse
        high = delta.astype(BF).astype(F32)
        extra = jnp.where(lane == ONES, high, jnp.where(lane == ONES + 1, delta - high, 0.0))
        qq_scr[h] = jnp.concatenate([plain, zero], axis=1)
        qr_scr[h] = jnp.concatenate([place, zero] if h == 0 else [zero, place], axis=1)
        dd_scr[h] = jnp.concatenate([zero, (g * inverse).astype(BF), extra.astype(BF)], axis=1)
    acc_scr[...] = jnp.zeros(acc_scr.shape, F32)
    accr_scr[...] = jnp.zeros(accr_scr.shape, F32)

    def step(n, carry):
        k0 = pl.multiple_of(list_scr[n] * KB, KB)
        r0 = pl.multiple_of(2 * length - base - k0 - W, 128)
        hot = hot_ref[pl.ds(k0, KB), :]
        window = rel_ref[pl.ds(r0, W), :]
        pad = jnp.zeros((R, W - KB), F32)
        for h in range(2):
            lanes = slice(128 * h, 128 * h + 128)
            p = p_ref[0, 0, h, n]
            keys = jnp.concatenate([kv_ref[pl.ds(k0, KB), lanes], hot], axis=1)
            dd = dd_scr[h]
            ds = (p.astype(F32) * mm(dd, keys, 1, 1)).astype(BF)
            acc_scr[h] += mm(ds, keys)
            turned = mm(ds, flip_scr[...])
            full = [
                pltpu.roll(
                    jnp.concatenate([turned[i * R : i * R + R], pad], axis=1),
                    0,
                    1,
                    stride=1,
                    stride_axis=0,
                )
                for i in range(2)
            ]
            full = jnp.concatenate(full, axis=0).astype(BF)
            accr_scr[h] += mm(full, window)
            drel_scr[pl.ds(r0, W), :] += mm(full, qr_scr[h], 0, 0)
            dkv_scr[pl.ds(k0, KB), lanes] += mm(ds, qq_scr[h], 0, 0) + mm(p, dd[:, :128], 0, 0)
        return carry

    lax.fori_loop(0, count, step, 0)
    hot_row = row_features(info_ref[:, 0:1])
    for h in range(2):
        half = slice(DH * h, DH * h + DH)
        acc = acc_scr[h]
        d_plain = acc[:, :DH] * SCALE
        d_place = accr_scr[h][:, half] * SCALE
        sums = jnp.where(lane < NS, acc[:, 128:], 0.0) * SCALE
        same = jnp.sum(sums * hot_row, axis=1, keepdims=True)
        other = jnp.sum(sums, axis=1, keepdims=True) - same
        d_label = same * vec_ref[3:4, half] + other * vec_ref[4:5, half]
        label = q_ref[:, half] + vec_ref[2:3, half]
        dq_ref[:, half] = (d_plain + d_place + d_label).astype(BF)
        terms = [d_plain, d_place, d_label, same * label, other * label]
        for row, term in enumerate(terms):
            small_ref[row : row + 1, half] += jnp.sum(term, axis=0, keepdims=True)

    @pl.when(block == nb - 1)
    def finish():
        across = lax.broadcasted_iota(jnp.int32, (length, 256), 1)
        factor = jnp.where((across % 128) < DH, LN2, 1.0)
        dkv_ref[...] = (dkv_scr[...] * factor).astype(BF)
        drel_ref[...] = (drel_scr[...] * LN2).astype(BF)


def attend_backward(base, live, p, q, g, o, inv, vec, info, kv, hot, rel):
    nb = q.shape[0] // (2 * R)
    pairs = q.shape[1] // 128
    length = kv.shape[0]
    nkb = length // KB
    rows = lambda width: pl.BlockSpec((2 * R, width), lambda p, b, *_: (b, p))
    return pl.pallas_call(
        functools.partial(backward_kernel, nkb, nb),
        grid_spec=pltpu.PrefetchScalarGridSpec(
            num_scalar_prefetch=2,
            grid=(pairs, nb),
            in_specs=[
                pl.BlockSpec((1, 1, 2, nkb, 2 * R, KB), lambda p, b, *_: (b, p, 0, 0, 0, 0)),
                rows(128),
                rows(128),
                rows(128),
                rows(128),
                pl.BlockSpec((8, 128), lambda p, b, *_: (0, p)),
                pl.BlockSpec((2 * R, 2), lambda p, b, *_: (b, 0)),
                pl.BlockSpec((length, 256), lambda p, b, *_: (0, p)),
                pl.BlockSpec((length, 128), lambda p, b, *_: (0, 0)),
                pl.BlockSpec((2 * length, 128), lambda p, b, *_: (0, p)),
            ],
            out_specs=[
                rows(128),
                pl.BlockSpec((length, 256), lambda p, b, *_: (0, p)),
                pl.BlockSpec((2 * length, 128), lambda p, b, *_: (0, p)),
                pl.BlockSpec((8, 128), lambda p, b, *_: (0, p)),
            ],
            scratch_shapes=[
                pltpu.VMEM((2, 2 * R, 128), BF),
                pltpu.VMEM((2, 2 * R, 128), BF),
                pltpu.VMEM((2, 2 * R, 256), BF),
                pltpu.VMEM((2, 2 * R, 256), F32),
                pltpu.VMEM((2, 2 * R, 128), F32),
                pltpu.VMEM((length, 256), F32),
                pltpu.VMEM((2 * length, 128), F32),
                pltpu.VMEM((KB, KB), BF),
                pltpu.SMEM((nkb + 1,), jnp.int32),
            ],
        ),
        out_shape=[
            jax.ShapeDtypeStruct(q.shape, BF),
            jax.ShapeDtypeStruct(kv.shape, BF),
            jax.ShapeDtypeStruct((2 * length, q.shape[1]), BF),
            jax.ShapeDtypeStruct((8, q.shape[1]), F32),
        ],
        compiler_params=pltpu.CompilerParams(
            dimension_semantics=("arbitrary", "arbitrary"), vmem_limit_bytes=58 * 2**20
        ),
        cost_estimate=pl.CostEstimate(
            flops=nb * pairs * nkb * 2 * 2 * 2 * R * KB * 1400,
            bytes_accessed=nb * pairs * nkb * 2 * 2 * 2 * R * KB,
            transcendentals=0,
        ),
        name="attend_backward",
    )(base, live, p, q, g, o, inv, vec, info, kv, hot, rel)


def layer_norm(vector, gain_row, shift_row):
    average = jnp.mean(vector, axis=-1, keepdims=True)
    centred = vector - average
    variance = jnp.mean(centred * centred, axis=-1, keepdims=True)
    return centred * lax.rsqrt(variance + EPSILON) * gain_row + shift_row


def gelu_tanh(vector):
    return jax.nn.gelu(vector, approximate=True)


def position_rows(offsets, model_width):
    half_width = model_width // 2
    powers = jnp.arange(half_width, dtype=F32) * (2.0 / model_width)
    inverse_freq = 1.0 / 10000.0**powers
    angles = offsets[:, None] * inverse_freq[None, :]
    return jnp.concatenate([jnp.sin(angles), jnp.cos(angles)], axis=1)


def body(
    content_in,
    query_in,
    segment_ids,
    parent_ids,
    rank_order,
    query_flags,
    query_weight,
    key_weight,
    value_weight,
    relative_weight,
    output_weight,
    inner_weight,
    outer_weight,
    inner_bias,
    outer_bias,
    attend_gain,
    attend_shift,
    feed_gain,
    feed_shift,
    content_bias,
    position_bias,
    segment_bias,
    segment_table,
    content_cot,
    query_cot,
):
    n = lax.axis_size("shard")
    nr = lax.axis_size("rep")
    trees, r, d = content_in.shape
    groups = 2 * trees
    m = n // groups
    length = r * n
    nkb = length // KB
    rh = r // 2
    ff = inner_weight.shape[1]
    dh = d // 2
    fh = ff // 2
    heads = dh // DH
    ws = query_weight.shape[0]
    fs = outer_weight.shape[0]
    me = lax.axis_index("shard")
    g, c = me // m, me % m
    k = lax.axis_index("rep") % 2
    first = k == 0

    def swap(x):
        return lax.ppermute(x, "rep", [(i, i ^ 1) for i in range(nr)])

    def far(x, step):
        return lax.ppermute(x, "shard", [(i, i ^ (m * step)) for i in range(n)])

    def near(x, step):
        return lax.ppermute(x, "shard", [(i, i ^ step) for i in range(n)])

    def pick(x, index, axis=0):
        return lax.dynamic_index_in_dim(x, index, axis, keepdims=False)

    def put(buffer, x, index, axis=0):
        return lax.dynamic_update_index_in_dim(buffer, x, index, axis)

    def ordered(mine, other, axis):
        return jnp.where(
            first,
            jnp.concatenate([mine, other], axis=axis),
            jnp.concatenate([other, mine], axis=axis),
        )

    def halves(x, axis, size):
        return (
            lax.dynamic_slice_in_dim(x, k * size, size, axis),
            lax.dynamic_slice_in_dim(x, (1 - k) * size, size, axis),
        )

    def gather(x):
        rows = jnp.zeros((groups,) + x.shape, x.dtype)
        for step in range(groups):
            rows = put(rows, far(x, step) if step else x, g ^ step)
        full = jnp.zeros((groups, m) + x.shape, x.dtype)
        for step in range(m):
            full = put(full, near(rows, step) if step else rows, c ^ step, 1)
        return full.reshape((n,) + x.shape)

    def scatter_near(x):
        total = pick(x, c).astype(F32)
        for step in range(1, m):
            total = total + near(pick(x, c ^ step), step).astype(F32)
        return total

    def scatter_far(x):
        total = pick(x, g).astype(F32)
        for step in range(1, groups):
            total = total + far(pick(x, g ^ step), step).astype(F32)
        return total

    def scatter(x):
        x = x.reshape((groups, m) + x.shape[1:])
        part = scatter_near(jnp.swapaxes(x, 0, 1)).astype(BF)
        return scatter_far(part)

    def trade_far(x):
        out = jnp.zeros_like(x)
        for step in range(groups):
            part = pick(x, g ^ step)
            out = put(out, far(part, step) if step else part, g ^ step)
        return out

    def to_trees(x):
        mine, other = halves(x, 1, rh)
        return trade_far(ordered(mine, swap(other), 0))

    def from_trees(x):
        back = trade_far(x)
        mine, other = halves(back, 0, trees)
        return ordered(mine, swap(other), 1)

    kv_shard = jnp.concatenate(
        [
            lax.dynamic_slice_in_dim(key_weight, k * dh, dh, 1).reshape(ws, heads, 1, DH),
            lax.dynamic_slice_in_dim(value_weight, k * dh, dh, 1).reshape(ws, heads, 1, DH),
        ],
        axis=2,
    ).reshape(ws, d)
    proj_shard = jnp.concatenate(
        [
            lax.dynamic_slice_in_dim(query_weight, k * dh, dh, 1),
            kv_shard,
            lax.dynamic_slice_in_dim(relative_weight, k * dh, dh, 1),
        ],
        axis=1,
    )
    vec_shard = jnp.concatenate(
        [
            outer_bias,
            attend_gain,
            attend_shift,
            feed_gain,
            feed_shift,
            content_bias,
            position_bias,
            segment_bias,
            segment_table[0],
            segment_table[1],
            inner_bias,
        ]
    )
    vec_width = vec_shard.shape[0]
    vec_row = jnp.pad(vec_shard, (0, 4 * dh - vec_width))[None]
    proj_all = gather(jnp.concatenate([proj_shard, vec_row], axis=0))
    proj = proj_all[:, :ws].reshape(d, 4 * dh)
    vectors = proj_all[:, ws, :vec_width].astype(F32)
    vecs = vectors[:, : 10 * ws].reshape(n, 10, ws).swapaxes(0, 1).reshape(10, d)
    inner_shift = vectors[:, 10 * ws :].reshape(n, 2, fs // 2).swapaxes(0, 1).reshape(2, fh)
    outer_shift, gain_one, shift_one, gain_two, shift_two = [vecs[i] for i in range(5)]
    head_vecs = lax.dynamic_slice_in_dim(vecs[5:], k * dh, dh, 1)

    codes = jnp.stack(
        [segment_ids, rank_order // 64, rank_order % 64, query_flags], axis=1
    ).astype(BF)
    codes = codes.reshape(trees, 4, 2, rh).swapaxes(1, 2).reshape(trees, 2, 1, 4 * rh)
    codes = jnp.pad(codes, ((0, 0), (0, 0), (0, 0), (0, d - 4 * rh)))
    content_rows = jnp.concatenate([content_in.reshape(trees, 2, rh, d), codes], axis=2)
    mine, other = halves(content_rows, 1, 1)
    content_half = trade_far(ordered(mine[:, 0], swap(other[:, 0]), 0))
    tree_half = jnp.zeros((groups, m, rh + 1, d), BF)
    for step in range(m):
        tree_half = put(tree_half, near(content_half, step) if step else content_half, c ^ step, 1)
    tree_other = swap(tree_half)
    tree_rows = jnp.zeros((groups, m, 2, rh + 1, d), BF)
    tree_rows = put(tree_rows, tree_half, k, 2)
    tree_rows = put(tree_rows, tree_other, 1 - k, 2)
    content_full = tree_rows[:, :, :, :rh].reshape(length, d)
    codes = tree_rows[:, :, :, rh, : 4 * rh].reshape(n, 2, 4, rh).astype(F32)
    key_segs = codes[:, :, 0].reshape(length)
    key_ranks = (codes[:, :, 1] * 64.0 + codes[:, :, 2]).reshape(length)
    key_flags = codes[:, :, 3].reshape(length)
    query_half = to_trees(query_in)
    query_other = swap(query_half)
    own_content = pick(tree_rows, c, 1)[:, :, :rh]
    own_query = ordered(query_half[:, None], query_other[:, None], 1)
    inputs = jnp.stack([own_content, own_query], axis=1).reshape(groups * 2 * r, d)
    half_inputs = jnp.stack([content_half[:, :rh], query_half], axis=1).reshape(groups * r, d)

    parents = ordered(parent_ids, swap(parent_ids), 0)
    parents = pick(parents, g)
    labels = jnp.arange(NS, dtype=jnp.int32)
    reached = jnp.eye(NS, dtype=F32) + (parents[:, None] == labels[None, :]).astype(F32)
    for repeat in range(4):
        reached = jnp.minimum(jnp.dot(reached, reached, precision=HIGHEST), 1.0)
    reach = jnp.pad(jnp.concatenate([reached, reached], axis=1), ((0, 128 - NS), (0, 128 - 2 * NS)))
    reach = reach.astype(BF)
    feature = jnp.arange(128, dtype=jnp.int32)
    folded = jnp.where(feature < 2 * NS, feature % NS, -1).astype(F32)
    ones_lane = (feature == ONES) | (feature == ONES + 1)
    hot = ((key_segs[:, None] == folded[None]) | ones_lane[None]).astype(BF)
    key_present = jnp.max(
        (key_segs.reshape(nkb, KB)[:, :, None] == labels.astype(F32)).astype(F32), axis=1
    )
    by_block = lambda x: pick(x.reshape(groups, m, r), c, 1)
    row_segs, row_ranks, row_flags = by_block(key_segs), by_block(key_ranks), by_block(key_flags)
    row_present = jnp.max((row_segs[:, :, None] == labels.astype(F32)).astype(F32), axis=1)
    seen = jnp.dot(row_present, reached, precision=HIGHEST)
    live = (jnp.dot(seen, key_present.T, precision=HIGHEST) > 0.5).astype(jnp.int32).reshape(-1)
    base = length - R - R * (jnp.arange(groups, dtype=jnp.int32) * m + c)
    limits = jnp.stack([row_ranks, row_ranks - row_flags], axis=1)
    info = jnp.stack([jnp.broadcast_to(row_segs[:, None], limits.shape), limits], axis=-1)
    info = info.reshape(groups * 2 * r, 2)

    offsets = (length - 1 - jnp.arange(2 * length, dtype=jnp.int32)).astype(F32)
    position_bf = position_rows(offsets, d).astype(BF)
    sign = jnp.where(jnp.arange(d) < d // 2, -1.0, 1.0)
    rel_weight = proj[:, 3 * dh :]
    turned_weight = (rel_weight.astype(F32) * sign[:, None]).astype(BF)
    rel = mm(position_bf, rel_weight).astype(BF)
    rel_turned = mm(position_bf, turned_weight).astype(BF)
    queries = mm(inputs, proj[:, :dh])
    kv_weight = proj[:, dh : 3 * dh]
    kv = mm(content_full, kv_weight).astype(BF)
    vec8 = jnp.pad(head_vecs, ((0, 3), (0, 0)))
    table = head_vecs[3:5].reshape(2, heads, DH).swapaxes(0, 1)
    table = jnp.where(feature < 2 * NS, table[..., None], 0.0)
    probs, mixed, inverse = attend_forward(
        base, live, queries, vec8, table, info, reach, kv, hot, rel, key_ranks[None]
    )

    cols = inner_weight.reshape(ws, n, 2, fs // 2)
    inner_shard = pick(cols, k, 2).reshape(ws, fh)
    early = gather(
        jnp.concatenate([lax.dynamic_slice_in_dim(output_weight, k * dh, dh, 1), inner_shard], 1)
    ).reshape(d, dh + fh)
    outer_half = gather(pick(outer_weight.reshape(2, fs // 2, d), k)).reshape(fh, d)
    early_other = swap(early)
    outer_other = swap(outer_half)
    output_full = ordered(early[:, :dh], early_other[:, :dh], 1)
    inner_w = (early[:, dh:], early_other[:, dh:])
    outer_w = (outer_half, outer_other)
    shifts = (pick(inner_shift, k), pick(inner_shift, 1 - k))

    mixed_rows = mixed.astype(BF).reshape(groups * 2, 2, rh, dh)
    mine, other = halves(mixed_rows, 1, 1)
    mixed_bf = ordered(mine, swap(other), 3).reshape(groups * r, d)
    residual = mm(mixed_bf, output_full) + half_inputs.astype(F32)
    normed = layer_norm(residual, gain_one, shift_one)
    normed_bf = normed.astype(BF)
    inner_pre = [mm(normed_bf, w) + s for w, s in zip(inner_w, shifts)]
    hidden_bf = [gelu_tanh(x).astype(BF) for x in inner_pre]
    summed = mm(hidden_bf[0], outer_w[0]) + mm(hidden_bf[1], outer_w[1]) + outer_shift + normed
    result = layer_norm(summed, gain_two, shift_two).astype(BF).reshape(groups, 2, rh, d)
    outs = from_trees(result.reshape(groups, r, d)[:, :rh]), from_trees(
        result.reshape(groups, r, d)[:, rh:]
    )
    cotangent = jnp.stack([to_trees(content_cot), to_trees(query_cot)], axis=1)
    cotangent = cotangent.reshape(groups * r, d).astype(F32)
    unused, final_back = jax.vjp(layer_norm, summed, gain_two, shift_two)
    grad_summed, grad_final_gain, grad_final_shift = final_back(cotangent)
    grad_summed_bf = grad_summed.astype(BF)
    grad_inner = []
    for pre, w in zip(inner_pre, outer_w):
        unused, gelu_back = jax.vjp(gelu_tanh, pre)
        grad_inner.append(gelu_back(mm(grad_summed_bf, w, 1, 1))[0])
    grad_inner_bf = [x.astype(BF) for x in grad_inner]
    grad_normed = (
        mm(grad_inner_bf[0], inner_w[0], 1, 1) + mm(grad_inner_bf[1], inner_w[1], 1, 1) + grad_summed
    )
    unused, first_back = jax.vjp(layer_norm, residual, gain_one, shift_one)
    grad_residual, grad_norm_gain, grad_norm_shift = first_back(grad_normed)
    grad_residual_bf = grad_residual.astype(BF)
    grad_mixed = mm(grad_residual_bf, output_full, 1, 1).astype(BF)
    mine, other = halves(grad_mixed, 1, dh)
    grad_heads = ordered(
        mine.reshape(groups * 2, 1, rh, dh), swap(other).reshape(groups * 2, 1, rh, dh), 1
    ).reshape(groups * 2 * r, dh)

    grad_output = mm(mixed_bf, grad_residual_bf, 0, 0).astype(BF)
    mine_output, other_output = halves(grad_output, 1, dh)
    grad_inner_w = [mm(normed_bf, x, 0, 0).astype(BF) for x in grad_inner_bf]
    grad_outer_w = [mm(x, grad_summed_bf, 0, 0).astype(BF) for x in hidden_bf]
    row_vecs = jnp.stack(
        [
            jnp.sum(grad_summed, axis=0),
            grad_norm_gain,
            grad_norm_shift,
            grad_final_gain,
            grad_final_shift,
        ]
    ).reshape(5, n, ws)
    row_vecs = row_vecs.swapaxes(0, 1).reshape(n, 5 * ws)
    inner_vecs = [jnp.sum(x, axis=0).reshape(n, fs // 2) for x in grad_inner]

    def pack(parts_vec, out_part, inner_part, outer_part):
        vec = jnp.pad(parts_vec, ((0, 0), (0, d - parts_vec.shape[1])))[:, None].astype(BF)
        return jnp.concatenate(
            [
                out_part.reshape(n, ws * dh // d, d),
                inner_part.reshape(n, ws * fh // d, d),
                outer_part.reshape(n, fs // 2, d),
                vec,
            ],
            axis=1,
        )

    vec_halves = [
        jnp.concatenate([row_vecs, inner_vecs[i]], axis=1) for i in range(2)
    ]
    mine_pack = pack(vec_halves[0], mine_output, grad_inner_w[0], grad_outer_w[0])
    other_pack = pack(vec_halves[1], other_output, grad_inner_w[1], grad_outer_w[1])
    pack_sum = (mine_pack.astype(F32) + swap(other_pack).astype(F32)).astype(BF)
    late = scatter(pack_sum)

    dq, dkv, drel, small = attend_backward(
        base, live, probs, queries, grad_heads, mixed, inverse, vec8, info, kv, hot, rel_turned
    )

    grad_q_weight = mm(inputs, dq, 0, 0)
    grad_kv_weight = mm(content_full, dkv, 0, 0)
    grad_rel_weight = mm(position_bf, drel, 0, 0) * sign[:, None]
    proj_grad = jnp.concatenate([grad_q_weight, grad_kv_weight, grad_rel_weight], axis=1)
    small = small[:5].reshape(5, n // 2, ws).swapaxes(0, 1)
    small_rows = jnp.zeros((n, 5 * ws), F32)
    small_rows = lax.dynamic_update_slice_in_dim(
        small_rows, small.reshape(n // 2, 5 * ws), k * (n // 2), 0
    )
    small_rows = jnp.pad(small_rows, ((0, 0), (0, 4 * dh - 5 * ws)))[:, None]
    proj_parts = scatter(
        jnp.concatenate([proj_grad.reshape(n, ws, 4 * dh), small_rows], axis=1).astype(BF)
    )

    content_kv = mm(dkv, kv_weight, 1, 1).astype(BF).reshape(n, 2, rh, d)
    query_part = mm(dq, proj[:, :dh], 1, 1).astype(BF).reshape(groups * 2, 2, rh, d)
    mine_kv, other_kv = halves(content_kv, 1, 1)
    mine_q, other_q = halves(query_part, 1, 1)
    got = swap(jnp.concatenate([other_kv, other_q], axis=0)[:, 0]).astype(F32)
    kv_sum = (mine_kv[:, 0].astype(F32) + got[:n]).astype(BF).reshape(groups, m, rh, d)
    q_sum = (mine_q[:, 0].astype(F32) + got[n:]).reshape(groups, 2, rh, d)
    q_sum = q_sum + grad_residual.reshape(groups, 2, rh, d)
    content_sum = scatter_near(kv_sum.swapaxes(0, 1)) + q_sum[:, 0]
    grads = from_trees(content_sum.astype(BF)), from_trees(q_sum[:, 1].astype(BF))

    bit = 2
    flat = jnp.concatenate([late.reshape(-1), proj_parts.reshape(-1)])
    while bit < nr:
        flat = flat + lax.ppermute(flat, "rep", [(i, i ^ bit) for i in range(nr)])
        bit *= 2
    flat_other = swap(flat)
    late_size = late.size
    both = [
        (x[:late_size].reshape(late.shape), x[late_size:].reshape(proj_parts.shape))
        for x in (flat, flat_other)
    ]
    (late_a, proj_a), (late_b, proj_b) = both
    lo = jnp.where(first, late_a, late_b), jnp.where(first, late_b, late_a)
    pr = jnp.where(first, proj_a, proj_b), jnp.where(first, proj_b, proj_a)
    cut1 = ws * dh // d
    cut2 = cut1 + ws * fh // d
    cut3 = cut2 + fs // 2
    grad_wo = jnp.concatenate([x[:cut1].reshape(ws, dh) for x in lo], axis=1)
    grad_w1 = jnp.stack([x[cut1:cut2].reshape(ws, n, fs // 2) for x in lo], axis=2).reshape(ws, ff)
    grad_w2 = jnp.concatenate([x[cut2:cut3] for x in lo], axis=0)
    vec_lo = [x[cut3] for x in lo]
    vec_rows = vec_lo[0][: 5 * ws].reshape(5, ws)
    grad_b1 = jnp.concatenate([x[5 * ws : 5 * ws + fs // 2] for x in vec_lo])
    grad_wq = jnp.concatenate([x[:ws, :dh] for x in pr], axis=1)
    kv_parts = [x[:ws, dh : 3 * dh].reshape(ws, heads, 2, DH) for x in pr]
    grad_wk = jnp.concatenate([x[:, :, 0].reshape(ws, dh) for x in kv_parts], axis=1)
    grad_wv = jnp.concatenate([x[:, :, 1].reshape(ws, dh) for x in kv_parts], axis=1)
    grad_wr = jnp.concatenate([x[:ws, 3 * dh :] for x in pr], axis=1)
    head_rows = (pr[0][ws, : 5 * ws] + pr[1][ws, : 5 * ws]).reshape(5, ws)
    return (
        outs[0],
        outs[1],
        grads[0],
        grads[1],
        grad_wq,
        grad_wk,
        grad_wv,
        grad_wr,
        grad_wo,
        grad_w1,
        grad_w2,
        grad_b1,
        vec_rows[0],
        vec_rows[1],
        vec_rows[2],
        vec_rows[3],
        vec_rows[4],
        head_rows[0],
        head_rows[1],
        head_rows[2],
        head_rows[3:5],
    )


def solution(mesh):
    in_specs = (
        P("rep", "shard", None),
        P("rep", "shard", None),
        P("rep", "shard"),
        P("rep", None),
        P("rep", "shard"),
        P("rep", "shard"),
        P("shard", None),
        P("shard", None),
        P("shard", None),
        P("shard", None),
        P("shard", None),
        P("shard", None),
        P("shard", None),
        P("shard"),
        P("shard"),
        P("shard"),
        P("shard"),
        P("shard"),
        P("shard"),
        P("shard"),
        P("shard"),
        P("shard"),
        P(None, "shard"),
        P("rep", "shard", None),
        P("rep", "shard", None),
    )
    out_specs = (
        P("rep", "shard", None),
        P("rep", "shard", None),
        P("rep", "shard", None),
        P("rep", "shard", None),
        P("shard", None),
        P("shard", None),
        P("shard", None),
        P("shard", None),
        P("shard", None),
        P("shard", None),
        P("shard", None),
        P("shard"),
        P("shard"),
        P("shard"),
        P("shard"),
        P("shard"),
        P("shard"),
        P("shard"),
        P("shard"),
        P("shard"),
        P(None, "shard"),
    )
    return jax.shard_map(body, mesh=mesh, in_specs=in_specs, out_specs=out_specs, check_vma=False)
```

```python
import functools
import math

import jax
import jax.numpy as jnp
from jax import lax
from jax.experimental import pallas as pl
from jax.experimental.pallas import tpu as pltpu
from jax.sharding import PartitionSpec as P

DH = 64
NS = 13
EPSILON = 1e-05
NEG = -1e30
F32 = jnp.float32
BF = jnp.bfloat16
HIGHEST = lax.Precision.HIGHEST

R = 128
KB = 256
W = R + KB
SCALE = DH**-0.5
LOG2E = 1.4426950408889634
LN2 = 0.6931471805599453
ONES = 32


def mm(a, b, ca=1, cb=0, precision=None):
    return lax.dot_general(
        a, b, (((ca,), (cb,)), ((), ())), preferred_element_type=F32, precision=precision
    )


def row_features(seg_col):
    lane = lax.broadcasted_iota(jnp.int32, (2 * R, 128), 1)
    folded = jnp.where(lane < NS, lane, lane - NS).astype(F32)
    return jnp.where((lane < 2 * NS) & (folded == seg_col), 1.0, 0.0)


def live_list(live_ref, list_ref, row, nkb):
    per = KB // R

    def step(kb, count):
        list_ref[count] = kb
        live = live_ref[row, kb * per]
        for i in range(1, per):
            live = jnp.maximum(live, live_ref[row, kb * per + i])
        return count + live

    return lax.fori_loop(0, nkb, step, 0)


def ordered(kernel, count, extra):
    def run(*refs):
        kernel(*refs[:count], *refs[count + extra :])

    return run


def forward_kernel(
    nkb,
    base_ref,
    live_ref,
    q_ref,
    vec_ref,
    table_ref,
    info_ref,
    reach_ref,
    kv_ref,
    hot_ref,
    rel_ref,
    rank_ref,
    p_ref,
    o_ref,
    inv_ref,
    ob_ref,
    qq_scr,
    qr_scr,
    s_scr,
    m_scr,
    acc_scr,
    list_scr,
):
    block = pl.program_id(0)
    row = base_ref[0] + base_ref[1] * block
    base = nkb * KB - R - R * row
    count = live_list(live_ref, list_scr, row, nkb)
    seg_col = info_ref[:, 0:1]
    limit = info_ref[:, 1:2]
    hot_row = row_features(seg_col)
    lane = lax.broadcasted_iota(jnp.int32, (2 * R, 128), 1)
    reach = mm(jnp.where(lane < NS, hot_row, 0.0).astype(BF), reach_ref[...])
    outside = jnp.where((lane < 2 * NS) & (reach < 0.5), NEG, 0.0)
    zero = jnp.zeros((2 * R, DH), BF)
    for h in range(2):
        half = slice(DH * h, DH * h + DH)
        q = q_ref[:, half]
        plain = ((q + vec_ref[0:1, half]) * (SCALE * LOG2E)).astype(BF)
        place = ((q + vec_ref[1:2, half]) * (SCALE * LOG2E)).astype(BF)
        label = q + vec_ref[2:3, half]
        same = mm(label, table_ref[h, 0], precision=HIGHEST)
        other = mm(label, table_ref[h, 1], precision=HIGHEST)
        term = jnp.where(hot_row > 0.5, same, other) * (SCALE * LOG2E) + outside
        high = term.astype(BF).astype(F32)
        extra = jnp.where(lane < NS, high, jnp.where(lane < 2 * NS, term - high, 0.0))
        side = lambda x: [x, zero] if h == 0 else [zero, x]
        qq_scr[h] = jnp.concatenate(side(plain) + [extra.astype(BF)], axis=1)
        qr_scr[h] = jnp.concatenate(side(place), axis=1)
    m_scr[...] = jnp.full(m_scr.shape, -jnp.inf, F32)
    acc_scr[...] = jnp.zeros(acc_scr.shape, F32)

    def score(n, carry):
        k0 = pl.multiple_of(list_scr[n] * KB, KB)
        ok = rank_ref[:, pl.ds(k0, KB)] <= limit
        window = rel_ref[pl.ds(pl.multiple_of(base + k0, 128), W), :]
        keys = jnp.concatenate([kv_ref[pl.ds(k0, KB), :128], hot_ref[pl.ds(k0, KB), :]], axis=1)
        for h in range(2):
            s = mm(qq_scr[h], keys, 1, 1)
            full = mm(qr_scr[h], window, 1, 1)
            shifted = [
                pltpu.roll(full[i * R : i * R + R], W - (R - 1), 1, stride=1, stride_axis=0)[
                    :, :KB
                ]
                for i in range(2)
            ]
            s = jnp.where(ok, s + jnp.concatenate(shifted, axis=0), NEG)
            s_scr[h, n] = s
            m_scr[h] = jnp.maximum(m_scr[h], jnp.maximum(s[:, :128], s[:, 128:]))
        return carry

    lax.fori_loop(0, count, score, 0)
    top = [jnp.max(m_scr[h], axis=1, keepdims=True) for h in range(2)]

    def mix(n, carry):
        k0 = pl.multiple_of(list_scr[n] * KB, KB)
        values = jnp.concatenate([kv_ref[pl.ds(k0, KB), 128:], hot_ref[pl.ds(k0, KB), :]], axis=1)
        for h in range(2):
            p = jnp.exp2(s_scr[h, n] - top[h]).astype(BF)
            p_ref[0, h, n] = p
            acc_scr[h] += mm(p, values)
        return carry

    lax.fori_loop(0, count, mix, 0)
    for h in range(2):
        half = slice(DH * h, DH * h + DH)
        acc = acc_scr[h]
        inverse = 1.0 / acc[:, 128 + ONES : 129 + ONES]
        mixed = acc[:, half] * inverse
        o_ref[:, half] = mixed
        ob_ref[:, half] = mixed.astype(BF)
        inv_ref[:, half] = jnp.broadcast_to(inverse, (2 * R, DH))


def attend_forward(pair, after, base, live, q, vec, table, info, reach, kv, hot, rel, rank):
    nb = q.shape[0] // (2 * R)
    length = kv.shape[0]
    nkb = length // KB
    whole = lambda *shape: pl.BlockSpec(shape, lambda b, *_: (0,) * len(shape))
    return pl.pallas_call(
        ordered(functools.partial(forward_kernel, nkb), 11, len(after)),
        grid_spec=pltpu.PrefetchScalarGridSpec(
            num_scalar_prefetch=2,
            grid=(nb,),
            in_specs=[
                pl.BlockSpec((2 * R, 128), lambda b, *_: (b, pair)),
                pl.BlockSpec((8, 128), lambda b, *_: (0, pair)),
                pl.BlockSpec((2, 2, DH, 128), lambda b, *_: (pair, 0, 0, 0)),
                pl.BlockSpec((2 * R, 128), lambda b, *_: (b, 0)),
                whole(128, 128),
                pl.BlockSpec((length, 256), lambda b, *_: (0, pair)),
                whole(length, 128),
                pl.BlockSpec((2 * length, 128), lambda b, *_: (0, pair)),
                whole(1, length),
            ]
            + [pl.BlockSpec(memory_space=pl.ANY)] * len(after),
            out_specs=[
                pl.BlockSpec((1, 2, nkb, 2 * R, KB), lambda b, *_: (b, 0, 0, 0, 0)),
                pl.BlockSpec((2 * R, 128), lambda b, *_: (b, 0)),
                pl.BlockSpec((2 * R, 128), lambda b, *_: (b, 0)),
                pl.BlockSpec((2 * R, 128), lambda b, *_: (b, 0)),
            ],
            scratch_shapes=[
                pltpu.VMEM((2, 2 * R, 256), BF),
                pltpu.VMEM((2, 2 * R, 128), BF),
                pltpu.VMEM((2, nkb, 2 * R, KB), F32),
                pltpu.VMEM((2, 2 * R, 128), F32),
                pltpu.VMEM((2, 2 * R, 256), F32),
                pltpu.SMEM((nkb + 1,), jnp.int32),
            ],
        ),
        out_shape=[
            jax.ShapeDtypeStruct((nb, 2, nkb, 2 * R, KB), BF),
            jax.ShapeDtypeStruct((q.shape[0], 128), F32),
            jax.ShapeDtypeStruct((q.shape[0], 128), F32),
            jax.ShapeDtypeStruct((q.shape[0], 128), BF),
        ],
        compiler_params=pltpu.CompilerParams(
            dimension_semantics=("arbitrary",), vmem_limit_bytes=58 * 2**20
        ),
        cost_estimate=pl.CostEstimate(
            flops=10**8, bytes_accessed=10**6, transcendentals=0
        ),
        name="attend_forward",
    )(base, live, q, vec, table, info, reach, kv, hot, rel, rank, *after)


def backward_kernel(
    nkb,
    nb,
    base_ref,
    live_ref,
    p_ref,
    q_ref,
    g_ref,
    o_ref,
    inv_ref,
    vec_ref,
    info_ref,
    kv_ref,
    hot_ref,
    rel_ref,
    dq_ref,
    dkv_ref,
    drel_ref,
    small_ref,
    qq_scr,
    qr_scr,
    dd_scr,
    acc_scr,
    accr_scr,
    dkv_scr,
    drel_scr,
    flip_scr,
    list_scr,
):
    block = pl.program_id(0)
    length = nkb * KB
    row = base_ref[0] + base_ref[1] * block
    base = nkb * KB - R - R * row
    count = live_list(live_ref, list_scr, row, nkb)

    @pl.when(block == 0)
    def start():
        dkv_scr[...] = jnp.zeros(dkv_scr.shape, F32)
        drel_scr[...] = jnp.zeros(drel_scr.shape, F32)
        small_ref[...] = jnp.zeros(small_ref.shape, F32)
        down = lax.broadcasted_iota(jnp.int32, (KB, KB), 0)
        across = lax.broadcasted_iota(jnp.int32, (KB, KB), 1)
        flip_scr[...] = jnp.where(down + across == KB - 1, 1.0, 0.0).astype(BF)

    lane = lax.broadcasted_iota(jnp.int32, (2 * R, 128), 1)
    zero = jnp.zeros((2 * R, DH), BF)
    for h in range(2):
        half = slice(DH * h, DH * h + DH)
        q = q_ref[:, half]
        plain = ((q + vec_ref[0:1, half]) * (SCALE * LOG2E)).astype(BF)
        place = ((q + vec_ref[1:2, half]) * (SCALE * LOG2E)).astype(BF)
        g = g_ref[:, half].astype(F32)
        inverse = inv_ref[:, DH * h : DH * h + 1]
        delta = -jnp.sum(g * o_ref[:, half], axis=1, keepdims=True) * inverse
        high = delta.astype(BF).astype(F32)
        extra = jnp.where(lane == ONES, high, jnp.where(lane == ONES + 1, delta - high, 0.0))
        side = lambda x: [x, zero] if h == 0 else [zero, x]
        qq_scr[h] = jnp.concatenate(side(plain), axis=1)
        qr_scr[h] = jnp.concatenate(side(place), axis=1)
        dd_scr[h] = jnp.concatenate(side((g * inverse).astype(BF)) + [extra.astype(BF)], axis=1)
    acc_scr[...] = jnp.zeros(acc_scr.shape, F32)
    accr_scr[...] = jnp.zeros(accr_scr.shape, F32)

    def step(n, carry):
        k0 = pl.multiple_of(list_scr[n] * KB, KB)
        r0 = pl.multiple_of(2 * length - base - k0 - W, 128)
        hot = hot_ref[pl.ds(k0, KB), :]
        window = rel_ref[pl.ds(r0, W), :]
        pad = jnp.zeros((R, W - KB), F32)
        keys = jnp.concatenate([kv_ref[pl.ds(k0, KB), :128], hot], axis=1)
        values = jnp.concatenate([kv_ref[pl.ds(k0, KB), 128:], hot], axis=1)
        d_keys = d_values = d_rel = 0.0
        for h in range(2):
            p = p_ref[0, h, n]
            dd = dd_scr[h]
            ds = (p.astype(F32) * mm(dd, values, 1, 1)).astype(BF)
            acc_scr[h] += mm(ds, keys)
            turned = mm(ds, flip_scr[...])
            full = [
                pltpu.roll(
                    jnp.concatenate([turned[i * R : i * R + R], pad], axis=1),
                    0,
                    1,
                    stride=1,
                    stride_axis=0,
                )
                for i in range(2)
            ]
            full = jnp.concatenate(full, axis=0).astype(BF)
            accr_scr[h] += mm(full, window)
            d_rel += mm(full, qr_scr[h], 0, 0)
            d_keys += mm(ds, qq_scr[h], 0, 0)
            d_values += mm(p, dd[:, :128], 0, 0)
        drel_scr[pl.ds(r0, W), :] += d_rel
        dkv_scr[pl.ds(k0, KB), :128] += d_keys
        dkv_scr[pl.ds(k0, KB), 128:] += d_values
        return carry

    lax.fori_loop(0, count, step, 0)
    hot_row = row_features(info_ref[:, 0:1])
    for h in range(2):
        half = slice(DH * h, DH * h + DH)
        acc = acc_scr[h]
        d_plain = acc[:, half] * SCALE
        d_place = accr_scr[h][:, half] * SCALE
        sums = jnp.where(lane < NS, acc[:, 128:], 0.0) * SCALE
        same = jnp.sum(sums * hot_row, axis=1, keepdims=True)
        other = jnp.sum(sums, axis=1, keepdims=True) - same
        d_label = same * vec_ref[3:4, half] + other * vec_ref[4:5, half]
        label = q_ref[:, half] + vec_ref[2:3, half]
        dq_ref[:, half] = (d_plain + d_place + d_label).astype(BF)
        terms = [d_plain, d_place, d_label, same * label, other * label]
        for row, term in enumerate(terms):
            small_ref[row : row + 1, half] += jnp.sum(term, axis=0, keepdims=True)

    @pl.when(block == nb - 1)
    def finish():
        across = lax.broadcasted_iota(jnp.int32, (length, 256), 1)
        factor = jnp.where(across < 128, LN2, 1.0)
        dkv_ref[...] = (dkv_scr[...] * factor).astype(BF)
        drel_ref[...] = (drel_scr[...] * LN2).astype(BF)


def attend_backward(pair, after, base, live, p, q, g, o, inv, vec, info, kv, hot, rel):
    nb = q.shape[0] // (2 * R)
    length = kv.shape[0]
    nkb = length // KB
    own = pl.BlockSpec((2 * R, 128), lambda b, *_: (b, 0))
    rows = pl.BlockSpec((2 * R, 128), lambda b, *_: (b, pair))
    return pl.pallas_call(
        ordered(functools.partial(backward_kernel, nkb, nb), 12, len(after)),
        grid_spec=pltpu.PrefetchScalarGridSpec(
            num_scalar_prefetch=2,
            grid=(nb,),
            in_specs=[
                pl.BlockSpec((1, 2, nkb, 2 * R, KB), lambda b, *_: (b, 0, 0, 0, 0)),
                rows,
                rows,
                own,
                own,
                pl.BlockSpec((8, 128), lambda b, *_: (0, pair)),
                pl.BlockSpec((2 * R, 128), lambda b, *_: (b, 0)),
                pl.BlockSpec((length, 256), lambda b, *_: (0, pair)),
                pl.BlockSpec((length, 128), lambda b, *_: (0, 0)),
                pl.BlockSpec((2 * length, 128), lambda b, *_: (0, pair)),
            ]
            + [pl.BlockSpec(memory_space=pl.ANY)] * len(after),
            out_specs=[
                own,
                pl.BlockSpec((length, 256), lambda b, *_: (0, 0)),
                pl.BlockSpec((2 * length, 128), lambda b, *_: (0, 0)),
                pl.BlockSpec((8, 128), lambda b, *_: (0, 0)),
            ],
            scratch_shapes=[
                pltpu.VMEM((2, 2 * R, 128), BF),
                pltpu.VMEM((2, 2 * R, 128), BF),
                pltpu.VMEM((2, 2 * R, 256), BF),
                pltpu.VMEM((2, 2 * R, 256), F32),
                pltpu.VMEM((2, 2 * R, 128), F32),
                pltpu.VMEM((length, 256), F32),
                pltpu.VMEM((2 * length, 128), F32),
                pltpu.VMEM((KB, KB), BF),
                pltpu.SMEM((nkb + 1,), jnp.int32),
            ],
        ),
        out_shape=[
            jax.ShapeDtypeStruct((q.shape[0], 128), BF),
            jax.ShapeDtypeStruct((length, 256), BF),
            jax.ShapeDtypeStruct((2 * length, 128), BF),
            jax.ShapeDtypeStruct((8, 128), F32),
        ],
        compiler_params=pltpu.CompilerParams(
            dimension_semantics=("arbitrary",), vmem_limit_bytes=58 * 2**20
        ),
        cost_estimate=pl.CostEstimate(
            flops=10**8, bytes_accessed=10**6, transcendentals=0
        ),
        name="attend_backward",
    )(base, live, p, q, g, o, inv, vec, info, kv, hot, rel, *after)


def whole_block(x):
    return pl.BlockSpec(x.shape, lambda i: (0,) * len(x.shape))


def pack_kernel(r, ws, low_ref, content_ref, seg_ref, rank_ref, flag_ref, parent_ref, *refs):
    vec_refs, weight_refs, (a_ref, b_ref, scr) = refs[:4], refs[4:8], refs[8:]
    low = low_ref[0]
    for e, out in enumerate((a_ref, b_ref)):
        tree = jnp.bitwise_xor(low, e)
        out[:r, :] = content_ref[tree]
        scr[...] = jnp.zeros(scr.shape, F32)
        row = lambda ref: ref[pl.ds(tree, 1), :]
        rank = row(rank_ref)
        scr[0:1, :r] = row(seg_ref).astype(F32)
        scr[0:1, r : 2 * r] = lax.shift_right_logical(rank, 6).astype(F32)
        scr[0:1, 2 * r : 3 * r] = jnp.bitwise_and(rank, 63).astype(F32)
        scr[0:1, 3 * r : 4 * r] = row(flag_ref).astype(F32)
        scr[0:1, 4 * r : 4 * r + NS] = row(parent_ref).astype(F32)
        for i in range(3):
            scr[i + 1 : i + 2, :ws] = vec_refs[i][...].astype(F32)
        scr[4:6, :ws] = vec_refs[3][...].astype(F32)
        out[r : r + 16, :] = scr[...].astype(BF)
        for i in range(4):
            out[r + 16 + i * ws : r + 16 + (i + 1) * ws, :] = weight_refs[i][...]


def pack(low, content, segs, ranks, flags, parents, vecs, weights):
    trees, r, d = content.shape
    ws = weights[0].shape[0]
    shape = jax.ShapeDtypeStruct((r + 16 + 4 * ws, d), BF)
    return pl.pallas_call(
        functools.partial(pack_kernel, r, ws),
        grid=(1,),
        in_specs=[pl.BlockSpec(memory_space=pltpu.SMEM), whole_block(content)]
        + [whole_block(x) for x in (segs, ranks, flags, parents, *vecs, *weights)],
        out_specs=[whole_block(shape)] * 2,
        out_shape=[shape, shape],
        scratch_shapes=[pltpu.VMEM((16, d), F32)],
        compiler_params=pltpu.CompilerParams(vmem_limit_bytes=24 * 2**20),
        name="pack",
    )(low, content, segs, ranks, flags, parents, *vecs, *weights)


def assemble_kernel(r, ws, dh, m, at_ref, a0, a1, t0, t1, q_own, q_other, *outs):
    content_ref, codes_ref, wq_ref, wkv_ref, wr_ref, inputs_ref = outs
    k, low, c = at_ref[0], at_ref[1], at_ref[2]
    h, zl = pl.program_id(0), pl.program_id(1)
    column = lambda start: pl.multiple_of(k * dh + start, 128)

    def fill(src, query):
        inputs_ref[0, 0, 0] = src[0, :r, :]
        inputs_ref[0, 0, 1] = query[...]
        for step in range(m):
            to = jnp.bitwise_xor(c, step)
            rows = lambda i: slice(r + 16 + i * ws, r + 16 + (i + 1) * ws)
            content_ref[0, 0, to] = src[step, :r, :]
            codes_ref[0, 0, to] = src[step, r : r + 16, :]
            wq_ref[0, 0, to] = src[step, rows(0), pl.ds(column(0), dh)]
            wr_ref[0, 0, to] = src[step, rows(3), pl.ds(column(0), dh)]
            for p in range(dh // 128):
                for i in range(2):
                    wkv_ref[0, 0, to, :, 256 * p + 128 * i : 256 * p + 128 * i + 128] = src[
                        step, rows(1 + i), pl.ds(column(128 * p), 128)
                    ]

    for mine in (True, False):
        for e in range(2):
            src = ((a0, a1) if mine else (t0, t1))[e]
            query = (q_own if mine else q_other).at[e]

            @pl.when(((h == k) == mine) & (jnp.bitwise_xor(zl, low) == e))
            def case(src=src, query=query):
                fill(src, query)


def assemble(at, near_rows, their_rows, q_own, q_other, r, ws):
    m, rows, d = near_rows[0].shape
    dh = d // 2
    sizes = [(m, r, d), (m, 16, d), (m, ws, dh), (m, ws, d), (m, ws, dh), (2, r, d)]
    return pl.pallas_call(
        functools.partial(assemble_kernel, r, ws, dh, m),
        grid=(2, 2),
        in_specs=[pl.BlockSpec(memory_space=pltpu.SMEM)]
        + [pl.BlockSpec((m, rows, d), lambda h, z: (0, 0, 0))] * 4
        + [pl.BlockSpec((2, r, d), lambda h, z: (0, 0, 0))] * 2,
        out_specs=[pl.BlockSpec((1, 1) + size, lambda h, z: (h, z, 0, 0, 0)) for size in sizes],
        out_shape=[jax.ShapeDtypeStruct((2, 2) + size, BF) for size in sizes],
        compiler_params=pltpu.CompilerParams(vmem_limit_bytes=48 * 2**20),
        name="assemble",
    )(at, *near_rows, *their_rows, q_own, q_other)


def pack_late_kernel(ws, w1_ref, wo_ref, w2_ref, *refs):
    vec_refs, out, scr = refs[:-2], refs[-2], refs[-1]
    d = wo_ref.shape[1]
    parts = w1_ref.shape[1] // d
    for j in range(parts):
        out[j * ws : (j + 1) * ws, :] = w1_ref[:, j * d : (j + 1) * d]
    out[parts * ws : (parts + 1) * ws, :] = wo_ref[...]
    out[(parts + 1) * ws : (2 * parts + 1) * ws, :] = w2_ref[...]
    scr[...] = jnp.zeros(scr.shape, F32)
    row = 0
    for ref in vec_refs:
        scr[row : row + ref.shape[0], :ws] = ref[...].astype(F32)
        row += ref.shape[0]
    out[(2 * parts + 1) * ws :, :] = scr[...].astype(BF)


def pack_late(w1, wo, w2, vecs):
    ws, d = wo.shape
    rows = ws + w1.shape[1] // d * ws + w2.shape[0] + 16
    return pl.pallas_call(
        functools.partial(pack_late_kernel, ws),
        grid=(1,),
        in_specs=[whole_block(x) for x in (w1, wo, w2, *vecs)],
        out_specs=pl.BlockSpec((rows, d), lambda i: (0, 0)),
        out_shape=jax.ShapeDtypeStruct((rows, d), BF),
        scratch_shapes=[pltpu.VMEM((16, d), F32)],
        compiler_params=pltpu.CompilerParams(vmem_limit_bytes=24 * 2**20),
        name="pack_late",
    )(w1, wo, w2, *vecs)


def assemble_late_kernel(ws, m, at_ref, *refs):
    mine_refs, their_refs, (w1_ref, wo_ref, w2_ref, vec_ref) = refs[:m], refs[m : 2 * m], refs[2 * m :]
    k, low, c = at_ref[0], at_ref[1], at_ref[2]
    h, zl = pl.program_id(0), pl.program_id(1)
    d = wo_ref.shape[-1]
    parts = w1_ref.shape[-1] // d
    e = jnp.bitwise_xor(zl, low)

    def fill(refs):
        for step, src in enumerate(refs):
            to = jnp.bitwise_xor(c, step)
            for j in range(parts):
                w1_ref[0, 0, to, :, j * d : (j + 1) * d] = src[e, j * ws : (j + 1) * ws, :]
            wo_ref[0, 0, to] = src[e, parts * ws : (parts + 1) * ws, :]
            w2_ref[0, 0, to] = src[e, (parts + 1) * ws : (2 * parts + 1) * ws, :]
            vec_ref[0, 0, to] = src[e, (2 * parts + 1) * ws :, :]

    @pl.when(h == k)
    def own():
        fill(mine_refs)

    @pl.when(h != k)
    def other():
        fill(their_refs)


def assemble_late(at, mine, theirs, ws, parts):
    m = len(mine)
    two, rows, d = mine[0].shape
    sizes = [(m, ws, parts * d), (m, ws, d), (m, parts * ws, d), (m, 16, d)]
    return pl.pallas_call(
        functools.partial(assemble_late_kernel, ws, m),
        grid=(2, 2),
        in_specs=[pl.BlockSpec(memory_space=pltpu.SMEM)]
        + [pl.BlockSpec((2, rows, d), lambda h, z: (0, 0, 0))] * (2 * m),
        out_specs=[pl.BlockSpec((1, 1) + size, lambda h, z: (h, z, 0, 0, 0)) for size in sizes],
        out_shape=[jax.ShapeDtypeStruct((2, 2) + size, BF) for size in sizes],
        compiler_params=pltpu.CompilerParams(vmem_limit_bytes=56 * 2**20),
        name="assemble_late",
    )(at, *mine, *theirs)


def relative_kernel(sa_ref, ca_ref, sb_ref, cb_ref, w_ref, pos_ref, rel_ref, turned_ref):
    half = sb_ref.shape[1]
    fine = sb_ref.shape[0]
    for i in range(KB // fine):
        rows = slice(i * fine, (i + 1) * fine)
        sa, ca = sa_ref[0, i : i + 1, :], ca_ref[0, i : i + 1, :]
        sine = sa * cb_ref[...] - ca * sb_ref[...]
        cosine = ca * cb_ref[...] + sa * sb_ref[...]
        pos_ref[rows, :half] = sine.astype(BF)
        pos_ref[rows, half:] = cosine.astype(BF)
    from_sine = mm(pos_ref[:, :half], w_ref[:half, :])
    from_cosine = mm(pos_ref[:, half:], w_ref[half:, :])
    rel_ref[...] = (from_cosine + from_sine).astype(BF)
    turned_ref[...] = (from_cosine - from_sine).astype(BF)


def relative(wr, length):
    d, width = wr.shape
    half, fine = d // 2, 64
    powers = jnp.arange(half, dtype=F32) * (2.0 / d)
    inverse_freq = 1.0 / 10000.0**powers
    coarse = (length - 1 - fine * jnp.arange(2 * length // fine, dtype=jnp.int32)).astype(F32)
    a = coarse[:, None] * inverse_freq[None]
    b = jnp.arange(fine, dtype=F32)[:, None] * inverse_freq[None]
    per = KB // fine
    tables = [jnp.sin(a).reshape(-1, per, half), jnp.cos(a).reshape(-1, per, half), jnp.sin(b), jnp.cos(b)]
    rows = lambda w: pl.BlockSpec((KB, w), lambda i: (i, 0))
    return pl.pallas_call(
        relative_kernel,
        grid=(2 * length // KB,),
        in_specs=[pl.BlockSpec((1, per, half), lambda i: (i, 0, 0))] * 2
        + [pl.BlockSpec((fine, half), lambda i: (0, 0))] * 2
        + [pl.BlockSpec((d, width), lambda i: (0, 0))],
        out_specs=[rows(d), rows(width), rows(width)],
        out_shape=[
            jax.ShapeDtypeStruct((2 * length, d), BF),
            jax.ShapeDtypeStruct((2 * length, width), BF),
            jax.ShapeDtypeStruct((2 * length, width), BF),
        ],
        compiler_params=pltpu.CompilerParams(vmem_limit_bytes=24 * 2**20),
        cost_estimate=pl.CostEstimate(
            flops=4 * length * d * width, bytes_accessed=8 * length * d, transcendentals=0
        ),
        name="relative",
    )(*tables, wr)


def input_grad_kernel(count, at_ref, *refs):
    parts, w_ref, out_ref = refs[:count], refs[count], refs[-1]
    total = 0.0
    start = 0
    for ref in parts:
        width = ref.shape[1]
        total += mm(ref[...], w_ref[:, start : start + width], 1, 1)
        start += width
    out_ref[...] = total.astype(out_ref.dtype)


def input_grad(half, parts, w, dtype, after):
    rows = parts[0].shape[0] // 2
    block = math.gcd(rows, 256)
    d = w.shape[0]
    return pl.pallas_call(
        ordered(functools.partial(input_grad_kernel, len(parts)), len(parts) + 2, len(after)),
        grid_spec=pltpu.PrefetchScalarGridSpec(
            num_scalar_prefetch=1,
            grid=(rows // block,),
            in_specs=[
                pl.BlockSpec((block, x.shape[1]), lambda i, at: (at[0] * (rows // block) + i, 0))
                for x in parts
            ]
            + [pl.BlockSpec(w.shape, lambda i, at: (0, 0))]
            + [pl.BlockSpec(memory_space=pl.ANY)] * len(after),
            out_specs=pl.BlockSpec((block, d), lambda i, at: (i, 0)),
        ),
        out_shape=jax.ShapeDtypeStruct((rows, d), dtype),
        compiler_params=pltpu.CompilerParams(vmem_limit_bytes=24 * 2**20),
        cost_estimate=pl.CostEstimate(
            flops=2 * rows * d * w.shape[1], bytes_accessed=4 * rows * d, transcendentals=0
        ),
        name="input_grad",
    )(half, *parts, w, *after)


def mask_kernel(n, m, r, c_ref, codes_ref, rank_ref, hot_ref, info_ref, reach_ref, live_ref):
    c = c_ref[0]
    iota = lambda shape, axis: lax.broadcasted_iota(jnp.int32, shape, axis)
    choose = iota((n, 16 * n), 1) == 16 * iota((n, 16 * n), 0)
    rows = mm(choose.astype(F32).astype(BF), codes_ref[...])
    part = lambda i: rows[:, i * r : (i + 1) * r]
    segs = part(0)
    ranks = part(1) * 64.0 + part(2)
    flags = part(3)
    seg_cols, rank_cols, flag_cols = segs.T, ranks.T, flags.T
    parent_col = rows[:, 4 * r : 4 * r + 128].T[:, 0:1]
    lane = iota((128, 128), 1)
    down = iota((128, 128), 0)
    feature = jnp.where(lane < NS, lane, jnp.where(lane < 2 * NS, lane - NS, -1))
    folded = feature.astype(F32)
    ones_lane = (lane == ONES) | (lane == ONES + 1)
    for i in range(n):
        rank_ref[0:1, i * r : (i + 1) * r] = ranks[i : i + 1, :]
        hit = (folded == seg_cols[:, i : i + 1]) | ones_lane
        hot_ref[i * r : (i + 1) * r, :] = jnp.where(hit, 1.0, 0.0).astype(BF)
    mine = iota((r, n), 1)
    for b in range(n // m):
        column = lambda x: jnp.sum(jnp.where(mine == b * m + c, x, 0.0), axis=1, keepdims=True)
        seg, limit = column(seg_cols), column(rank_cols)
        lower = limit - column(flag_cols)
        for i, value in enumerate((limit, lower)):
            start = (2 * b + i) * r
            info_ref[start : start + r, :] = jnp.where(lane == 0, seg, value)
    inside = (down < NS) & (lane < NS)
    link = inside & ((down == lane) | (parent_col == lane.astype(F32)))
    reached = jnp.where(link, 1.0, 0.0)
    for repeat in range(4):
        half = reached.astype(BF)
        reached = jnp.minimum(mm(half, half), 1.0)
    reached = reached.astype(BF)
    twice = jnp.where(down == feature, 1.0, 0.0).astype(BF)
    reach_ref[...] = mm(reached, twice).astype(BF)
    spot = iota((n, 128), 1)
    present = jnp.zeros((n, 128), F32)
    for t in range(NS):
        any_t = jnp.max(jnp.where(segs == t, 1.0, 0.0), axis=1, keepdims=True)
        present = jnp.where(spot == t, any_t, present)
    present = present.astype(BF)
    seen = jnp.minimum(mm(present, reached), 1.0).astype(BF)
    live_ref[...] = jnp.minimum(mm(seen, present, 1, 1), 1.0).astype(jnp.int32)


def masks(c, codes, m, r):
    n, length = codes.shape[0] // 16, codes.shape[0] // 16 * r
    return pl.pallas_call(
        functools.partial(mask_kernel, n, m, r),
        grid=(1,),
        in_specs=[pl.BlockSpec(memory_space=pltpu.SMEM), whole_block(codes)],
        out_specs=[
            pl.BlockSpec(size, lambda i: (0, 0))
            for size in ((1, length), (length, 128), (n // m * 2 * r, 128), (128, 128), (n, n))
        ],
        out_shape=[
            jax.ShapeDtypeStruct((1, length), F32),
            jax.ShapeDtypeStruct((length, 128), BF),
            jax.ShapeDtypeStruct((n // m * 2 * r, 128), F32),
            jax.ShapeDtypeStruct((128, 128), BF),
            jax.ShapeDtypeStruct((n, n), jnp.int32),
        ],
        compiler_params=pltpu.CompilerParams(vmem_limit_bytes=24 * 2**20),
        name="masks",
    )(c, codes)


def hold_kernel(a_ref, b_ref, out_ref):
    out_ref[0] = a_ref[...]
    out_ref[1] = b_ref[...]


def hold(a, b, after):
    spec = pl.BlockSpec(a.shape, lambda i: (0, 0))
    return pl.pallas_call(
        ordered(hold_kernel, 2, len(after)),
        grid=(1,),
        in_specs=[spec, spec] + [pl.BlockSpec(memory_space=pl.ANY)] * len(after),
        out_specs=pl.BlockSpec((2,) + a.shape, lambda i: (0, 0, 0)),
        out_shape=jax.ShapeDtypeStruct((2,) + a.shape, a.dtype),
        compiler_params=pltpu.CompilerParams(vmem_limit_bytes=24 * 2**20),
        name="hold",
    )(a, b, *after)


def proj_grad_kernel(count, steps, x_ref, c_ref, pos_ref, *refs):
    dq, dkv, drel = refs[:count], refs[count : 2 * count], refs[2 * count : 3 * count]
    extra = refs[3 * count : -4]
    out_ref, q_scr, kv_scr, r_scr = refs[-4:]
    i = pl.program_id(0)

    @pl.when(i == 0)
    def start():
        for scr in (q_scr, kv_scr, r_scr):
            scr[...] = jnp.zeros(scr.shape, F32)

    for p in range(count):
        r_scr[p] += mm(drel[p][...], pos_ref[...], 0, 0)

    @pl.when(i < steps[1])
    def keys():
        for p in range(count):
            kv_scr[p] += mm(dkv[p][...], c_ref[...], 0, 0)

    @pl.when(i < steps[0])
    def queries():
        for p in range(count):
            q_scr[p] += mm(dq[p][...], x_ref[...], 0, 0)

    @pl.when(i == steps[2] - 1)
    def finish():
        d = pos_ref.shape[1]
        lane = lax.broadcasted_iota(jnp.int32, (128, d), 1)
        for p in range(count):
            at = 512 * p
            out_ref[:, at : at + 128] = q_scr[p].T.astype(BF)
            out_ref[:, at + 128 : at + 384] = kv_scr[p].T.astype(BF)
            turned = jnp.where(lane < d // 2, -r_scr[p], r_scr[p])
            out_ref[:, at + 384 : at + 512] = turned.T.astype(BF)
        for ref in extra:
            out_ref[:, 512 * count :] = ref[...]


def proj_grads(x, content, position, parts, extra, after):
    count = len(parts)
    d = x.shape[1]
    steps = [a.shape[0] // KB for a in (x, content, position)]
    spec = lambda width, kind: pl.BlockSpec(
        (KB, width), lambda i: (jnp.minimum(i, steps[kind] - 1), 0)
    )
    operands = [x, content, position]
    specs = [spec(d, kind) for kind in range(3)]
    for index, width, kind in ((0, 128, 0), (1, 256, 1), (2, 128, 2)):
        operands += [b[index] for b in parts]
        specs += [spec(width, kind)] * count
    operands += extra
    specs += [pl.BlockSpec(e.shape, lambda i: (0, 0)) for e in extra]
    width = 512 * count + sum(e.shape[1] for e in extra)
    total = len(operands)
    return pl.pallas_call(
        ordered(functools.partial(proj_grad_kernel, count, steps), total, len(after)),
        grid=(steps[2],),
        in_specs=specs + [pl.BlockSpec(memory_space=pl.ANY)] * len(after),
        out_specs=pl.BlockSpec((d, width), lambda i: (0, 0)),
        out_shape=jax.ShapeDtypeStruct((d, width), BF),
        scratch_shapes=[
            pltpu.VMEM((count, 128, d), F32),
            pltpu.VMEM((count, 256, d), F32),
            pltpu.VMEM((count, 128, d), F32),
        ],
        compiler_params=pltpu.CompilerParams(vmem_limit_bytes=32 * 2**20),
        cost_estimate=pl.CostEstimate(flops=10**9, bytes_accessed=10**6, transcendentals=0),
        name="proj_grads",
    )(*operands, *after)


def add_kernel(count, *refs):
    total = refs[0][...].astype(F32)
    for ref in refs[1:count]:
        total += ref[...].astype(F32)
    refs[-1][...] = total.astype(refs[-1].dtype)


def add_up(parts, dtype, after):
    shape = parts[0].shape
    rows = parts[0].size // shape[-1]
    flat = [x.reshape(rows, shape[-1]) for x in parts]
    block = rows // 2 if rows % 32 == 0 else rows
    spec = pl.BlockSpec((block, shape[-1]), lambda i: (i, 0))
    out = pl.pallas_call(
        ordered(functools.partial(add_kernel, len(parts)), len(parts), len(after)),
        grid=(rows // block,),
        in_specs=[spec] * len(parts) + [pl.BlockSpec(memory_space=pl.ANY)] * len(after),
        out_specs=spec,
        out_shape=jax.ShapeDtypeStruct((rows, shape[-1]), dtype),
        compiler_params=pltpu.CompilerParams(vmem_limit_bytes=32 * 2**20),
        cost_estimate=pl.CostEstimate(flops=rows, bytes_accessed=10**6, transcendentals=0),
        name="add_up",
    )(*flat, *after)
    return out.reshape(shape)


def layer_norm(vector, gain_row, shift_row):
    average = jnp.mean(vector, axis=-1, keepdims=True)
    centred = vector - average
    variance = jnp.mean(centred * centred, axis=-1, keepdims=True)
    return centred * lax.rsqrt(variance + EPSILON) * gain_row + shift_row


def gelu_tanh(vector):
    return jax.nn.gelu(vector, approximate=True)


def position_rows(offsets, model_width):
    half_width = model_width // 2
    powers = jnp.arange(half_width, dtype=F32) * (2.0 / model_width)
    inverse_freq = 1.0 / 10000.0**powers
    angles = offsets[:, None] * inverse_freq[None, :]
    return jnp.concatenate([jnp.sin(angles), jnp.cos(angles)], axis=1)


def body(
    content_in,
    query_in,
    segment_ids,
    parent_ids,
    rank_order,
    query_flags,
    query_weight,
    key_weight,
    value_weight,
    relative_weight,
    output_weight,
    inner_weight,
    outer_weight,
    inner_bias,
    outer_bias,
    attend_gain,
    attend_shift,
    feed_gain,
    feed_shift,
    content_bias,
    position_bias,
    segment_bias,
    segment_table,
    content_cot,
    query_cot,
):
    n = lax.axis_size("shard")
    nr = lax.axis_size("rep")
    trees, r, d = content_in.shape
    groups = 2 * trees
    m = n // groups
    length = r * n
    nkb = length // KB
    ff = inner_weight.shape[1]
    dh = d // 2
    heads = dh // DH
    pairs = heads // 2
    ws = query_weight.shape[0]
    fs = outer_weight.shape[0]
    me = lax.axis_index("shard")
    g, c = me // m, me % m
    low = g % 2
    k = lax.axis_index("rep") % 2
    first = k == 0
    tie = lax.optimization_barrier

    def swap(x):
        return lax.ppermute(x, "rep", [(i, i ^ 1) for i in range(nr)])

    def far(x, step):
        return lax.ppermute(x, "shard", [(i, i ^ (m * step)) for i in range(n)])

    def near(x, step):
        return lax.ppermute(x, "shard", [(i, i ^ step) for i in range(n)])

    def across(x, e):
        moves = []
        for i in range(nr):
            for j in range(n):
                z = j // m
                to = (i - i % 2 + z // 2) * n + (2 * (i % 2) + (z % 2 ^ e)) * m + j % m
                moves.append((i * n + j, to))
        return lax.ppermute(x, ("rep", "shard"), moves)

    def pick(x, index, axis=0):
        return lax.dynamic_index_in_dim(x, index, axis, keepdims=False)

    def put(buffer, x, index, axis=0):
        return lax.dynamic_update_index_in_dim(buffer, x, index, axis)

    def pair_of(mine, other, index, axis=0):
        return put(jnp.stack([mine, mine], axis), other, 1 - index, axis)

    def cross(parts):
        got = [across(pick(parts, low ^ e), e) for e in range(2)]
        return pair_of(got[0], got[1], low)

    def near_gather(x, downward):
        bits = [b for b in range(m.bit_length() - 1)]
        held = {0: x}
        for b in bits[::-1] if downward else bits:
            held.update({o | 1 << b: near(y, 1 << b) for o, y in list(held.items())})
        return jnp.stack([held[o] for o in range(m)])

    def near_parts(x, axis):
        sent = [near(pick(x, c ^ step, axis), step) for step in range(1, m)]
        return [pick(x, c, axis)] + sent

    def far_sum(x):
        total = pick(x, g).astype(F32)
        for step in range(1, groups):
            total = total + far(pick(x, g ^ step), step).astype(F32)
        return total

    weights = [query_weight, key_weight, value_weight, relative_weight]
    low_array = low.astype(jnp.int32).reshape(1)
    vec_rows = [x.reshape(1, ws) for x in (content_bias, position_bias, segment_bias)]
    packed = pack(
        low_array,
        content_in,
        segment_ids,
        rank_order,
        query_flags,
        parent_ids,
        vec_rows + [segment_table],
        weights,
    )
    at = jnp.stack([k, low, c]).astype(jnp.int32)
    got = [across(packed[e], e) for e in range(2)]
    own_query = jnp.stack([across(pick(query_in, low ^ e), e) for e in range(2)])
    near_rows = [near_gather(got[e], e) for e in range(2)]
    their_rows = [swap(x) for x in near_rows]
    content_full, codes, wq, kv_weight, wr, inputs = assemble(
        at, near_rows, their_rows, own_query, swap(own_query), r, ws
    )
    content_full = content_full.reshape(length, d)
    wq, kv_weight, wr = wq.reshape(d, dh), kv_weight.reshape(d, d), wr.reshape(d, dh)
    own_inputs = pick(inputs, k).reshape(groups * r, d)
    inputs = inputs.reshape(groups * 2 * r, d)
    codes = codes.reshape(n, 16, d)
    key_ranks, hot, info, reach, live = masks(
        c.astype(jnp.int32).reshape(1), codes.reshape(n * 16, d), m, r
    )
    base = jnp.stack([c, m]).astype(jnp.int32)
    vectors = codes[:, 1:6, :ws].astype(F32).swapaxes(0, 1).reshape(5, 2, dh)
    head_vecs = jnp.where(first, vectors[:, 0], vectors[:, 1])

    late_pack = pack_late(
        inner_weight,
        output_weight,
        outer_weight,
        [x.reshape(1, ws) for x in (outer_bias, attend_gain, attend_shift, feed_gain, feed_shift)]
        + [inner_bias.reshape(fs // ws, ws)],
    )
    late_pack, unused = tie((late_pack, got[1]))
    late = [across(late_pack, e) for e in range(2)]
    content_cot, query_cot, unused = tie((content_cot, query_cot, content_full))
    cots = cross(jnp.stack([content_cot, query_cot], axis=1))

    position_bf, rel, rel_turned = relative(wr, length)
    queries = mm(inputs, wq)
    kv = mm(content_full, kv_weight).astype(BF)
    vec8 = jnp.pad(head_vecs, ((0, 3), (0, 0)))
    table = head_vecs[3:5].reshape(2, heads, DH).swapaxes(0, 1)
    table = jnp.where(jnp.arange(128) < 2 * NS, table[..., None], 0.0)
    late = hold(late[0], late[1], [content_full, wr])
    late_near = [late] + [near(late, step) for step in range(1, m)]
    late_theirs = [swap(x) for x in late_near]
    forward = []
    got_mixed = []
    for pair in range(pairs):
        after = [[late], [], late_near + [cots]][min(pair, 2)]
        after = after + [f[1] for f in forward[-1:]]
        forward.append(
            attend_forward(
                pair,
                after,
                base,
                live,
                queries,
                vec8,
                table,
                info,
                reach,
                kv,
                hot,
                rel,
                key_ranks,
            )
        )
        got_mixed.append(swap(pick(forward[-1][3].reshape(2, groups * r, 128), 1 - k)))

    inner_w, output_w, outer_w, vecs = assemble_late(at, late_near, late_theirs, ws, ff // d)
    inner_w, output_w = inner_w.reshape(d, ff), output_w.reshape(d, d)
    outer_w = outer_w.reshape(ff, d)
    vecs = vecs.reshape(n, 16, d)[:, : 5 + fs // ws, :ws].astype(F32)
    inner_shift = vecs[:, 5:].reshape(ff)
    vecs = vecs[:, :5].swapaxes(0, 1).reshape(5, d)
    outer_shift, gain_one, shift_one, gain_two, shift_two = [vecs[i] for i in range(5)]

    own_mixed = [pick(f[3].reshape(2, groups * r, 128), k) for f in forward]
    mixed_bf = jnp.where(
        first,
        jnp.concatenate(own_mixed + got_mixed, axis=1),
        jnp.concatenate(got_mixed + own_mixed, axis=1),
    )
    residual = mm(mixed_bf, output_w) + own_inputs.astype(F32)
    normed = layer_norm(residual, gain_one, shift_one)
    normed_bf = normed.astype(BF)
    inner_pre = mm(normed_bf, inner_w) + inner_shift
    hidden_bf = gelu_tanh(inner_pre).astype(BF)
    summed = mm(hidden_bf, outer_w) + outer_shift + normed
    result = layer_norm(summed, gain_two, shift_two).astype(BF).reshape(2, 2, r, d)
    outs = cross(result)
    cotangent = cots.reshape(groups * r, d).astype(F32)
    unused, final_back = jax.vjp(layer_norm, summed, gain_two, shift_two)
    grad_summed, grad_final_gain, grad_final_shift = final_back(cotangent)
    grad_summed_bf = grad_summed.astype(BF)
    unused, gelu_back = jax.vjp(gelu_tanh, inner_pre)
    (grad_inner,) = gelu_back(mm(grad_summed_bf, outer_w, 1, 1))
    grad_inner_bf = grad_inner.astype(BF)
    grad_normed = mm(grad_inner_bf, inner_w, 1, 1) + grad_summed
    unused, first_back = jax.vjp(layer_norm, residual, gain_one, shift_one)
    grad_residual, grad_norm_gain, grad_norm_shift = first_back(grad_normed)
    grad_residual_bf = grad_residual.astype(BF)
    grad_mixed = mm(grad_residual_bf, output_w, 1, 1).astype(BF)
    mine_grad = lax.dynamic_slice_in_dim(grad_mixed, k * dh, dh, 1)
    got_grad = swap(lax.dynamic_slice_in_dim(grad_mixed, (1 - k) * dh, dh, 1))
    grad_heads = pair_of(mine_grad, got_grad, k).reshape(groups * 2 * r, dh)

    grad_late = mm(hidden_bf, grad_summed_bf, 0, 0).astype(BF).reshape(2, ff // 2, d)
    row_vecs = jnp.stack(
        [
            jnp.sum(grad_summed, axis=0),
            grad_norm_gain,
            grad_norm_shift,
            grad_final_gain,
            grad_final_shift,
        ],
        axis=1,
    )
    inner_vecs = jnp.sum(grad_inner, axis=0).reshape(n, fs // ws, ws).swapaxes(1, 2)
    row_vecs = jnp.concatenate([row_vecs, inner_vecs.reshape(d, fs // ws)], axis=1)
    row_vecs = jnp.pad(row_vecs, ((0, 0), (0, 128 - row_vecs.shape[1])))
    grad_early = jnp.concatenate(
        [
            mm(normed_bf, grad_inner_bf, 0, 0).astype(BF),
            mm(mixed_bf, grad_residual_bf, 0, 0).astype(BF),
            row_vecs.astype(BF),
        ],
        axis=1,
    ).reshape(2, d // 2, ff + d + 128)

    def cross_parts(x):
        return [across(pick(x, low ^ e), e) for e in range(2)]

    backward = []

    def back(pair, after):
        f = forward[pair]
        after = after + [b[0] for b in backward[-1:]]
        backward.append(
            attend_backward(
                pair,
                after,
                base,
                live,
                f[0],
                queries,
                grad_heads,
                f[1],
                f[2],
                vec8,
                info,
                kv,
                hot,
                rel_turned,
            )
        )

    def half_sum(x, rows, after):
        half = add_up([pick(x, k), swap(pick(x, 1 - k))], BF, after)
        return half.reshape(2, m, rows, x.shape[-1])

    def proj_some(some, extra, after):
        return proj_grads(
            inputs, content_full, position_bf, [backward[p] for p in some], extra, after
        ).reshape(groups, m, ws, -1)

    late_half = half_sum(grad_late, fs, [])
    late_parts = near_parts(late_half, 1)
    back(0, [late_half])
    after = [backward[0][0]]
    late_near = add_up(late_parts, BF, after)
    late_cross = cross_parts(late_near)
    early_half = half_sum(grad_early, ws, after)
    early_parts = near_parts(early_half, 1)
    back(1, [early_half, late_near, outs])
    some_grads = proj_some(range(pairs - 1), [], early_parts[1:] + late_cross)
    some_parts = near_parts(some_grads, 1)
    early_near = add_up(early_parts, BF, [])
    early_cross = cross_parts(early_near)
    back(2, [early_near, some_grads])

    which = [jnp.asarray(x, jnp.int32).reshape(1) for x in (k, 1 - k)]
    dkv_parts = [b[1] for b in backward]
    dq_parts = [b[0] for b in backward]
    got_kv = swap(input_grad(which[1], dkv_parts, kv_weight, BF, some_parts[1:] + early_cross))
    got_q = swap(input_grad(which[1], dq_parts, wq, BF, []))
    own_kv = input_grad(which[0], dkv_parts, kv_weight, F32, [])
    own_q = input_grad(which[0], dq_parts, wq, F32, [])
    kv_sum = add_up([own_kv, got_kv], BF, [])
    content_parts = near_parts(kv_sum.reshape(2, m, r, d), 1)
    q_sum = own_q + got_q.astype(F32) + grad_residual
    q_sum = q_sum.reshape(2, 2, r, d)
    query_grads = cross(q_sum[:, 1].astype(BF))

    small = jnp.concatenate([b[3][:5] for b in backward], axis=1)
    small = jnp.where(
        first,
        jnp.concatenate([small, jnp.zeros_like(small)], axis=1),
        jnp.concatenate([jnp.zeros_like(small), small], axis=1),
    )
    small = jnp.pad(small.T, ((0, 0), (0, 128 - 5))).astype(BF)
    last_grads = proj_some([pairs - 1], [small], [kv_sum])
    last_parts = near_parts(last_grads, 1)
    late_sum = add_up(late_cross, BF, [kv_sum])
    early_sum = add_up(early_cross, BF, [kv_sum])
    late_total = late_sum.astype(F32) + swap(late_sum).astype(F32)
    content_sum = sum([x.astype(F32) for x in content_parts]) + q_sum[:, 0]
    content_grads = cross(content_sum.astype(BF))
    some_near, last_near = [
        sum([x.astype(F32) for x in parts]).astype(BF) for parts in (some_parts, last_parts)
    ]
    proj_sum = far_sum(jnp.concatenate([some_near, last_near], axis=2))

    early_total = early_sum.astype(F32) + swap(early_sum).astype(F32)
    bit = 2
    while bit < nr:
        turn = [(i, i ^ bit) for i in range(nr)]
        early_total = early_total + lax.ppermute(early_total, "rep", turn)
        late_total = late_total + lax.ppermute(late_total, "rep", turn)
        proj_sum = proj_sum + lax.ppermute(proj_sum, "rep", turn)
        bit *= 2
    proj_other = swap(proj_sum)
    halves = jnp.where(first, proj_sum, proj_other), jnp.where(first, proj_other, proj_sum)

    def columns(index):
        return jnp.concatenate(
            [
                x[:, 512 * p + 128 * index : 512 * p + 128 * index + 128]
                for x in halves
                for p in range(pairs)
            ],
            axis=1,
        )

    vec_cols = early_total[:, ff + d :]
    head_cols = (proj_sum + proj_other)[:, 512 * pairs :]
    return (
        outs[:, 0],
        outs[:, 1],
        content_grads,
        query_grads,
        columns(0),
        columns(1),
        columns(2),
        columns(3),
        early_total[:, ff : ff + d],
        early_total[:, :ff],
        late_total,
        vec_cols[:, 5 : 5 + fs // ws].T.reshape(fs),
        vec_cols[:, 0],
        vec_cols[:, 1],
        vec_cols[:, 2],
        vec_cols[:, 3],
        vec_cols[:, 4],
        head_cols[:, 0],
        head_cols[:, 1],
        head_cols[:, 2],
        head_cols[:, 3:5].T,
    )


def solution(mesh):
    in_specs = (
        P("rep", "shard", None),
        P("rep", "shard", None),
        P("rep", "shard"),
        P("rep", None),
        P("rep", "shard"),
        P("rep", "shard"),
        P("shard", None),
        P("shard", None),
        P("shard", None),
        P("shard", None),
        P("shard", None),
        P("shard", None),
        P("shard", None),
        P("shard"),
        P("shard"),
        P("shard"),
        P("shard"),
        P("shard"),
        P("shard"),
        P("shard"),
        P("shard"),
        P("shard"),
        P(None, "shard"),
        P("rep", "shard", None),
        P("rep", "shard", None),
    )
    out_specs = (
        P("rep", "shard", None),
        P("rep", "shard", None),
        P("rep", "shard", None),
        P("rep", "shard", None),
        P("shard", None),
        P("shard", None),
        P("shard", None),
        P("shard", None),
        P("shard", None),
        P("shard", None),
        P("shard", None),
        P("shard"),
        P("shard"),
        P("shard"),
        P("shard"),
        P("shard"),
        P("shard"),
        P("shard"),
        P("shard"),
        P("shard"),
        P(None, "shard"),
    )
    return jax.shard_map(body, mesh=mesh, in_specs=in_specs, out_specs=out_specs, check_vma=False)
```

```python
import functools
import math

import jax
import jax.numpy as jnp
from jax import lax
from jax.experimental import pallas as pl
from jax.experimental.pallas import tpu as pltpu
from jax.sharding import PartitionSpec as P

DH = 64
NS = 13
EPSILON = 1e-05
NEG = -1e30
F32 = jnp.float32
BF = jnp.bfloat16
HIGHEST = lax.Precision.HIGHEST

R = 128
KB = 256
W = R + KB
SCALE = DH**-0.5
LOG2E = 1.4426950408889634
LN2 = 0.6931471805599453
VMEM = 60 * 2**20
SMALL = 32 * 2**20
ONES = 32


def mm(a, b, ca=1, cb=0, precision=None):
    return lax.dot_general(
        a, b, (((ca,), (cb,)), ((), ())), preferred_element_type=F32, precision=precision
    )


def row_features(seg_col):
    lane = lax.broadcasted_iota(jnp.int32, (2 * R, 128), 1)
    folded = jnp.where(lane < NS, lane, lane - NS).astype(F32)
    return jnp.where((lane < 2 * NS) & (folded == seg_col), 1.0, 0.0)


def live_list(live_ref, list_ref, row, nkb):
    per = KB // R

    def step(kb, count):
        list_ref[count] = kb
        live = live_ref[row, kb * per]
        for i in range(1, per):
            live = jnp.maximum(live, live_ref[row, kb * per + i])
        return count + live

    return lax.fori_loop(0, nkb, step, 0)


def ordered(kernel, count, extra):
    def run(*refs):
        kernel(*refs[:count], *refs[count + extra :])

    return run


def forward_kernel(
    nkb,
    base_ref,
    live_ref,
    q_ref,
    vec_ref,
    table_ref,
    info_ref,
    reach_ref,
    kv_ref,
    hot_ref,
    rel_ref,
    rank_ref,
    p_ref,
    o_ref,
    inv_ref,
    ob_ref,
    qq_scr,
    qr_scr,
    s_scr,
    m_scr,
    acc_scr,
    list_scr,
):
    block = pl.program_id(0)
    row = base_ref[0] + base_ref[1] * block
    base = nkb * KB - R - R * row
    count = live_list(live_ref, list_scr, row, nkb)
    seg_col = info_ref[:, 0:1]
    limit = info_ref[:, 1:2]
    hot_row = row_features(seg_col)
    lane = lax.broadcasted_iota(jnp.int32, (2 * R, 128), 1)
    reach = mm(jnp.where(lane < NS, hot_row, 0.0).astype(BF), reach_ref[...])
    outside = jnp.where((lane < 2 * NS) & (reach < 0.5), NEG, 0.0)
    zero = jnp.zeros((2 * R, DH), BF)
    for h in range(2):
        half = slice(DH * h, DH * h + DH)
        q = q_ref[:, half]
        plain = ((q + vec_ref[0:1, half]) * (SCALE * LOG2E)).astype(BF)
        place = ((q + vec_ref[1:2, half]) * (SCALE * LOG2E)).astype(BF)
        label = q + vec_ref[2:3, half]
        same = mm(label, table_ref[h, 0], precision=HIGHEST)
        other = mm(label, table_ref[h, 1], precision=HIGHEST)
        term = jnp.where(hot_row > 0.5, same, other) * (SCALE * LOG2E) + outside
        high = term.astype(BF).astype(F32)
        extra = jnp.where(lane < NS, high, jnp.where(lane < 2 * NS, term - high, 0.0))
        side = lambda x: [x, zero] if h == 0 else [zero, x]
        qq_scr[h] = jnp.concatenate(side(plain) + [extra.astype(BF)], axis=1)
        qr_scr[h] = jnp.concatenate(side(place), axis=1)
    m_scr[...] = jnp.full(m_scr.shape, -jnp.inf, F32)
    acc_scr[...] = jnp.zeros(acc_scr.shape, F32)

    def score(n, carry):
        k0 = pl.multiple_of(list_scr[n] * KB, KB)
        ok = rank_ref[:, pl.ds(k0, KB)] <= limit
        window = rel_ref[pl.ds(pl.multiple_of(base + k0, 128), W), :]
        keys = jnp.concatenate([kv_ref[pl.ds(k0, KB), :128], hot_ref[pl.ds(k0, KB), :]], axis=1)
        for h in range(2):
            s = mm(qq_scr[h], keys, 1, 1)
            full = mm(qr_scr[h], window, 1, 1)
            shifted = [
                pltpu.roll(full[i * R : i * R + R], W - (R - 1), 1, stride=1, stride_axis=0)[
                    :, :KB
                ]
                for i in range(2)
            ]
            s = jnp.where(ok, s + jnp.concatenate(shifted, axis=0), NEG)
            s_scr[h, n] = s
            m_scr[h] = jnp.maximum(m_scr[h], jnp.maximum(s[:, :128], s[:, 128:]))
        return carry

    lax.fori_loop(0, count, score, 0)
    top = [jnp.max(m_scr[h], axis=1, keepdims=True) for h in range(2)]

    def mix(n, carry):
        k0 = pl.multiple_of(list_scr[n] * KB, KB)
        values = jnp.concatenate([kv_ref[pl.ds(k0, KB), 128:], hot_ref[pl.ds(k0, KB), :]], axis=1)
        for h in range(2):
            p = jnp.exp2(s_scr[h, n] - top[h]).astype(BF)
            p_ref[0, h, n] = p
            acc_scr[h] += mm(p, values)
        return carry

    lax.fori_loop(0, count, mix, 0)
    for h in range(2):
        half = slice(DH * h, DH * h + DH)
        acc = acc_scr[h]
        inverse = 1.0 / acc[:, 128 + ONES : 129 + ONES]
        mixed = acc[:, half] * inverse
        o_ref[:, half] = mixed
        ob_ref[:, half] = mixed.astype(BF)
        inv_ref[:, half] = jnp.broadcast_to(inverse, (2 * R, DH))


def attend_forward(pair, after, base, live, q, vec, table, info, reach, kv, hot, rel, rank):
    nb = q.shape[0] // (2 * R)
    length = kv.shape[0]
    nkb = length // KB
    whole = lambda *shape: pl.BlockSpec(shape, lambda b, *_: (0,) * len(shape))
    return pl.pallas_call(
        ordered(functools.partial(forward_kernel, nkb), 11, len(after)),
        grid_spec=pltpu.PrefetchScalarGridSpec(
            num_scalar_prefetch=2,
            grid=(nb,),
            in_specs=[
                pl.BlockSpec((2 * R, 128), lambda b, *_: (b, pair)),
                pl.BlockSpec((8, 128), lambda b, *_: (0, pair)),
                pl.BlockSpec((2, 2, DH, 128), lambda b, *_: (pair, 0, 0, 0)),
                pl.BlockSpec((2 * R, 128), lambda b, *_: (b, 0)),
                whole(128, 128),
                pl.BlockSpec((length, 256), lambda b, *_: (0, pair)),
                whole(length, 128),
                pl.BlockSpec((2 * length, 128), lambda b, *_: (0, pair)),
                whole(1, length),
            ]
            + [pl.BlockSpec(memory_space=pl.ANY)] * len(after),
            out_specs=[
                pl.BlockSpec((1, 2, nkb, 2 * R, KB), lambda b, *_: (b, 0, 0, 0, 0)),
                pl.BlockSpec((2 * R, 128), lambda b, *_: (b, 0)),
                pl.BlockSpec((2 * R, 128), lambda b, *_: (b, 0)),
                pl.BlockSpec((2 * R, 128), lambda b, *_: (b, 0)),
            ],
            scratch_shapes=[
                pltpu.VMEM((2, 2 * R, 256), BF),
                pltpu.VMEM((2, 2 * R, 128), BF),
                pltpu.VMEM((2, nkb, 2 * R, KB), F32),
                pltpu.VMEM((2, 2 * R, 128), F32),
                pltpu.VMEM((2, 2 * R, 256), F32),
                pltpu.SMEM((nkb + 1,), jnp.int32),
            ],
        ),
        out_shape=[
            jax.ShapeDtypeStruct((nb, 2, nkb, 2 * R, KB), BF),
            jax.ShapeDtypeStruct((q.shape[0], 128), F32),
            jax.ShapeDtypeStruct((q.shape[0], 128), F32),
            jax.ShapeDtypeStruct((q.shape[0], 128), BF),
        ],
        compiler_params=pltpu.CompilerParams(
            dimension_semantics=("arbitrary",), vmem_limit_bytes=VMEM
        ),
        cost_estimate=pl.CostEstimate(
            flops=10**8, bytes_accessed=10**6, transcendentals=0
        ),
        name="attend_forward",
    )(base, live, q, vec, table, info, reach, kv, hot, rel, rank, *after)


def backward_kernel(
    nkb,
    nb,
    base_ref,
    live_ref,
    p_ref,
    q_ref,
    g_ref,
    o_ref,
    inv_ref,
    vec_ref,
    info_ref,
    kv_ref,
    hot_ref,
    rel_ref,
    dq_ref,
    dkv_ref,
    drel_ref,
    small_ref,
    turn_scr,
    dd_scr,
    acc_scr,
    accr_scr,
    dkv_scr,
    drel_scr,
    flip_scr,
    list_scr,
):
    block = pl.program_id(0)
    length = nkb * KB
    row = base_ref[0] + base_ref[1] * block
    base = nkb * KB - R - R * row
    count = live_list(live_ref, list_scr, row, nkb)

    @pl.when(block == 0)
    def start():
        dkv_scr[...] = jnp.zeros(dkv_scr.shape, F32)
        drel_scr[...] = jnp.zeros(drel_scr.shape, F32)
        small_ref[...] = jnp.zeros(small_ref.shape, F32)
        down = lax.broadcasted_iota(jnp.int32, (KB, KB), 0)
        across = lax.broadcasted_iota(jnp.int32, (KB, KB), 1)
        flip_scr[...] = jnp.where(down + across == KB - 1, 1.0, 0.0).astype(BF)

    lane = lax.broadcasted_iota(jnp.int32, (2 * R, 128), 1)
    zero = jnp.zeros((2 * R, DH), BF)
    for h in range(2):
        half = slice(DH * h, DH * h + DH)
        q = q_ref[:, half]
        plain = (q + vec_ref[0:1, half]) * (SCALE * LOG2E)
        place = (q + vec_ref[1:2, half]) * (SCALE * LOG2E)
        g = g_ref[:, half].astype(F32)
        inverse = inv_ref[:, DH * h : DH * h + 1]
        delta = -jnp.sum(g * o_ref[:, half], axis=1, keepdims=True) * inverse
        high = delta.astype(BF).astype(F32)
        extra = jnp.where(lane == ONES, high, jnp.where(lane == ONES + 1, delta - high, 0.0))
        side = lambda x: [x, zero] if h == 0 else [zero, x]
        scaled = g * inverse
        dd_scr[h] = jnp.concatenate(side(scaled.astype(BF)) + [extra.astype(BF)], axis=1)
        for i, x in enumerate((plain, scaled, place)):
            turn_scr[h, i] = x.T.astype(BF)
    acc_scr[...] = jnp.zeros(acc_scr.shape, F32)
    accr_scr[...] = jnp.zeros(accr_scr.shape, F32)

    def step(n, carry):
        k0 = pl.multiple_of(list_scr[n] * KB, KB)
        r0 = pl.multiple_of(2 * length - base - k0 - W, 128)
        hot = hot_ref[pl.ds(k0, KB), :]
        window = rel_ref[pl.ds(r0, W), :]
        pad = jnp.zeros((R, W - KB), F32)
        keys = jnp.concatenate([kv_ref[pl.ds(k0, KB), :128], hot], axis=1)
        values = jnp.concatenate([kv_ref[pl.ds(k0, KB), 128:], hot], axis=1)
        for h in range(2):
            p = p_ref[0, h, n]
            dd = dd_scr[h]
            ds = (p.astype(F32) * mm(dd, values, 1, 1)).astype(BF)
            acc_scr[h] += mm(ds, keys)
            turned = mm(ds, flip_scr[...])
            full = [
                pltpu.roll(
                    jnp.concatenate([turned[i * R : i * R + R], pad], axis=1),
                    0,
                    1,
                    stride=1,
                    stride_axis=0,
                )
                for i in range(2)
            ]
            full = jnp.concatenate(full, axis=0).astype(BF)
            accr_scr[h] += mm(full, window)
            low, high = DH * h, DH * h + DH
            dkv_scr[low:high, pl.ds(k0, KB)] += mm(turn_scr[h, 0], ds)
            dkv_scr[128 + low : 128 + high, pl.ds(k0, KB)] += mm(turn_scr[h, 1], p)
            drel_scr[low:high, pl.ds(r0, W)] += mm(turn_scr[h, 2], full)
        return carry

    lax.fori_loop(0, count, step, 0)
    hot_row = row_features(info_ref[:, 0:1])
    for h in range(2):
        half = slice(DH * h, DH * h + DH)
        acc = acc_scr[h]
        d_plain = acc[:, half] * SCALE
        d_place = accr_scr[h][:, half] * SCALE
        sums = jnp.where(lane < NS, acc[:, 128:], 0.0) * SCALE
        same = jnp.sum(sums * hot_row, axis=1, keepdims=True)
        other = jnp.sum(sums, axis=1, keepdims=True) - same
        d_label = same * vec_ref[3:4, half] + other * vec_ref[4:5, half]
        label = q_ref[:, half] + vec_ref[2:3, half]
        dq_ref[:, half] = (d_plain + d_place + d_label).astype(BF)
        terms = [d_plain, d_place, d_label, same * label, other * label]
        for row, term in enumerate(terms):
            small_ref[row : row + 1, half] += jnp.sum(term, axis=0, keepdims=True)

    @pl.when(block == nb - 1)
    def finish():
        dkv_ref[:128, :] = (dkv_scr[:128, :] * LN2).astype(BF)
        dkv_ref[128:, :] = dkv_scr[128:, :].astype(BF)
        drel_ref[...] = (drel_scr[...] * LN2).astype(BF)


def attend_backward(pair, after, base, live, p, q, g, o, inv, vec, info, kv, hot, rel):
    nb = q.shape[0] // (2 * R)
    length = kv.shape[0]
    nkb = length // KB
    own = pl.BlockSpec((2 * R, 128), lambda b, *_: (b, 0))
    rows = pl.BlockSpec((2 * R, 128), lambda b, *_: (b, pair))
    return pl.pallas_call(
        ordered(functools.partial(backward_kernel, nkb, nb), 12, len(after)),
        grid_spec=pltpu.PrefetchScalarGridSpec(
            num_scalar_prefetch=2,
            grid=(nb,),
            in_specs=[
                pl.BlockSpec((1, 2, nkb, 2 * R, KB), lambda b, *_: (b, 0, 0, 0, 0)),
                rows,
                rows,
                own,
                own,
                pl.BlockSpec((8, 128), lambda b, *_: (0, pair)),
                pl.BlockSpec((2 * R, 128), lambda b, *_: (b, 0)),
                pl.BlockSpec((length, 256), lambda b, *_: (0, pair)),
                pl.BlockSpec((length, 128), lambda b, *_: (0, 0)),
                pl.BlockSpec((2 * length, 128), lambda b, *_: (0, pair)),
            ]
            + [pl.BlockSpec(memory_space=pl.ANY)] * len(after),
            out_specs=[
                own,
                pl.BlockSpec((256, length), lambda b, *_: (0, 0)),
                pl.BlockSpec((128, 2 * length), lambda b, *_: (0, 0)),
                pl.BlockSpec((8, 128), lambda b, *_: (0, 0)),
            ],
            scratch_shapes=[
                pltpu.VMEM((2, 3, DH, 2 * R), BF),
                pltpu.VMEM((2, 2 * R, 256), BF),
                pltpu.VMEM((2, 2 * R, 256), F32),
                pltpu.VMEM((2, 2 * R, 128), F32),
                pltpu.VMEM((256, length), F32),
                pltpu.VMEM((128, 2 * length), F32),
                pltpu.VMEM((KB, KB), BF),
                pltpu.SMEM((nkb + 1,), jnp.int32),
            ],
        ),
        out_shape=[
            jax.ShapeDtypeStruct((q.shape[0], 128), BF),
            jax.ShapeDtypeStruct((256, length), BF),
            jax.ShapeDtypeStruct((128, 2 * length), BF),
            jax.ShapeDtypeStruct((8, 128), F32),
        ],
        compiler_params=pltpu.CompilerParams(
            dimension_semantics=("arbitrary",), vmem_limit_bytes=VMEM
        ),
        cost_estimate=pl.CostEstimate(
            flops=10**8, bytes_accessed=10**6, transcendentals=0
        ),
        name="attend_backward",
    )(base, live, p, q, g, o, inv, vec, info, kv, hot, rel, *after)


def whole_block(x):
    return pl.BlockSpec(x.shape, lambda i: (0,) * len(x.shape))


def pack_kernel(r, ws, low_ref, content_ref, seg_ref, rank_ref, flag_ref, parent_ref, *refs):
    vec_refs, weight_refs, (a_ref, b_ref, scr) = refs[:4], refs[4:8], refs[8:]
    low = low_ref[0]
    for e, out in enumerate((a_ref, b_ref)):
        tree = jnp.bitwise_xor(low, e)
        out[:r, :] = content_ref[tree]
        scr[...] = jnp.zeros(scr.shape, F32)
        row = lambda ref: ref[pl.ds(tree, 1), :]
        rank = row(rank_ref)
        scr[0:1, :r] = row(seg_ref).astype(F32)
        scr[0:1, r : 2 * r] = lax.shift_right_logical(rank, 6).astype(F32)
        scr[0:1, 2 * r : 3 * r] = jnp.bitwise_and(rank, 63).astype(F32)
        scr[0:1, 3 * r : 4 * r] = row(flag_ref).astype(F32)
        scr[0:1, 4 * r : 4 * r + NS] = row(parent_ref).astype(F32)
        for i in range(3):
            scr[i + 1 : i + 2, :ws] = vec_refs[i][...].astype(F32)
        scr[4:6, :ws] = vec_refs[3][...].astype(F32)
        out[r : r + 16, :] = scr[...].astype(BF)
        for i in range(4):
            out[r + 16 + i * ws : r + 16 + (i + 1) * ws, :] = weight_refs[i][...]


def pack(low, content, segs, ranks, flags, parents, vecs, weights):
    trees, r, d = content.shape
    ws = weights[0].shape[0]
    shape = jax.ShapeDtypeStruct((r + 16 + 4 * ws, d), BF)
    return pl.pallas_call(
        functools.partial(pack_kernel, r, ws),
        grid=(1,),
        in_specs=[pl.BlockSpec(memory_space=pltpu.SMEM), whole_block(content)]
        + [whole_block(x) for x in (segs, ranks, flags, parents, *vecs, *weights)],
        out_specs=[whole_block(shape)] * 2,
        out_shape=[shape, shape],
        scratch_shapes=[pltpu.VMEM((16, d), F32)],
        compiler_params=pltpu.CompilerParams(vmem_limit_bytes=VMEM),
        name="pack",
    )(low, content, segs, ranks, flags, parents, *vecs, *weights)


def assemble_kernel(r, ws, dh, m, at_ref, a0, a1, t0, t1, q_own, q_other, *outs):
    content_ref, codes_ref, wq_ref, wkv_ref, wr_ref, inputs_ref = outs
    k, low, c = at_ref[0], at_ref[1], at_ref[2]
    h, zl = pl.program_id(0), pl.program_id(1)
    column = lambda start: pl.multiple_of(k * dh + start, 128)

    def fill(src, query):
        inputs_ref[0, 0, 0] = src[0, :r, :]
        inputs_ref[0, 0, 1] = query[...]
        for step in range(m):
            to = jnp.bitwise_xor(c, step)
            rows = lambda i: slice(r + 16 + i * ws, r + 16 + (i + 1) * ws)
            content_ref[0, 0, to] = src[step, :r, :]
            codes_ref[0, 0, to] = src[step, r : r + 16, :]
            wq_ref[0, 0, to] = src[step, rows(0), pl.ds(column(0), dh)]
            wr_ref[0, 0, to] = src[step, rows(3), pl.ds(column(0), dh)]
            for p in range(dh // 128):
                for i in range(2):
                    wkv_ref[0, 0, to, :, 256 * p + 128 * i : 256 * p + 128 * i + 128] = src[
                        step, rows(1 + i), pl.ds(column(128 * p), 128)
                    ]

    for mine in (True, False):
        for e in range(2):
            src = ((a0, a1) if mine else (t0, t1))[e]
            query = (q_own if mine else q_other).at[e]

            @pl.when(((h == k) == mine) & (jnp.bitwise_xor(zl, low) == e))
            def case(src=src, query=query):
                fill(src, query)


def assemble(at, near_rows, their_rows, q_own, q_other, r, ws, after):
    m, rows, d = near_rows[0].shape
    dh = d // 2
    sizes = [(m, r, d), (m, 16, d), (m, ws, dh), (m, ws, d), (m, ws, dh), (2, r, d)]
    return pl.pallas_call(
        ordered(functools.partial(assemble_kernel, r, ws, dh, m), 7, len(after)),
        grid=(2, 2),
        in_specs=[pl.BlockSpec(memory_space=pltpu.SMEM)]
        + [pl.BlockSpec((m, rows, d), lambda h, z: (0, 0, 0))] * 4
        + [pl.BlockSpec((2, r, d), lambda h, z: (0, 0, 0))] * 2
        + [pl.BlockSpec(memory_space=pl.ANY)] * len(after),
        out_specs=[pl.BlockSpec((1, 1) + size, lambda h, z: (h, z, 0, 0, 0)) for size in sizes],
        out_shape=[jax.ShapeDtypeStruct((2, 2) + size, BF) for size in sizes],
        compiler_params=pltpu.CompilerParams(vmem_limit_bytes=SMALL),
        name="assemble",
    )(at, *near_rows, *their_rows, q_own, q_other, *after)


def pack_late_kernel(ws, w1_ref, wo_ref, w2_ref, *refs):
    vec_refs, out, scr = refs[:-2], refs[-2], refs[-1]
    d = wo_ref.shape[1]
    parts = w1_ref.shape[1] // d
    for j in range(parts):
        out[j * ws : (j + 1) * ws, :] = w1_ref[:, j * d : (j + 1) * d]
    out[parts * ws : (parts + 1) * ws, :] = wo_ref[...]
    out[(parts + 1) * ws : (2 * parts + 1) * ws, :] = w2_ref[...]
    scr[...] = jnp.zeros(scr.shape, F32)
    row = 0
    for ref in vec_refs:
        scr[row : row + ref.shape[0], : ref.shape[1]] = ref[...].astype(F32)
        row += ref.shape[0]
    out[(2 * parts + 1) * ws :, :] = scr[...].astype(BF)


def pack_late(w1, wo, w2, vecs):
    ws, d = wo.shape
    rows = ws + w1.shape[1] // d * ws + w2.shape[0] + 16
    return pl.pallas_call(
        functools.partial(pack_late_kernel, ws),
        grid=(1,),
        in_specs=[whole_block(x) for x in (w1, wo, w2, *vecs)],
        out_specs=pl.BlockSpec((rows, d), lambda i: (0, 0)),
        out_shape=jax.ShapeDtypeStruct((rows, d), BF),
        scratch_shapes=[pltpu.VMEM((16, d), F32)],
        compiler_params=pltpu.CompilerParams(vmem_limit_bytes=SMALL),
        name="pack_late",
    )(w1, wo, w2, *vecs)


def assemble_late_kernel(ws, m, at_ref, *refs):
    mine_refs, their_refs, (w1_ref, wo_ref, w2_ref, vec_ref) = refs[:m], refs[m : 2 * m], refs[2 * m :]
    k, low, c = at_ref[0], at_ref[1], at_ref[2]
    h, zl = pl.program_id(0), pl.program_id(1)
    d = wo_ref.shape[-1]
    parts = w1_ref.shape[-1] // d
    e = jnp.bitwise_xor(zl, low)

    def fill(refs):
        for step, src in enumerate(refs):
            to = jnp.bitwise_xor(c, step)
            for j in range(parts):
                w1_ref[0, 0, to, :, j * d : (j + 1) * d] = src[e, j * ws : (j + 1) * ws, :]
            wo_ref[0, 0, to] = src[e, parts * ws : (parts + 1) * ws, :]
            w2_ref[0, 0, to] = src[e, (parts + 1) * ws : (2 * parts + 1) * ws, :]
            vec_ref[0, 0, to] = src[e, (2 * parts + 1) * ws :, :]

    @pl.when(h == k)
    def own():
        fill(mine_refs)

    @pl.when(h != k)
    def other():
        fill(their_refs)


def assemble_late(at, mine, theirs, ws, parts):
    m = len(mine)
    two, rows, d = mine[0].shape
    sizes = [(m, ws, parts * d), (m, ws, d), (m, parts * ws, d), (m, 16, d)]
    return pl.pallas_call(
        functools.partial(assemble_late_kernel, ws, m),
        grid=(2, 2),
        in_specs=[pl.BlockSpec(memory_space=pltpu.SMEM)]
        + [pl.BlockSpec((2, rows, d), lambda h, z: (0, 0, 0))] * (2 * m),
        out_specs=[pl.BlockSpec((1, 1) + size, lambda h, z: (h, z, 0, 0, 0)) for size in sizes],
        out_shape=[jax.ShapeDtypeStruct((2, 2) + size, BF) for size in sizes],
        compiler_params=pltpu.CompilerParams(vmem_limit_bytes=SMALL),
        name="assemble_late",
    )(at, *mine, *theirs)


def relative_kernel(sa_ref, ca_ref, sb_ref, cb_ref, w_ref, pos_ref, rel_ref, turned_ref):
    half = sb_ref.shape[1]
    fine = sb_ref.shape[0]
    for i in range(KB // fine):
        rows = slice(i * fine, (i + 1) * fine)
        sa, ca = sa_ref[0, i : i + 1, :], ca_ref[0, i : i + 1, :]
        sine = sa * cb_ref[...] - ca * sb_ref[...]
        cosine = ca * cb_ref[...] + sa * sb_ref[...]
        pos_ref[rows, :half] = sine.astype(BF)
        pos_ref[rows, half:] = cosine.astype(BF)
    from_sine = mm(pos_ref[:, :half], w_ref[:half, :])
    from_cosine = mm(pos_ref[:, half:], w_ref[half:, :])
    rel_ref[...] = (from_cosine + from_sine).astype(BF)
    turned_ref[...] = (from_cosine - from_sine).astype(BF)


def relative(wr, length):
    d, width = wr.shape
    half, fine = d // 2, 64
    powers = jnp.arange(half, dtype=F32) * (2.0 / d)
    inverse_freq = 1.0 / 10000.0**powers
    coarse = (length - 1 - fine * jnp.arange(2 * length // fine, dtype=jnp.int32)).astype(F32)
    a = coarse[:, None] * inverse_freq[None]
    b = jnp.arange(fine, dtype=F32)[:, None] * inverse_freq[None]
    per = KB // fine
    tables = [jnp.sin(a).reshape(-1, per, half), jnp.cos(a).reshape(-1, per, half), jnp.sin(b), jnp.cos(b)]
    rows = lambda w: pl.BlockSpec((KB, w), lambda i: (i, 0))
    return pl.pallas_call(
        relative_kernel,
        grid=(2 * length // KB,),
        in_specs=[pl.BlockSpec((1, per, half), lambda i: (i, 0, 0))] * 2
        + [pl.BlockSpec((fine, half), lambda i: (0, 0))] * 2
        + [pl.BlockSpec((d, width), lambda i: (0, 0))],
        out_specs=[rows(d), rows(width), rows(width)],
        out_shape=[
            jax.ShapeDtypeStruct((2 * length, d), BF),
            jax.ShapeDtypeStruct((2 * length, width), BF),
            jax.ShapeDtypeStruct((2 * length, width), BF),
        ],
        compiler_params=pltpu.CompilerParams(vmem_limit_bytes=SMALL),
        cost_estimate=pl.CostEstimate(
            flops=4 * length * d * width, bytes_accessed=8 * length * d, transcendentals=0
        ),
        name="relative",
    )(*tables, wr)


def input_grad_kernel(count, turned, at_ref, *refs):
    parts, w_ref, out_ref = refs[:count], refs[count], refs[-1]
    total = 0.0
    start = 0
    for ref in parts:
        width = ref.shape[0 if turned else 1]
        total += mm(ref[...], w_ref[:, start : start + width], 0 if turned else 1, 1)
        start += width
    out_ref[...] = total.astype(out_ref.dtype)


def input_grad(half, parts, w, dtype, after, turned=False):
    rows = parts[0].shape[1 if turned else 0] // 2
    block = math.gcd(rows, 256)
    blocks = rows // block
    d = w.shape[0]
    return pl.pallas_call(
        ordered(
            functools.partial(input_grad_kernel, len(parts), turned), len(parts) + 2, len(after)
        ),
        grid_spec=pltpu.PrefetchScalarGridSpec(
            num_scalar_prefetch=1,
            grid=(rows // block,),
            in_specs=[
                pl.BlockSpec((x.shape[0], block), lambda i, at: (0, at[0] * blocks + i))
                if turned
                else pl.BlockSpec((block, x.shape[1]), lambda i, at: (at[0] * blocks + i, 0))
                for x in parts
            ]
            + [pl.BlockSpec(w.shape, lambda i, at: (0, 0))]
            + [pl.BlockSpec(memory_space=pl.ANY)] * len(after),
            out_specs=pl.BlockSpec((block, d), lambda i, at: (i, 0)),
        ),
        out_shape=jax.ShapeDtypeStruct((rows, d), dtype),
        compiler_params=pltpu.CompilerParams(vmem_limit_bytes=SMALL),
        cost_estimate=pl.CostEstimate(
            flops=2 * rows * d * w.shape[1], bytes_accessed=4 * rows * d, transcendentals=0
        ),
        name="input_grad",
    )(half, *parts, w, *after)


def mask_kernel(n, m, r, c_ref, codes_ref, rank_ref, hot_ref, info_ref, reach_ref, live_ref):
    c = c_ref[0]
    iota = lambda shape, axis: lax.broadcasted_iota(jnp.int32, shape, axis)
    choose = iota((n, 16 * n), 1) == 16 * iota((n, 16 * n), 0)
    rows = mm(choose.astype(F32).astype(BF), codes_ref[...])
    part = lambda i: rows[:, i * r : (i + 1) * r]
    segs = part(0)
    ranks = part(1) * 64.0 + part(2)
    flags = part(3)
    seg_cols, rank_cols, flag_cols = segs.T, ranks.T, flags.T
    parent_col = rows[:, 4 * r : 4 * r + 128].T[:, 0:1]
    lane = iota((128, 128), 1)
    down = iota((128, 128), 0)
    feature = jnp.where(lane < NS, lane, jnp.where(lane < 2 * NS, lane - NS, -1))
    folded = feature.astype(F32)
    ones_lane = (lane == ONES) | (lane == ONES + 1)
    for i in range(n):
        rank_ref[0:1, i * r : (i + 1) * r] = ranks[i : i + 1, :]
        hit = (folded == seg_cols[:, i : i + 1]) | ones_lane
        hot_ref[i * r : (i + 1) * r, :] = jnp.where(hit, 1.0, 0.0).astype(BF)
    mine = iota((r, n), 1)
    for b in range(n // m):
        column = lambda x: jnp.sum(jnp.where(mine == b * m + c, x, 0.0), axis=1, keepdims=True)
        seg, limit = column(seg_cols), column(rank_cols)
        lower = limit - column(flag_cols)
        for i, value in enumerate((limit, lower)):
            start = (2 * b + i) * r
            info_ref[start : start + r, :] = jnp.where(lane == 0, seg, value)
    inside = (down < NS) & (lane < NS)
    link = inside & ((down == lane) | (parent_col == lane.astype(F32)))
    reached = jnp.where(link, 1.0, 0.0)
    for repeat in range(4):
        half = reached.astype(BF)
        reached = jnp.minimum(mm(half, half), 1.0)
    reached = reached.astype(BF)
    twice = jnp.where(down == feature, 1.0, 0.0).astype(BF)
    reach_ref[...] = mm(reached, twice).astype(BF)
    spot = iota((n, 128), 1)
    present = jnp.zeros((n, 128), F32)
    for t in range(NS):
        any_t = jnp.max(jnp.where(segs == t, 1.0, 0.0), axis=1, keepdims=True)
        present = jnp.where(spot == t, any_t, present)
    present = present.astype(BF)
    seen = jnp.minimum(mm(present, reached), 1.0).astype(BF)
    live_ref[...] = jnp.minimum(mm(seen, present, 1, 1), 1.0).astype(jnp.int32)


def masks(c, codes, m, r):
    n, length = codes.shape[0] // 16, codes.shape[0] // 16 * r
    return pl.pallas_call(
        functools.partial(mask_kernel, n, m, r),
        grid=(1,),
        in_specs=[pl.BlockSpec(memory_space=pltpu.SMEM), whole_block(codes)],
        out_specs=[
            pl.BlockSpec(size, lambda i: (0, 0))
            for size in ((1, length), (length, 128), (n // m * 2 * r, 128), (128, 128), (n, n))
        ],
        out_shape=[
            jax.ShapeDtypeStruct((1, length), F32),
            jax.ShapeDtypeStruct((length, 128), BF),
            jax.ShapeDtypeStruct((n // m * 2 * r, 128), F32),
            jax.ShapeDtypeStruct((128, 128), BF),
            jax.ShapeDtypeStruct((n, n), jnp.int32),
        ],
        compiler_params=pltpu.CompilerParams(vmem_limit_bytes=SMALL),
        name="masks",
    )(c, codes)


def hold_kernel(a_ref, b_ref, out_ref):
    out_ref[0] = a_ref[...]
    out_ref[1] = b_ref[...]


def hold(a, b, after):
    spec = pl.BlockSpec(a.shape, lambda i: (0, 0))
    return pl.pallas_call(
        ordered(hold_kernel, 2, len(after)),
        grid=(1,),
        in_specs=[spec, spec] + [pl.BlockSpec(memory_space=pl.ANY)] * len(after),
        out_specs=pl.BlockSpec((2,) + a.shape, lambda i: (0, 0, 0)),
        out_shape=jax.ShapeDtypeStruct((2,) + a.shape, a.dtype),
        compiler_params=pltpu.CompilerParams(vmem_limit_bytes=SMALL),
        name="hold",
    )(a, b, *after)


def proj_grad_kernel(count, steps, x_ref, c_ref, pos_ref, *refs):
    dq, dkv, drel = refs[:count], refs[count : 2 * count], refs[2 * count : 3 * count]
    extra = refs[3 * count : -4]
    out_ref, q_scr, kv_scr, r_scr = refs[-4:]
    i = pl.program_id(0)

    @pl.when(i == 0)
    def start():
        for scr in (q_scr, kv_scr, r_scr):
            scr[...] = jnp.zeros(scr.shape, F32)

    beside = lambda refs, axis: jnp.concatenate([ref[...] for ref in refs], axis=axis)
    r_scr[...] += mm(beside(drel, 0), pos_ref[...])

    @pl.when(i < steps[1])
    def keys():
        kv_scr[...] += mm(beside(dkv, 0), c_ref[...])

    @pl.when(i < steps[0])
    def queries():
        q_scr[...] += mm(beside(dq, 1), x_ref[...], 0, 0)

    @pl.when(i == steps[2] - 1)
    def finish():
        d = pos_ref.shape[1]
        lane = lax.broadcasted_iota(jnp.int32, (128, d), 1)
        for p in range(count):
            at = 512 * p
            rows = slice(128 * p, 128 * p + 128)
            out_ref[:, at : at + 128] = q_scr[rows, :].T.astype(BF)
            out_ref[:, at + 128 : at + 384] = kv_scr[256 * p : 256 * p + 256, :].T.astype(BF)
            turned = jnp.where(lane < d // 2, -r_scr[rows, :], r_scr[rows, :])
            out_ref[:, at + 384 : at + 512] = turned.T.astype(BF)
        for ref in extra:
            out_ref[:, 512 * count :] = ref[...]


def proj_grads(x, content, position, parts, extra, after):
    count = len(parts)
    d = x.shape[1]
    size = 512
    steps = [a.shape[0] // size for a in (x, content, position)]
    spec = lambda width, kind: pl.BlockSpec(
        (size, width), lambda i: (jnp.minimum(i, steps[kind] - 1), 0)
    )
    turned = lambda width, kind: pl.BlockSpec(
        (width, size), lambda i: (0, jnp.minimum(i, steps[kind] - 1))
    )
    operands = [x, content, position]
    specs = [spec(d, kind) for kind in range(3)]
    for index, one in enumerate((spec(128, 0), turned(256, 1), turned(128, 2))):
        operands += [b[index] for b in parts]
        specs += [one] * count
    operands += extra
    specs += [pl.BlockSpec(e.shape, lambda i: (0, 0)) for e in extra]
    width = 512 * count + sum(e.shape[1] for e in extra)
    total = len(operands)
    return pl.pallas_call(
        ordered(functools.partial(proj_grad_kernel, count, steps), total, len(after)),
        grid=(steps[2],),
        in_specs=specs + [pl.BlockSpec(memory_space=pl.ANY)] * len(after),
        out_specs=pl.BlockSpec((d, width), lambda i: (0, 0)),
        out_shape=jax.ShapeDtypeStruct((d, width), BF),
        scratch_shapes=[
            pltpu.VMEM((count * 128, d), F32),
            pltpu.VMEM((count * 256, d), F32),
            pltpu.VMEM((count * 128, d), F32),
        ],
        compiler_params=pltpu.CompilerParams(vmem_limit_bytes=VMEM),
        cost_estimate=pl.CostEstimate(flops=10**9, bytes_accessed=10**6, transcendentals=0),
        name="proj_grads",
    )(*operands, *after)


def add_kernel(count, *refs):
    total = refs[0][...].astype(F32)
    for ref in refs[1:count]:
        total += ref[...].astype(F32)
    refs[-1][...] = total.astype(refs[-1].dtype)


def add_up(parts, dtype, after):
    shape = parts[0].shape
    rows = parts[0].size // shape[-1]
    flat = [x.reshape(rows, shape[-1]) for x in parts]
    block = rows // 2 if rows % 32 == 0 else rows
    spec = pl.BlockSpec((block, shape[-1]), lambda i: (i, 0))
    out = pl.pallas_call(
        ordered(functools.partial(add_kernel, len(parts)), len(parts), len(after)),
        grid=(rows // block,),
        in_specs=[spec] * len(parts) + [pl.BlockSpec(memory_space=pl.ANY)] * len(after),
        out_specs=spec,
        out_shape=jax.ShapeDtypeStruct((rows, shape[-1]), dtype),
        compiler_params=pltpu.CompilerParams(vmem_limit_bytes=SMALL),
        cost_estimate=pl.CostEstimate(flops=rows, bytes_accessed=10**6, transcendentals=0),
        name="add_up",
    )(*flat, *after)
    return out.reshape(shape)


def fold_kernel(m, count, at_ref, *refs):
    for step in range(m):
        total = refs[step * count][0, 0].astype(F32)
        for ref in refs[step * count + 1 : (step + 1) * count]:
            total += ref[0, 0].astype(F32)
        refs[m * count + step][0] = total.astype(BF)


def fold(at, arrays, after):
    two, m, rows, width = arrays[0].shape
    count = len(arrays)
    spec = lambda step: pl.BlockSpec(
        (1, 1, rows, width), lambda i, at: (i, jnp.bitwise_xor(at[2], step), 0, 0)
    )
    return pl.pallas_call(
        ordered(functools.partial(fold_kernel, m, count), m * count + 1, len(after)),
        grid_spec=pltpu.PrefetchScalarGridSpec(
            num_scalar_prefetch=1,
            grid=(2,),
            in_specs=[spec(step) for step in range(m) for x in arrays]
            + [pl.BlockSpec(memory_space=pl.ANY)] * len(after),
            out_specs=[pl.BlockSpec((1, rows, width), lambda i, at: (i, 0, 0))] * m,
        ),
        out_shape=[jax.ShapeDtypeStruct((2, rows, width), BF)] * m,
        compiler_params=pltpu.CompilerParams(vmem_limit_bytes=SMALL),
        cost_estimate=pl.CostEstimate(flops=rows, bytes_accessed=10**6, transcendentals=0),
        name="fold",
    )(at, *(list(arrays) * m), *after)


def join_kernel(count, at_ref, *refs):
    for e in range(2):
        total = refs[e * count][0].astype(F32)
        for ref in refs[e * count + 1 : (e + 1) * count]:
            total += ref[0].astype(F32)
        refs[2 * count + e][...] = total.astype(BF)


def join(at, arrays, after):
    two, rows, width = arrays[0].shape
    count = len(arrays)
    spec = lambda e: pl.BlockSpec(
        (1, rows, width), lambda i, at: (jnp.bitwise_xor(at[1], e), 0, 0)
    )
    return pl.pallas_call(
        ordered(functools.partial(join_kernel, count), 2 * count + 1, len(after)),
        grid_spec=pltpu.PrefetchScalarGridSpec(
            num_scalar_prefetch=1,
            grid=(1,),
            in_specs=[spec(e) for e in range(2) for x in arrays]
            + [pl.BlockSpec(memory_space=pl.ANY)] * len(after),
            out_specs=[pl.BlockSpec((rows, width), lambda i, at: (0, 0))] * 2,
        ),
        out_shape=[jax.ShapeDtypeStruct((rows, width), BF)] * 2,
        compiler_params=pltpu.CompilerParams(vmem_limit_bytes=SMALL),
        cost_estimate=pl.CostEstimate(flops=rows, bytes_accessed=10**6, transcendentals=0),
        name="join",
    )(at, *(list(arrays) * 2), *after)


GELU_A = 0.7978845608028654
GELU_B = 0.044715


def gelu_and_slope(v):
    square = v * v
    t = jnp.tanh(GELU_A * (v + GELU_B * (v * square)))
    half = 0.5 + 0.5 * t
    slope = half + 0.5 * v * (1.0 - t * t) * (GELU_A * (1.0 + 3.0 * GELU_B * square))
    return v * half, slope


def norm_forward(x):
    average = jnp.mean(x, axis=1, keepdims=True)
    centred = x - average
    inverse = lax.rsqrt(jnp.mean(centred * centred, axis=1, keepdims=True) + EPSILON)
    return centred * inverse, inverse


def norm_backward(grad, gain, unit, inverse):
    scaled = grad * gain
    pull = jnp.mean(scaled, axis=1, keepdims=True)
    twist = jnp.mean(scaled * unit, axis=1, keepdims=True)
    return inverse * (scaled - pull - unit * twist)


def dense_kernel(m, n, ws, pairs, at_ref, *refs):
    own_mixed, got_mixed = refs[:pairs], refs[pairs : 2 * pairs]
    x_ref, cot_ref = refs[2 * pairs : 2 * pairs + 2]
    pieces = refs[2 * pairs + 2 : 2 * pairs + 2 + 2 * m]
    rest = refs[2 * pairs + 2 + 2 * m :]
    result_ref, gr_ref, gm_own, gm_other, vec_ref, b1_ref = rest[:6]
    early_own, early_other, late_own, late_other = rest[6:10]
    w1, w2, wo, vp, slope, hidden, unit_bf, mixed, early, late, bias, sems, out_sems = rest[10:]
    k, low, c = at_ref[0], at_ref[1], at_ref[2]
    d = x_ref.shape[1]
    ff = w1.shape[1]
    parts = ff // d
    fs = parts * ws
    places = []
    for index, piece in enumerate(pieces):
        h = k if index < m else 1 - k
        for e in range(2):
            s = (2 * h + jnp.bitwise_xor(low, e)) * m + jnp.bitwise_xor(c, index % m)
            places.append((piece.at[e], s))
    kinds = 2 + parts + 1

    def load(i, kind, j=0):
        src, s = places[i]
        to = pl.ds(pl.multiple_of(s * ws, 16), ws)
        if kind == 0:
            pair = (src.at[pl.ds(parts * ws, ws), :], wo.at[to, :])
        elif kind == 1:
            pair = (src.at[pl.ds((2 * parts + 1) * ws, 16), :], vp.at[s])
        elif kind == 2:
            rows = pl.ds(pl.multiple_of(j * ws, 16), ws)
            pair = (src.at[rows, :], w1.at[to, pl.ds(pl.multiple_of(j * d, 128), d)])
        else:
            to = pl.ds(pl.multiple_of(s * fs, 16), fs)
            pair = (src.at[pl.ds((parts + 1) * ws, fs), :], w2.at[to, :])
        at = i * kinds + (kind if kind < 2 else 2 + j if kind == 2 else kinds - 1)
        return pltpu.make_async_copy(*pair, sems.at[at])

    count = len(places)
    for kind in (0, 1):
        for i in range(count):
            load(i, kind).start()
    for j in range(parts):
        for i in range(count):
            load(i, 2, j).start()
    for i in range(count):
        load(i, 3).start()

    for p in range(pairs):
        lanes = slice(128 * p, 128 * p + 128)
        other = slice(d // 2 + 128 * p, d // 2 + 128 * p + 128)

        @pl.when(k == 0)
        def low_core():
            mixed[:, lanes] = own_mixed[p][...]
            mixed[:, other] = got_mixed[p][...]

        @pl.when(k != 0)
        def high_core():
            mixed[:, lanes] = got_mixed[p][...]
            mixed[:, other] = own_mixed[p][...]

    for kind in (0, 1):
        for i in range(count):
            load(i, kind).wait()
    spot = lax.broadcasted_iota(jnp.int32, (128, d), 1)
    down = lax.broadcasted_iota(jnp.int32, (128, d), 0)
    vecs = jnp.zeros((16, d), F32)
    for s in range(n):
        place = jnp.where((spot == s * ws + down) & (down < ws), 1.0, 0.0).astype(BF)
        vecs += mm(vp[s, :, :128], place)
    per = (d // 2) // fs
    spot = lax.broadcasted_iota(jnp.int32, (256, d // 2), 1)
    down = lax.broadcasted_iota(jnp.int32, (256, d // 2), 0)
    place = [
        jnp.where((spot == t * fs + down) & (down < fs), 1.0, 0.0).astype(BF) for t in range(per)
    ]
    for q in range(n // per):
        row = sum(mm(vp[q * per + t, :, :256], place[t]) for t in range(per))
        bias[:, q * (d // 2) : (q + 1) * (d // 2)] = row[:8]
    outer_shift, gain_one, shift_one, gain_two, shift_two = [vecs[i : i + 1] for i in range(5)]

    residual = mm(mixed[...], wo[...]) + x_ref[...].astype(F32)
    unit_one, inverse_one = norm_forward(residual)
    normed = unit_one * gain_one + shift_one
    unit_bf[...] = normed.astype(BF)
    total = normed + outer_shift

    def wait_chunk(j):
        for i in range(count):
            load(i, 2, j).wait()

    for j in range(parts):
        wait_chunk(j)
        cols = slice(j * d, (j + 1) * d)
        value, slant = gelu_and_slope(mm(unit_bf[...], w1[:, cols]) + bias[5:6, cols])
        hidden[:, cols] = value.astype(BF)
        slope[:, cols] = slant
    for i in range(count):
        load(i, 3).wait()
    summed = total + mm(hidden[...], w2[...])
    unit_two, inverse_two = norm_forward(summed)
    result_ref[...] = (unit_two * gain_two + shift_two).astype(BF)
    cot = cot_ref[...].astype(F32)
    grad_summed = norm_backward(cot, gain_two, unit_two, inverse_two)
    row_sum = lambda x: jnp.sum(x, axis=0, keepdims=True)
    vec_ref[0:1, :] = row_sum(grad_summed)
    vec_ref[3:4, :] = row_sum(cot * unit_two)
    vec_ref[4:5, :] = row_sum(cot)
    grad_bf = grad_summed.astype(BF)
    grad_normed = grad_summed
    copies = []
    deep = early.shape[0] // 2
    split = ff // 2 // d

    def send(half, src, own, other):
        sem = out_sems.at[len(copies)]
        copies.append(pltpu.make_async_copy(src, own, sem))

        @pl.when(k == half)
        def keep():
            pltpu.make_async_copy(src, own, sem).start()

        @pl.when(k != half)
        def give():
            pltpu.make_async_copy(src, other, sem).start()

    def send_early(cols):
        for half in range(2):
            src = early.at[half * deep : (half + 1) * deep, cols]
            send(half, src, early_own.at[:, cols], early_other.at[:, cols])

    for j in range(parts):
        cols = slice(j * d, (j + 1) * d)
        grad_inner = mm(grad_bf, w2[cols, :], 1, 1) * slope[:, cols]
        b1_ref[0:1, cols] = row_sum(grad_inner)
        inner_bf = grad_inner.astype(BF)
        late[cols, :] = mm(hidden[:, cols], grad_bf, 0, 0).astype(BF)
        to = pl.ds((j % split) * d, d)
        send(j // split, late.at[cols, :], late_own.at[to, :], late_other.at[to, :])
        early[:, cols] = mm(unit_bf[...], inner_bf, 0, 0).astype(BF)
        send_early(cols)
        grad_normed += mm(inner_bf, w1[:, cols], 1, 1)
    vec_ref[1:2, :] = row_sum(grad_normed * unit_one)
    vec_ref[2:3, :] = row_sum(grad_normed)
    grad_residual = norm_backward(grad_normed, gain_one, unit_one, inverse_one)
    gr_ref[...] = grad_residual
    residual_bf = grad_residual.astype(BF)
    early[:, ff:] = mm(mixed[...], residual_bf, 0, 0).astype(BF)
    send_early(slice(ff, ff + d))
    grad_mixed = mm(residual_bf, wo[...], 1, 1).astype(BF)
    for half in range(2):
        part = grad_mixed[:, half * (d // 2) : (half + 1) * (d // 2)]

        @pl.when(k == half)
        def keep(part=part):
            gm_own[...] = part

        @pl.when(k != half)
        def give(part=part):
            gm_other[...] = part

    for copy in copies:
        copy.wait()


def dense(at, own_mixed, got_mixed, inputs, cots, mine, theirs, ws, ff):
    m = len(mine)
    pairs = len(own_mixed)
    rows, d = cots.shape
    n = d // ws
    parts = ff // d
    anywhere = pl.BlockSpec(memory_space=pl.ANY)
    half = lambda width: pl.BlockSpec((rows, width), lambda i, at: (at[0], 0))
    fixed = lambda *shape: pl.BlockSpec(shape, lambda i, at: (0,) * len(shape))
    return pl.pallas_call(
        functools.partial(dense_kernel, m, n, ws, pairs),
        grid_spec=pltpu.PrefetchScalarGridSpec(
            num_scalar_prefetch=1,
            grid=(1,),
            in_specs=[half(128)] * pairs
            + [fixed(rows, 128)] * pairs
            + [half(d), fixed(rows, d)]
            + [anywhere] * (2 * m),
            out_specs=[
                fixed(rows, d),
                fixed(rows, d),
                fixed(rows, d // 2),
                fixed(rows, d // 2),
                fixed(8, d),
                fixed(8, ff),
            ]
            + [anywhere] * 4,
            scratch_shapes=[
                pltpu.VMEM((d, ff), BF),
                pltpu.VMEM((ff, d), BF),
                pltpu.VMEM((d, d), BF),
                pltpu.VMEM((n, 16, d), BF),
                pltpu.VMEM((rows, ff), F32),
                pltpu.VMEM((rows, ff), BF),
                pltpu.VMEM((rows, d), BF),
                pltpu.VMEM((rows, d), BF),
                pltpu.VMEM((d, ff + d), BF),
                pltpu.VMEM((ff, d), BF),
                pltpu.VMEM((8, ff), F32),
                pltpu.SemaphoreType.DMA((4 * m * (3 + parts),)),
                pltpu.SemaphoreType.DMA((3 * parts + 2,)),
            ],
        ),
        out_shape=[
            jax.ShapeDtypeStruct((rows, d), BF),
            jax.ShapeDtypeStruct((rows, d), F32),
            jax.ShapeDtypeStruct((rows, d // 2), BF),
            jax.ShapeDtypeStruct((rows, d // 2), BF),
            jax.ShapeDtypeStruct((8, d), F32),
            jax.ShapeDtypeStruct((8, ff), F32),
            jax.ShapeDtypeStruct((d // 2, ff + d), BF),
            jax.ShapeDtypeStruct((d // 2, ff + d), BF),
            jax.ShapeDtypeStruct((ff // 2, d), BF),
            jax.ShapeDtypeStruct((ff // 2, d), BF),
        ],
        compiler_params=pltpu.CompilerParams(vmem_limit_bytes=VMEM),
        cost_estimate=pl.CostEstimate(flops=10**9, bytes_accessed=10**6, transcendentals=0),
        name="dense",
    )(at, *own_mixed, *got_mixed, inputs, cots, *mine, *theirs)


def dense_plain(at, own_mixed, got_mixed, inputs, cots, mine, theirs, ws, ff):
    rows, d = cots.shape
    n, fs = d // ws, ff * ws // d
    k = at[0]
    mine_half = lambda x: lax.dynamic_slice_in_dim(x, k * rows, rows, 0)
    inner_w, output_w, outer_w, vecs = assemble_late(at, mine, theirs, ws, ff // d)
    inner_w, output_w = inner_w.reshape(d, ff), output_w.reshape(d, d)
    outer_w = outer_w.reshape(ff, d)
    vecs = vecs.reshape(n, 16, d).astype(F32)
    inner_shift = vecs[:, 5, :fs].reshape(ff)
    vecs = vecs[:, :5, :ws].swapaxes(0, 1).reshape(5, d)
    outer_shift, gain_one, shift_one, gain_two, shift_two = [vecs[i] for i in range(5)]
    own = [mine_half(x) for x in own_mixed]
    mixed = jnp.where(
        k == 0,
        jnp.concatenate(own + got_mixed, axis=1),
        jnp.concatenate(got_mixed + own, axis=1),
    )
    residual = mm(mixed, output_w) + mine_half(inputs).astype(F32)
    unit_one, inverse_one = norm_forward(residual)
    normed = unit_one * gain_one + shift_one
    normed_bf = normed.astype(BF)
    value, slope = gelu_and_slope(mm(normed_bf, inner_w) + inner_shift)
    hidden = value.astype(BF)
    summed = mm(hidden, outer_w) + outer_shift + normed
    unit_two, inverse_two = norm_forward(summed)
    result = (unit_two * gain_two + shift_two).astype(BF)
    cot = cots.astype(F32)
    grad_summed = norm_backward(cot, gain_two, unit_two, inverse_two)
    grad_bf = grad_summed.astype(BF)
    grad_inner = mm(grad_bf, outer_w, 1, 1) * slope
    inner_bf = grad_inner.astype(BF)
    grad_normed = mm(inner_bf, inner_w, 1, 1) + grad_summed
    grad_residual = norm_backward(grad_normed, gain_one, unit_one, inverse_one)
    residual_bf = grad_residual.astype(BF)
    grad_mixed = mm(residual_bf, output_w, 1, 1).astype(BF)
    terms = [grad_summed, grad_normed * unit_one, grad_normed, cot * unit_two, cot]
    early = jnp.concatenate([mm(normed_bf, inner_bf, 0, 0), mm(mixed, residual_bf, 0, 0)], axis=1)

    def halves(x, axis):
        size = x.shape[axis] // 2
        return [lax.dynamic_slice_in_dim(x, i * size, size, axis).astype(BF) for i in (k, 1 - k)]

    return (
        result,
        grad_residual,
        *halves(grad_mixed, 1),
        jnp.stack([jnp.sum(x, axis=0) for x in terms]),
        jnp.sum(grad_inner, axis=0)[None],
        *halves(early, 0),
        *halves(mm(hidden, grad_bf, 0, 0), 0),
    )


def body(
    content_in,
    query_in,
    segment_ids,
    parent_ids,
    rank_order,
    query_flags,
    query_weight,
    key_weight,
    value_weight,
    relative_weight,
    output_weight,
    inner_weight,
    outer_weight,
    inner_bias,
    outer_bias,
    attend_gain,
    attend_shift,
    feed_gain,
    feed_shift,
    content_bias,
    position_bias,
    segment_bias,
    segment_table,
    content_cot,
    query_cot,
):
    n = lax.axis_size("shard")
    nr = lax.axis_size("rep")
    trees, r, d = content_in.shape
    groups = 2 * trees
    m = n // groups
    length = r * n
    nkb = length // KB
    ff = inner_weight.shape[1]
    dh = d // 2
    heads = dh // DH
    pairs = heads // 2
    ws = query_weight.shape[0]
    fs = outer_weight.shape[0]
    me = lax.axis_index("shard")
    g, c = me // m, me % m
    low = g % 2
    k = lax.axis_index("rep") % 2
    first = k == 0
    tie = lax.optimization_barrier

    def swap(x):
        return lax.ppermute(x, "rep", [(i, i ^ 1) for i in range(nr)])

    def far(x, step):
        return lax.ppermute(x, "shard", [(i, i ^ (m * step)) for i in range(n)])

    def near(x, step):
        return lax.ppermute(x, "shard", [(i, i ^ step) for i in range(n)])

    def across(x, e):
        moves = []
        for i in range(nr):
            for j in range(n):
                z = j // m
                to = (i - i % 2 + z // 2) * n + (2 * (i % 2) + (z % 2 ^ e)) * m + j % m
                moves.append((i * n + j, to))
        return lax.ppermute(x, ("rep", "shard"), moves)

    def pick(x, index, axis=0):
        return lax.dynamic_index_in_dim(x, index, axis, keepdims=False)

    def put(buffer, x, index, axis=0):
        return lax.dynamic_update_index_in_dim(buffer, x, index, axis)

    def pair_of(mine, other, index, axis=0):
        return put(jnp.stack([mine, mine], axis), other, 1 - index, axis)

    def cross(parts):
        got = [across(pick(parts, low ^ e), e) for e in range(2)]
        return pair_of(got[0], got[1], low)

    def near_gather(x, downward):
        bits = [b for b in range(m.bit_length() - 1)]
        held = {0: x}
        for b in bits[::-1] if downward else bits:
            held.update({o | 1 << b: near(y, 1 << b) for o, y in list(held.items())})
        return jnp.stack([held[o] for o in range(m)])

    def near_parts(x, axis):
        sent = [near(pick(x, c ^ step, axis), step) for step in range(1, m)]
        return [pick(x, c, axis)] + sent

    def far_sum(x):
        total = pick(x, g).astype(F32)
        for step in range(1, groups):
            total = total + far(pick(x, g ^ step), step).astype(F32)
        return total

    weights = [query_weight, key_weight, value_weight, relative_weight]
    low_array = low.astype(jnp.int32).reshape(1)
    vec_rows = [x.reshape(1, ws) for x in (content_bias, position_bias, segment_bias)]
    packed = pack(
        low_array,
        content_in,
        segment_ids,
        rank_order,
        query_flags,
        parent_ids,
        vec_rows + [segment_table],
        weights,
    )
    at = jnp.stack([k, low, c]).astype(jnp.int32)
    got = [across(packed[e], e) for e in range(2)]
    own_query = jnp.stack([across(pick(query_in, low ^ e), e) for e in range(2)])
    near_rows = [near_gather(got[e], e) for e in range(2)]
    their_rows = [swap(x) for x in near_rows]
    late_pack = pack_late(
        inner_weight,
        output_weight,
        outer_weight,
        [x.reshape(1, ws) for x in (outer_bias, attend_gain, attend_shift, feed_gain, feed_shift)]
        + [inner_bias.reshape(1, fs)],
    )
    late_pack, unused = tie((late_pack, got[1]))
    late = [across(late_pack, e) for e in range(2)]
    content_full, codes, wq, kv_weight, wr, inputs = assemble(
        at, near_rows, their_rows, own_query, swap(own_query), r, ws, []
    )
    content_full = content_full.reshape(length, d)
    wq, kv_weight, wr = wq.reshape(d, dh), kv_weight.reshape(d, d), wr.reshape(d, dh)
    inputs = inputs.reshape(groups * 2 * r, d)
    codes = codes.reshape(n, 16, d)
    key_ranks, hot, info, reach, live = masks(
        c.astype(jnp.int32).reshape(1), codes.reshape(n * 16, d), m, r
    )
    base = jnp.stack([c, m]).astype(jnp.int32)
    vectors = codes[:, 1:6, :ws].astype(F32).swapaxes(0, 1).reshape(5, 2, dh)
    head_vecs = jnp.where(first, vectors[:, 0], vectors[:, 1])


    content_cot, query_cot, unused = tie((content_cot, query_cot, content_full))
    cots = cross(jnp.stack([content_cot, query_cot], axis=1))

    position_bf, rel, rel_turned = relative(wr, length)
    queries = mm(inputs, wq)
    kv = mm(content_full, kv_weight).astype(BF)
    vec8 = jnp.pad(head_vecs, ((0, 3), (0, 0)))
    table = head_vecs[3:5].reshape(2, heads, DH).swapaxes(0, 1)
    table = jnp.where(jnp.arange(128) < 2 * NS, table[..., None], 0.0)
    late = hold(late[0], late[1], [content_full])
    late_near = [late] + [near(late, step) for step in range(1, m)]
    forward = []
    got_mixed = []
    for pair in range(pairs):
        after = [[late], [cots], late_near[1:]][min(pair, 2)]
        if pair == 2:
            *held, unused = tie((*late_near, forward[1][1]))
            late_theirs = [swap(x) for x in held]
        after = after + [f[1] for f in forward[-1:]]
        forward.append(
            attend_forward(
                pair,
                after,
                base,
                live,
                queries,
                vec8,
                table,
                info,
                reach,
                kv,
                hot,
                rel,
                key_ranks,
            )
        )
        got_mixed.append(swap(pick(forward[-1][3].reshape(2, groups * r, 128), 1 - k)))

    (
        result,
        grad_residual,
        mine_grad,
        other_grad,
        row_vecs,
        inner_vecs,
        early_mine,
        early_other,
        late_mine,
        late_other,
    ) = (dense if ws % 16 == 0 else dense_plain)(
        at,
        [f[3] for f in forward],
        got_mixed,
        inputs,
        cots.reshape(groups * r, d),
        late_near,
        late_theirs,
        ws,
        ff,
    )
    grad_heads = pair_of(mine_grad, swap(other_grad), k).reshape(groups * 2 * r, dh)

    backward = []

    def back(pair, after):
        f = forward[pair]
        after = after + [b[0] for b in backward[-1:]]
        backward.append(
            attend_backward(
                pair,
                after,
                base,
                live,
                f[0],
                queries,
                grad_heads,
                f[1],
                f[2],
                vec8,
                info,
                kv,
                hot,
                rel_turned,
            )
        )

    def near_fold(arrays, rows, after):
        parts = fold(at, [x.reshape(2, m, rows, x.shape[-1]) for x in arrays], after)
        return [parts[0]] + [near(parts[step], step) for step in range(1, m)]

    def cross_join(parts, after):
        return [across(x, e) for e, x in enumerate(join(at, parts, after))]

    def proj_some(some, extra, after):
        return proj_grads(
            inputs, content_full, position_bf, [backward[p] for p in some], extra, after
        ).reshape(groups, m, ws, -1)

    late_parts = near_fold([late_mine, swap(late_other)], fs, [])
    back(0, late_parts[:1])
    after = [backward[0][0]]
    early_parts = near_fold([early_mine, swap(early_other)], ws, after)
    late_cross = cross_join(late_parts, after)
    result, unused = tie((result, backward[0][0]))
    outs = cross(result.reshape(2, 2, r, d))
    back(1, [early_parts[0]])
    some_grads = proj_some(range(pairs - 1), [], early_parts[1:] + late_cross + [outs])
    some_parts = near_parts(some_grads, 1)
    early_cross = cross_join(early_parts, [])
    late_sum = add_up(late_cross, BF, [some_grads])
    late_got = swap(late_sum)
    back(2, [some_grads])

    small = jnp.concatenate([b[3][:5] for b in backward], axis=1)
    small = jnp.where(
        first,
        jnp.concatenate([small, jnp.zeros_like(small)], axis=1),
        jnp.concatenate([jnp.zeros_like(small), small], axis=1),
    )
    inner_vecs = inner_vecs[0].reshape(n, fs // ws, ws).swapaxes(1, 2).reshape(d, fs // ws)
    small = jnp.concatenate([small.T, row_vecs[:5].T, inner_vecs], axis=1)
    small = jnp.pad(small, ((0, 0), (0, 128 - small.shape[1]))).astype(BF)
    last_grads = proj_some([pairs - 1], [small], some_parts[1:] + early_cross + [late_got])
    early_sum = add_up(early_cross, BF, [last_grads])
    late_sum, late_got, unused = tie((late_sum, late_got, last_grads))
    early_got = swap(early_sum)
    last_parts = near_parts(last_grads, 1)
    which = [jnp.asarray(x, jnp.int32).reshape(1) for x in (k, 1 - k)]
    dkv_parts = [b[1] for b in backward]
    dq_parts = [b[0] for b in backward]
    got_kv = swap(input_grad(which[1], dkv_parts, kv_weight, BF, [last_grads], True))
    got_q = swap(input_grad(which[1], dq_parts, wq, BF, [last_grads]))
    own_kv = input_grad(which[0], dkv_parts, kv_weight, F32, [last_grads], True)
    own_q = input_grad(which[0], dq_parts, wq, F32, [last_grads])
    content_parts = near_fold([own_kv, got_kv], r, [own_q, early_got] + last_parts[1:])
    q_sum = own_q + got_q.astype(F32) + grad_residual
    q_sum = q_sum.reshape(2, 2, r, d)
    query_rows, unused = tie((q_sum[:, 1].astype(BF), content_parts[1]))
    query_grads = cross(query_rows)
    late_total = late_sum.astype(F32) + late_got.astype(F32)
    content_sum = sum([x.astype(F32) for x in content_parts]) + q_sum[:, 0]
    content_grads = cross(content_sum.astype(BF))
    some_near, last_near = [
        add_up(parts, BF, content_parts[:1]) for parts in (some_parts, last_parts)
    ]
    proj_sum = far_sum(jnp.concatenate([some_near, last_near], axis=2))

    early_total = early_sum.astype(F32) + early_got.astype(F32)
    bit = 2
    while bit < nr:
        turn = [(i, i ^ bit) for i in range(nr)]
        early_total = early_total + lax.ppermute(early_total, "rep", turn)
        late_total = late_total + lax.ppermute(late_total, "rep", turn)
        proj_sum = proj_sum + lax.ppermute(proj_sum, "rep", turn)
        bit *= 2
    proj_other = swap(proj_sum)
    halves = jnp.where(first, proj_sum, proj_other), jnp.where(first, proj_other, proj_sum)

    def columns(index):
        return jnp.concatenate(
            [
                x[:, 512 * p + 128 * index : 512 * p + 128 * index + 128]
                for x in halves
                for p in range(pairs)
            ],
            axis=1,
        )

    head_cols = (proj_sum + proj_other)[:, 512 * pairs :]
    vec_cols = head_cols[:, 5:]
    return (
        outs[:, 0],
        outs[:, 1],
        content_grads,
        query_grads,
        columns(0),
        columns(1),
        columns(2),
        columns(3),
        early_total[:, ff : ff + d],
        early_total[:, :ff],
        late_total,
        vec_cols[:, 5 : 5 + fs // ws].T.reshape(fs),
        vec_cols[:, 0],
        vec_cols[:, 1],
        vec_cols[:, 2],
        vec_cols[:, 3],
        vec_cols[:, 4],
        head_cols[:, 0],
        head_cols[:, 1],
        head_cols[:, 2],
        head_cols[:, 3:5].T,
    )


def solution(mesh):
    in_specs = (
        P("rep", "shard", None),
        P("rep", "shard", None),
        P("rep", "shard"),
        P("rep", None),
        P("rep", "shard"),
        P("rep", "shard"),
        P("shard", None),
        P("shard", None),
        P("shard", None),
        P("shard", None),
        P("shard", None),
        P("shard", None),
        P("shard", None),
        P("shard"),
        P("shard"),
        P("shard"),
        P("shard"),
        P("shard"),
        P("shard"),
        P("shard"),
        P("shard"),
        P("shard"),
        P(None, "shard"),
        P("rep", "shard", None),
        P("rep", "shard", None),
    )
    out_specs = (
        P("rep", "shard", None),
        P("rep", "shard", None),
        P("rep", "shard", None),
        P("rep", "shard", None),
        P("shard", None),
        P("shard", None),
        P("shard", None),
        P("shard", None),
        P("shard", None),
        P("shard", None),
        P("shard", None),
        P("shard"),
        P("shard"),
        P("shard"),
        P("shard"),
        P("shard"),
        P("shard"),
        P("shard"),
        P("shard"),
        P("shard"),
        P(None, "shard"),
    )
    return jax.shard_map(body, mesh=mesh, in_specs=in_specs, out_specs=out_specs, check_vma=False)
```

```python
import functools
import math

import jax
import jax.numpy as jnp
from jax import lax
from jax.experimental import pallas as pl
from jax.experimental.pallas import tpu as pltpu
from jax.sharding import PartitionSpec as P

DH = 64
NS = 13
EPSILON = 1e-05
NEG = -1e30
F32 = jnp.float32
BF = jnp.bfloat16
HIGHEST = lax.Precision.HIGHEST

R = 128
KB = 256
W = R + KB
SCALE = DH**-0.5
LOG2E = 1.4426950408889634
LN2 = 0.6931471805599453
VMEM = 60 * 2**20
SMALL = 32 * 2**20
ONES = 32


def mm(a, b, ca=1, cb=0, precision=None):
    return lax.dot_general(
        a, b, (((ca,), (cb,)), ((), ())), preferred_element_type=F32, precision=precision
    )


def row_features(seg_col):
    lane = lax.broadcasted_iota(jnp.int32, (2 * R, 128), 1)
    folded = jnp.where(lane < NS, lane, lane - NS).astype(F32)
    return jnp.where((lane < 2 * NS) & (folded == seg_col), 1.0, 0.0)


def live_list(live_ref, list_ref, row, nkb):
    per = KB // R

    def step(kb, count):
        list_ref[count] = kb
        live = live_ref[row, kb * per]
        for i in range(1, per):
            live = jnp.maximum(live, live_ref[row, kb * per + i])
        return count + live

    return lax.fori_loop(0, nkb, step, 0)


def ordered(kernel, count, extra):
    def run(*refs):
        kernel(*refs[:count], *refs[count + extra :])

    return run


def reversal():
    down = lax.broadcasted_iota(jnp.int32, (KB, KB), 0)
    across = lax.broadcasted_iota(jnp.int32, (KB, KB), 1)
    return jnp.where(down + across == KB - 1, 1.0, 0.0).astype(BF)


def by_two(count, work):
    def step(i, carry):
        work([2 * i, 2 * i + 1])
        return carry

    lax.fori_loop(0, count // 2, step, 0)

    @pl.when(count % 2 == 1)
    def last():
        work([count - 1])


def forward_kernel(
    nkb,
    base_ref,
    live_ref,
    q_ref,
    vec_ref,
    table_ref,
    info_ref,
    reach_ref,
    kv_ref,
    hot_ref,
    rel_ref,
    rank_ref,
    p_ref,
    o_ref,
    inv_ref,
    ob_ref,
    qq_scr,
    qr_scr,
    s_scr,
    m_scr,
    acc_scr,
    flip_scr,
    list_scr,
):
    block = pl.program_id(0)

    @pl.when(block == 0)
    def start():
        flip_scr[...] = reversal()

    row = base_ref[0] + base_ref[1] * block
    base = nkb * KB - R - R * row
    count = live_list(live_ref, list_scr, row, nkb)
    seg_col = info_ref[:, 0:1]
    limit = info_ref[:, 1:2]
    hot_row = row_features(seg_col)
    lane = lax.broadcasted_iota(jnp.int32, (2 * R, 128), 1)
    reach = mm(jnp.where(lane < NS, hot_row, 0.0).astype(BF), reach_ref[...])
    outside = jnp.where((lane < 2 * NS) & (reach < 0.5), NEG, 0.0)
    zero = jnp.zeros((2 * R, DH), BF)
    for h in range(2):
        half = slice(DH * h, DH * h + DH)
        q = q_ref[:, half]
        plain = ((q + vec_ref[0:1, half]) * (SCALE * LOG2E)).astype(BF)
        place = ((q + vec_ref[1:2, half]) * (SCALE * LOG2E)).astype(BF)
        label = q + vec_ref[2:3, half]
        top_part = label.astype(BF)
        rest = (label - top_part.astype(F32)).astype(BF)
        both = mm(jnp.concatenate([top_part, rest], axis=1), table_ref[h])
        same, other = both[:, :128], both[:, 128:]
        term = jnp.where(hot_row > 0.5, same, other) * (SCALE * LOG2E) + outside
        high = term.astype(BF).astype(F32)
        extra = jnp.where(lane < NS, high, jnp.where(lane < 2 * NS, term - high, 0.0))
        side = lambda x: [x, zero] if h == 0 else [zero, x]
        qq_scr[h] = jnp.concatenate(side(plain) + [extra.astype(BF)], axis=1)
        qr_scr[h] = jnp.concatenate(side(place), axis=1)
    m_scr[...] = jnp.full(m_scr.shape, -jnp.inf, F32)
    acc_scr[...] = jnp.zeros(acc_scr.shape, F32)

    def score(blocks):
        highest = [m_scr[h] for h in range(2)]
        for n in blocks:
            k0 = pl.multiple_of(list_scr[n] * KB, KB)
            ok = rank_ref[:, pl.ds(k0, KB)] <= limit
            window = rel_ref[pl.ds(pl.multiple_of(base + k0, 128), W), :]
            keys = jnp.concatenate(
                [kv_ref[pl.ds(k0, KB), :128], hot_ref[pl.ds(k0, KB), :]], axis=1
            )
            for h in range(2):
                s = mm(qq_scr[h], keys, 1, 1)
                full = mm(qr_scr[h], window, 1, 1)
                shifted = [
                    pltpu.roll(
                        full[i * R : i * R + R], W - (R - 1), 1, stride=1, stride_axis=0
                    )[:, :KB]
                    for i in range(2)
                ]
                s = jnp.where(ok, s + jnp.concatenate(shifted, axis=0), NEG)
                s_scr[h, n] = s
                highest[h] = jnp.maximum(highest[h], jnp.maximum(s[:, :128], s[:, 128:]))
        for h in range(2):
            m_scr[h] = highest[h]

    by_two(count, score)
    top = [jnp.max(m_scr[h], axis=1, keepdims=True) for h in range(2)]

    def mix(blocks):
        totals = [0.0, 0.0]
        for n in blocks:
            k0 = pl.multiple_of(list_scr[n] * KB, KB)
            values = jnp.concatenate(
                [kv_ref[pl.ds(k0, KB), 128:], hot_ref[pl.ds(k0, KB), :]], axis=1
            )
            for h in range(2):
                p = jnp.exp2(s_scr[h, n] - top[h]).astype(BF)
                p_ref[0, h, n] = mm(p, flip_scr[...]).astype(BF)
                totals[h] += mm(p, values)
        for h in range(2):
            acc_scr[h] += totals[h]

    by_two(count, mix)
    for h in range(2):
        half = slice(DH * h, DH * h + DH)
        acc = acc_scr[h]
        inverse = 1.0 / acc[:, 128 + ONES : 129 + ONES]
        mixed = acc[:, half] * inverse
        o_ref[:, half] = mixed
        ob_ref[:, half] = mixed.astype(BF)
        inv_ref[:, half] = jnp.broadcast_to(inverse, (2 * R, DH))


def attend_forward(pair, after, base, live, q, vec, table, info, reach, kv, hot, rel, rank):
    nb = q.shape[0] // (2 * R)
    length = kv.shape[0]
    nkb = length // KB
    whole = lambda *shape: pl.BlockSpec(shape, lambda b, *_: (0,) * len(shape))
    return pl.pallas_call(
        ordered(functools.partial(forward_kernel, nkb), 11, len(after)),
        grid_spec=pltpu.PrefetchScalarGridSpec(
            num_scalar_prefetch=2,
            grid=(nb,),
            in_specs=[
                pl.BlockSpec((2 * R, 128), lambda b, *_: (b, pair)),
                pl.BlockSpec((8, 128), lambda b, *_: (0, pair)),
                pl.BlockSpec((2, 2 * DH, 256), lambda b, *_: (pair, 0, 0)),
                pl.BlockSpec((2 * R, 128), lambda b, *_: (b, 0)),
                whole(128, 128),
                pl.BlockSpec((length, 256), lambda b, *_: (0, pair)),
                whole(length, 128),
                pl.BlockSpec((2 * length, 128), lambda b, *_: (0, pair)),
                whole(1, length),
            ]
            + [pl.BlockSpec(memory_space=pl.ANY)] * len(after),
            out_specs=[
                pl.BlockSpec((1, 2, nkb, 2 * R, KB), lambda b, *_: (b, 0, 0, 0, 0)),
                pl.BlockSpec((2 * R, 128), lambda b, *_: (b, 0)),
                pl.BlockSpec((2 * R, 128), lambda b, *_: (b, 0)),
                pl.BlockSpec((2 * R, 128), lambda b, *_: (b, 0)),
            ],
            scratch_shapes=[
                pltpu.VMEM((2, 2 * R, 256), BF),
                pltpu.VMEM((2, 2 * R, 128), BF),
                pltpu.VMEM((2, nkb, 2 * R, KB), F32),
                pltpu.VMEM((2, 2 * R, 128), F32),
                pltpu.VMEM((2, 2 * R, 256), F32),
                pltpu.VMEM((KB, KB), BF),
                pltpu.SMEM((nkb + 1,), jnp.int32),
            ],
        ),
        out_shape=[
            jax.ShapeDtypeStruct((nb, 2, nkb, 2 * R, KB), BF),
            jax.ShapeDtypeStruct((q.shape[0], 128), F32),
            jax.ShapeDtypeStruct((q.shape[0], 128), F32),
            jax.ShapeDtypeStruct((q.shape[0], 128), BF),
        ],
        compiler_params=pltpu.CompilerParams(
            dimension_semantics=("arbitrary",), vmem_limit_bytes=VMEM
        ),
        cost_estimate=pl.CostEstimate(
            flops=10**8, bytes_accessed=10**6, transcendentals=0
        ),
        name="attend_forward",
    )(base, live, q, vec, table, info, reach, kv, hot, rel, rank, *after)


def backward_kernel(
    nkb,
    nb,
    base_ref,
    live_ref,
    p_ref,
    q_ref,
    g_ref,
    o_ref,
    inv_ref,
    vec_ref,
    info_ref,
    kv_ref,
    hot_ref,
    rel_ref,
    dq_ref,
    dkv_ref,
    drel_ref,
    small_ref,
    turn_scr,
    dd_scr,
    acc_scr,
    accr_scr,
    dkv_scr,
    drel_scr,
    keys_scr,
    flip_scr,
    list_scr,
):
    block = pl.program_id(0)
    length = nkb * KB
    row = base_ref[0] + base_ref[1] * block
    base = nkb * KB - R - R * row
    count = live_list(live_ref, list_scr, row, nkb)

    @pl.when(block == 0)
    def start():
        dkv_scr[...] = jnp.zeros(dkv_scr.shape, F32)
        drel_scr[...] = jnp.zeros(drel_scr.shape, F32)
        small_ref[...] = jnp.zeros(small_ref.shape, F32)
        flip = reversal()
        flip_scr[...] = flip
        for kb in range(nkb):
            rows = slice(kb * KB, (kb + 1) * KB)
            keys_scr[rows, :256] = mm(flip, kv_ref[rows, :]).astype(BF)
            keys_scr[rows, 256:] = mm(flip, hot_ref[rows, :]).astype(BF)

    lane = lax.broadcasted_iota(jnp.int32, (2 * R, 128), 1)
    zero = jnp.zeros((2 * R, DH), BF)
    for h in range(2):
        half = slice(DH * h, DH * h + DH)
        q = q_ref[:, half]
        plain = (q + vec_ref[0:1, half]) * (SCALE * LOG2E)
        place = (q + vec_ref[1:2, half]) * (SCALE * LOG2E)
        g = g_ref[:, half].astype(F32)
        inverse = inv_ref[:, DH * h : DH * h + 1]
        delta = -jnp.sum(g * o_ref[:, half], axis=1, keepdims=True) * inverse
        high = delta.astype(BF).astype(F32)
        extra = jnp.where(lane == ONES, high, jnp.where(lane == ONES + 1, delta - high, 0.0))
        side = lambda x: [x, zero] if h == 0 else [zero, x]
        scaled = g * inverse
        dd_scr[h] = jnp.concatenate(side(scaled.astype(BF)) + [extra.astype(BF)], axis=1)
        for i, x in enumerate((plain, scaled, place)):
            turn_scr[h, i] = x.T.astype(BF)
    acc_scr[...] = jnp.zeros(acc_scr.shape, F32)
    accr_scr[...] = jnp.zeros(accr_scr.shape, F32)

    def step(blocks):
        pad = jnp.zeros((R, W - KB), F32)
        d_query = [0.0, 0.0]
        d_place = [0.0, 0.0]
        for n in blocks:
            k0 = pl.multiple_of(list_scr[n] * KB, KB)
            r0 = pl.multiple_of(2 * length - base - k0 - W, 128)
            window = rel_ref[pl.ds(r0, W), :]
            keys = jnp.concatenate(
                [keys_scr[pl.ds(k0, KB), :128], keys_scr[pl.ds(k0, KB), 256:]], axis=1
            )
            values = keys_scr[pl.ds(k0, KB), 128:]
            for h in range(2):
                p = p_ref[0, h, n]
                wide = p.astype(F32) * mm(dd_scr[h], values, 1, 1)
                ds = wide.astype(BF)
                d_query[h] += mm(ds, keys)
                full = [
                    pltpu.roll(
                        jnp.concatenate([wide[i * R : i * R + R], pad], axis=1),
                        0,
                        1,
                        stride=1,
                        stride_axis=0,
                    )
                    for i in range(2)
                ]
                full = jnp.concatenate(full, axis=0).astype(BF)
                d_place[h] += mm(full, window)
                low, high = DH * h, DH * h + DH
                dkv_scr[low:high, pl.ds(k0, KB)] += mm(turn_scr[h, 0], ds)
                dkv_scr[128 + low : 128 + high, pl.ds(k0, KB)] += mm(turn_scr[h, 1], p)
                drel_scr[low:high, pl.ds(r0, W)] += mm(turn_scr[h, 2], full)
        for h in range(2):
            acc_scr[h] += d_query[h]
            accr_scr[h] += d_place[h]

    by_two(count, step)
    hot_row = row_features(info_ref[:, 0:1])
    for h in range(2):
        half = slice(DH * h, DH * h + DH)
        acc = acc_scr[h]
        d_plain = acc[:, half] * SCALE
        d_place = accr_scr[h][:, half] * SCALE
        sums = jnp.where(lane < NS, acc[:, 128:], 0.0) * SCALE
        same = jnp.sum(sums * hot_row, axis=1, keepdims=True)
        other = jnp.sum(sums, axis=1, keepdims=True) - same
        d_label = same * vec_ref[3:4, half] + other * vec_ref[4:5, half]
        label = q_ref[:, half] + vec_ref[2:3, half]
        dq_ref[:, half] = (d_plain + d_place + d_label).astype(BF)
        terms = [d_plain, d_place, d_label, same * label, other * label]
        for row, term in enumerate(terms):
            small_ref[row : row + 1, half] += jnp.sum(term, axis=0, keepdims=True)

    @pl.when(block == nb - 1)
    def finish():
        down = lax.broadcasted_iota(jnp.int32, (256, KB), 0)
        factor = jnp.where(down < 128, LN2, 1.0)
        for kb in range(nkb):
            cols = slice(kb * KB, (kb + 1) * KB)
            dkv_ref[:, cols] = mm((dkv_scr[:, cols] * factor).astype(BF), flip_scr[...]).astype(BF)
        drel_ref[...] = (drel_scr[...] * LN2).astype(BF)


def attend_backward(pair, after, base, live, p, q, g, o, inv, vec, info, kv, hot, rel):
    nb = q.shape[0] // (2 * R)
    length = kv.shape[0]
    nkb = length // KB
    own = pl.BlockSpec((2 * R, 128), lambda b, *_: (b, 0))
    rows = pl.BlockSpec((2 * R, 128), lambda b, *_: (b, pair))
    return pl.pallas_call(
        ordered(functools.partial(backward_kernel, nkb, nb), 12, len(after)),
        grid_spec=pltpu.PrefetchScalarGridSpec(
            num_scalar_prefetch=2,
            grid=(nb,),
            in_specs=[
                pl.BlockSpec((1, 2, nkb, 2 * R, KB), lambda b, *_: (b, 0, 0, 0, 0)),
                rows,
                rows,
                own,
                own,
                pl.BlockSpec((8, 128), lambda b, *_: (0, pair)),
                pl.BlockSpec((2 * R, 128), lambda b, *_: (b, 0)),
                pl.BlockSpec((length, 256), lambda b, *_: (0, pair)),
                pl.BlockSpec((length, 128), lambda b, *_: (0, 0)),
                pl.BlockSpec((2 * length, 128), lambda b, *_: (0, pair)),
            ]
            + [pl.BlockSpec(memory_space=pl.ANY)] * len(after),
            out_specs=[
                own,
                pl.BlockSpec((256, length), lambda b, *_: (0, 0)),
                pl.BlockSpec((128, 2 * length), lambda b, *_: (0, 0)),
                pl.BlockSpec((8, 128), lambda b, *_: (0, 0)),
            ],
            scratch_shapes=[
                pltpu.VMEM((2, 3, DH, 2 * R), BF),
                pltpu.VMEM((2, 2 * R, 256), BF),
                pltpu.VMEM((2, 2 * R, 256), F32),
                pltpu.VMEM((2, 2 * R, 128), F32),
                pltpu.VMEM((256, length), F32),
                pltpu.VMEM((128, 2 * length), F32),
                pltpu.VMEM((length, 384), BF),
                pltpu.VMEM((KB, KB), BF),
                pltpu.SMEM((nkb + 1,), jnp.int32),
            ],
        ),
        out_shape=[
            jax.ShapeDtypeStruct((q.shape[0], 128), BF),
            jax.ShapeDtypeStruct((256, length), BF),
            jax.ShapeDtypeStruct((128, 2 * length), BF),
            jax.ShapeDtypeStruct((8, 128), F32),
        ],
        compiler_params=pltpu.CompilerParams(
            dimension_semantics=("arbitrary",), vmem_limit_bytes=VMEM
        ),
        cost_estimate=pl.CostEstimate(
            flops=10**8, bytes_accessed=10**6, transcendentals=0
        ),
        name="attend_backward",
    )(base, live, p, q, g, o, inv, vec, info, kv, hot, rel, *after)


def whole_block(x):
    return pl.BlockSpec(x.shape, lambda i: (0,) * len(x.shape))


def pack_kernel(r, ws, low_ref, content_ref, seg_ref, rank_ref, flag_ref, parent_ref, *refs):
    vec_refs, weight_refs, (a_ref, b_ref, scr) = refs[:4], refs[4:8], refs[8:]
    low = low_ref[0]
    for e, out in enumerate((a_ref, b_ref)):
        tree = jnp.bitwise_xor(low, e)
        out[:r, :] = content_ref[tree]
        scr[...] = jnp.zeros(scr.shape, F32)
        row = lambda ref: ref[pl.ds(tree, 1), :]
        rank = row(rank_ref)
        scr[0:1, :r] = row(seg_ref).astype(F32)
        scr[0:1, r : 2 * r] = lax.shift_right_logical(rank, 6).astype(F32)
        scr[0:1, 2 * r : 3 * r] = jnp.bitwise_and(rank, 63).astype(F32)
        scr[0:1, 3 * r : 4 * r] = row(flag_ref).astype(F32)
        scr[0:1, 4 * r : 4 * r + NS] = row(parent_ref).astype(F32)
        for i in range(3):
            scr[i + 1 : i + 2, :ws] = vec_refs[i][...].astype(F32)
        scr[4:6, :ws] = vec_refs[3][...].astype(F32)
        out[r : r + 16, :] = scr[...].astype(BF)
        for i in range(4):
            out[r + 16 + i * ws : r + 16 + (i + 1) * ws, :] = weight_refs[i][...]


def pack(low, content, segs, ranks, flags, parents, vecs, weights):
    trees, r, d = content.shape
    ws = weights[0].shape[0]
    shape = jax.ShapeDtypeStruct((r + 16 + 4 * ws, d), BF)
    return pl.pallas_call(
        functools.partial(pack_kernel, r, ws),
        grid=(1,),
        in_specs=[pl.BlockSpec(memory_space=pltpu.SMEM), whole_block(content)]
        + [whole_block(x) for x in (segs, ranks, flags, parents, *vecs, *weights)],
        out_specs=[whole_block(shape)] * 2,
        out_shape=[shape, shape],
        scratch_shapes=[pltpu.VMEM((16, d), F32)],
        compiler_params=pltpu.CompilerParams(vmem_limit_bytes=VMEM),
        name="pack",
    )(low, content, segs, ranks, flags, parents, *vecs, *weights)


def assemble_kernel(r, ws, dh, m, at_ref, a0, a1, t0, t1, q_own, q_other, *outs):
    content_ref, codes_ref, wq_ref, wkv_ref, wr_ref, inputs_ref = outs
    k, low, c = at_ref[0], at_ref[1], at_ref[2]
    h, zl = pl.program_id(0), pl.program_id(1)
    column = lambda start: pl.multiple_of(k * dh + start, 128)

    def fill(src, query):
        inputs_ref[0, 0, 0] = src[0, :r, :]
        inputs_ref[0, 0, 1] = query[...]
        for step in range(m):
            to = jnp.bitwise_xor(c, step)
            rows = lambda i: slice(r + 16 + i * ws, r + 16 + (i + 1) * ws)
            content_ref[0, 0, to] = src[step, :r, :]
            codes_ref[0, 0, to] = src[step, r : r + 16, :]
            wq_ref[0, 0, to] = src[step, rows(0), pl.ds(column(0), dh)]
            wr_ref[0, 0, to] = src[step, rows(3), pl.ds(column(0), dh)]
            for p in range(dh // 128):
                for i in range(2):
                    wkv_ref[0, 0, to, :, 256 * p + 128 * i : 256 * p + 128 * i + 128] = src[
                        step, rows(1 + i), pl.ds(column(128 * p), 128)
                    ]

    for mine in (True, False):
        for e in range(2):
            src = ((a0, a1) if mine else (t0, t1))[e]
            query = (q_own if mine else q_other).at[e]

            @pl.when(((h == k) == mine) & (jnp.bitwise_xor(zl, low) == e))
            def case(src=src, query=query):
                fill(src, query)


def assemble(at, near_rows, their_rows, q_own, q_other, r, ws, after):
    m, rows, d = near_rows[0].shape
    dh = d // 2
    sizes = [(m, r, d), (m, 16, d), (m, ws, dh), (m, ws, d), (m, ws, dh), (2, r, d)]
    return pl.pallas_call(
        ordered(functools.partial(assemble_kernel, r, ws, dh, m), 7, len(after)),
        grid=(2, 2),
        in_specs=[pl.BlockSpec(memory_space=pltpu.SMEM)]
        + [pl.BlockSpec((m, rows, d), lambda h, z: (0, 0, 0))] * 4
        + [pl.BlockSpec((2, r, d), lambda h, z: (0, 0, 0))] * 2
        + [pl.BlockSpec(memory_space=pl.ANY)] * len(after),
        out_specs=[pl.BlockSpec((1, 1) + size, lambda h, z: (h, z, 0, 0, 0)) for size in sizes],
        out_shape=[jax.ShapeDtypeStruct((2, 2) + size, BF) for size in sizes],
        compiler_params=pltpu.CompilerParams(vmem_limit_bytes=SMALL),
        name="assemble",
    )(at, *near_rows, *their_rows, q_own, q_other, *after)


def pack_late_kernel(ws, w1_ref, wo_ref, w2_ref, *refs):
    vec_refs, out, scr = refs[:-2], refs[-2], refs[-1]
    d = wo_ref.shape[1]
    parts = w1_ref.shape[1] // d
    for j in range(parts):
        out[j * ws : (j + 1) * ws, :] = w1_ref[:, j * d : (j + 1) * d]
    out[parts * ws : (parts + 1) * ws, :] = wo_ref[...]
    out[(parts + 1) * ws : (2 * parts + 1) * ws, :] = w2_ref[...]
    scr[...] = jnp.zeros(scr.shape, F32)
    row = 0
    for ref in vec_refs:
        scr[row : row + ref.shape[0], : ref.shape[1]] = ref[...].astype(F32)
        row += ref.shape[0]
    out[(2 * parts + 1) * ws :, :] = scr[...].astype(BF)


def pack_late(w1, wo, w2, vecs):
    ws, d = wo.shape
    rows = ws + w1.shape[1] // d * ws + w2.shape[0] + 16
    return pl.pallas_call(
        functools.partial(pack_late_kernel, ws),
        grid=(1,),
        in_specs=[whole_block(x) for x in (w1, wo, w2, *vecs)],
        out_specs=pl.BlockSpec((rows, d), lambda i: (0, 0)),
        out_shape=jax.ShapeDtypeStruct((rows, d), BF),
        scratch_shapes=[pltpu.VMEM((16, d), F32)],
        compiler_params=pltpu.CompilerParams(vmem_limit_bytes=SMALL),
        name="pack_late",
    )(w1, wo, w2, *vecs)


def assemble_late_kernel(ws, m, at_ref, *refs):
    mine_refs, their_refs, (w1_ref, wo_ref, w2_ref, vec_ref) = refs[:m], refs[m : 2 * m], refs[2 * m :]
    k, low, c = at_ref[0], at_ref[1], at_ref[2]
    h, zl = pl.program_id(0), pl.program_id(1)
    d = wo_ref.shape[-1]
    parts = w1_ref.shape[-1] // d
    e = jnp.bitwise_xor(zl, low)

    def fill(refs):
        for step, src in enumerate(refs):
            to = jnp.bitwise_xor(c, step)
            for j in range(parts):
                w1_ref[0, 0, to, :, j * d : (j + 1) * d] = src[e, j * ws : (j + 1) * ws, :]
            wo_ref[0, 0, to] = src[e, parts * ws : (parts + 1) * ws, :]
            w2_ref[0, 0, to] = src[e, (parts + 1) * ws : (2 * parts + 1) * ws, :]
            vec_ref[0, 0, to] = src[e, (2 * parts + 1) * ws :, :]

    @pl.when(h == k)
    def own():
        fill(mine_refs)

    @pl.when(h != k)
    def other():
        fill(their_refs)


def assemble_late(at, mine, theirs, ws, parts):
    m = len(mine)
    two, rows, d = mine[0].shape
    sizes = [(m, ws, parts * d), (m, ws, d), (m, parts * ws, d), (m, 16, d)]
    return pl.pallas_call(
        functools.partial(assemble_late_kernel, ws, m),
        grid=(2, 2),
        in_specs=[pl.BlockSpec(memory_space=pltpu.SMEM)]
        + [pl.BlockSpec((2, rows, d), lambda h, z: (0, 0, 0))] * (2 * m),
        out_specs=[pl.BlockSpec((1, 1) + size, lambda h, z: (h, z, 0, 0, 0)) for size in sizes],
        out_shape=[jax.ShapeDtypeStruct((2, 2) + size, BF) for size in sizes],
        compiler_params=pltpu.CompilerParams(vmem_limit_bytes=SMALL),
        name="assemble_late",
    )(at, *mine, *theirs)


def relative_kernel(sa_ref, ca_ref, sb_ref, cb_ref, w_ref, pos_ref, rel_ref, turned_ref):
    half = sb_ref.shape[1]
    fine = sb_ref.shape[0]
    for i in range(KB // fine):
        rows = slice(i * fine, (i + 1) * fine)
        sa, ca = sa_ref[0, i : i + 1, :], ca_ref[0, i : i + 1, :]
        sine = sa * cb_ref[...] - ca * sb_ref[...]
        cosine = ca * cb_ref[...] + sa * sb_ref[...]
        pos_ref[rows, :half] = sine.astype(BF)
        pos_ref[rows, half:] = cosine.astype(BF)
    from_sine = mm(pos_ref[:, :half], w_ref[:half, :])
    from_cosine = mm(pos_ref[:, half:], w_ref[half:, :])
    rel_ref[...] = (from_cosine + from_sine).astype(BF)
    turned_ref[...] = (from_cosine - from_sine).astype(BF)


def relative(wr, length):
    d, width = wr.shape
    half, fine = d // 2, 64
    powers = jnp.arange(half, dtype=F32) * (2.0 / d)
    inverse_freq = 1.0 / 10000.0**powers
    coarse = (length - 1 - fine * jnp.arange(2 * length // fine, dtype=jnp.int32)).astype(F32)
    a = coarse[:, None] * inverse_freq[None]
    b = jnp.arange(fine, dtype=F32)[:, None] * inverse_freq[None]
    per = KB // fine
    tables = [jnp.sin(a).reshape(-1, per, half), jnp.cos(a).reshape(-1, per, half), jnp.sin(b), jnp.cos(b)]
    rows = lambda w: pl.BlockSpec((KB, w), lambda i: (i, 0))
    return pl.pallas_call(
        relative_kernel,
        grid=(2 * length // KB,),
        in_specs=[pl.BlockSpec((1, per, half), lambda i: (i, 0, 0))] * 2
        + [pl.BlockSpec((fine, half), lambda i: (0, 0))] * 2
        + [pl.BlockSpec((d, width), lambda i: (0, 0))],
        out_specs=[rows(d), rows(width), rows(width)],
        out_shape=[
            jax.ShapeDtypeStruct((2 * length, d), BF),
            jax.ShapeDtypeStruct((2 * length, width), BF),
            jax.ShapeDtypeStruct((2 * length, width), BF),
        ],
        compiler_params=pltpu.CompilerParams(vmem_limit_bytes=SMALL),
        cost_estimate=pl.CostEstimate(
            flops=4 * length * d * width, bytes_accessed=8 * length * d, transcendentals=0
        ),
        name="relative",
    )(*tables, wr)


def input_grad_kernel(count, turned, at_ref, *refs):
    parts, w_ref, out_ref = refs[:count], refs[count], refs[-1]
    total = 0.0
    start = 0
    for ref in parts:
        width = ref.shape[0 if turned else 1]
        total += mm(ref[...], w_ref[:, start : start + width], 0 if turned else 1, 1)
        start += width
    out_ref[...] = total.astype(out_ref.dtype)


def input_grad(half, parts, w, dtype, after, turned=False):
    rows = parts[0].shape[1 if turned else 0] // 2
    block = math.gcd(rows, 256)
    blocks = rows // block
    d = w.shape[0]
    return pl.pallas_call(
        ordered(
            functools.partial(input_grad_kernel, len(parts), turned), len(parts) + 2, len(after)
        ),
        grid_spec=pltpu.PrefetchScalarGridSpec(
            num_scalar_prefetch=1,
            grid=(rows // block,),
            in_specs=[
                pl.BlockSpec((x.shape[0], block), lambda i, at: (0, at[0] * blocks + i))
                if turned
                else pl.BlockSpec((block, x.shape[1]), lambda i, at: (at[0] * blocks + i, 0))
                for x in parts
            ]
            + [pl.BlockSpec(w.shape, lambda i, at: (0, 0))]
            + [pl.BlockSpec(memory_space=pl.ANY)] * len(after),
            out_specs=pl.BlockSpec((block, d), lambda i, at: (i, 0)),
        ),
        out_shape=jax.ShapeDtypeStruct((rows, d), dtype),
        compiler_params=pltpu.CompilerParams(vmem_limit_bytes=SMALL),
        cost_estimate=pl.CostEstimate(
            flops=2 * rows * d * w.shape[1], bytes_accessed=4 * rows * d, transcendentals=0
        ),
        name="input_grad",
    )(half, *parts, w, *after)


def mask_kernel(n, m, r, c_ref, codes_ref, rank_ref, hot_ref, info_ref, reach_ref, live_ref):
    c = c_ref[0]
    iota = lambda shape, axis: lax.broadcasted_iota(jnp.int32, shape, axis)
    choose = iota((n, 16 * n), 1) == 16 * iota((n, 16 * n), 0)
    rows = mm(choose.astype(F32).astype(BF), codes_ref[...])
    part = lambda i: rows[:, i * r : (i + 1) * r]
    segs = part(0)
    ranks = part(1) * 64.0 + part(2)
    flags = part(3)
    seg_cols, rank_cols, flag_cols = segs.T, ranks.T, flags.T
    parent_col = rows[:, 4 * r : 4 * r + 128].T[:, 0:1]
    lane = iota((128, 128), 1)
    down = iota((128, 128), 0)
    feature = jnp.where(lane < NS, lane, jnp.where(lane < 2 * NS, lane - NS, -1))
    folded = feature.astype(F32)
    ones_lane = (lane == ONES) | (lane == ONES + 1)
    for i in range(n):
        rank_ref[0:1, i * r : (i + 1) * r] = ranks[i : i + 1, :]
        hit = (folded == seg_cols[:, i : i + 1]) | ones_lane
        hot_ref[i * r : (i + 1) * r, :] = jnp.where(hit, 1.0, 0.0).astype(BF)
    mine = iota((r, n), 1)
    for b in range(n // m):
        column = lambda x: jnp.sum(jnp.where(mine == b * m + c, x, 0.0), axis=1, keepdims=True)
        seg, limit = column(seg_cols), column(rank_cols)
        lower = limit - column(flag_cols)
        for i, value in enumerate((limit, lower)):
            start = (2 * b + i) * r
            info_ref[start : start + r, :] = jnp.where(lane == 0, seg, value)
    inside = (down < NS) & (lane < NS)
    link = inside & ((down == lane) | (parent_col == lane.astype(F32)))
    reached = jnp.where(link, 1.0, 0.0)
    for repeat in range(4):
        half = reached.astype(BF)
        reached = jnp.minimum(mm(half, half), 1.0)
    reached = reached.astype(BF)
    twice = jnp.where(down == feature, 1.0, 0.0).astype(BF)
    reach_ref[...] = mm(reached, twice).astype(BF)
    spot = iota((n, 128), 1)
    present = jnp.zeros((n, 128), F32)
    for t in range(NS):
        any_t = jnp.max(jnp.where(segs == t, 1.0, 0.0), axis=1, keepdims=True)
        present = jnp.where(spot == t, any_t, present)
    present = present.astype(BF)
    seen = jnp.minimum(mm(present, reached), 1.0).astype(BF)
    live_ref[...] = jnp.minimum(mm(seen, present, 1, 1), 1.0).astype(jnp.int32)


def masks(c, codes, m, r):
    n, length = codes.shape[0] // 16, codes.shape[0] // 16 * r
    return pl.pallas_call(
        functools.partial(mask_kernel, n, m, r),
        grid=(1,),
        in_specs=[pl.BlockSpec(memory_space=pltpu.SMEM), whole_block(codes)],
        out_specs=[
            pl.BlockSpec(size, lambda i: (0, 0))
            for size in ((1, length), (length, 128), (n // m * 2 * r, 128), (128, 128), (n, n))
        ],
        out_shape=[
            jax.ShapeDtypeStruct((1, length), F32),
            jax.ShapeDtypeStruct((length, 128), BF),
            jax.ShapeDtypeStruct((n // m * 2 * r, 128), F32),
            jax.ShapeDtypeStruct((128, 128), BF),
            jax.ShapeDtypeStruct((n, n), jnp.int32),
        ],
        compiler_params=pltpu.CompilerParams(vmem_limit_bytes=SMALL),
        name="masks",
    )(c, codes)


def hold_kernel(a_ref, b_ref, out_ref):
    out_ref[0] = a_ref[...]
    out_ref[1] = b_ref[...]


def hold(a, b, after):
    spec = pl.BlockSpec(a.shape, lambda i: (0, 0))
    return pl.pallas_call(
        ordered(hold_kernel, 2, len(after)),
        grid=(1,),
        in_specs=[spec, spec] + [pl.BlockSpec(memory_space=pl.ANY)] * len(after),
        out_specs=pl.BlockSpec((2,) + a.shape, lambda i: (0, 0, 0)),
        out_shape=jax.ShapeDtypeStruct((2,) + a.shape, a.dtype),
        compiler_params=pltpu.CompilerParams(vmem_limit_bytes=SMALL),
        name="hold",
    )(a, b, *after)


def proj_grad_kernel(count, steps, x_ref, c_ref, pos_ref, *refs):
    dq, dkv, drel = refs[:count], refs[count : 2 * count], refs[2 * count : 3 * count]
    extra = refs[3 * count : -4]
    out_ref, q_scr, kv_scr, r_scr = refs[-4:]
    i = pl.program_id(0)

    @pl.when(i == 0)
    def start():
        for scr in (q_scr, kv_scr, r_scr):
            scr[...] = jnp.zeros(scr.shape, F32)

    beside = lambda refs, axis: jnp.concatenate([ref[...] for ref in refs], axis=axis)
    r_scr[...] += mm(beside(drel, 0), pos_ref[...])

    @pl.when(i < steps[1])
    def keys():
        kv_scr[...] += mm(beside(dkv, 0), c_ref[...])

    @pl.when(i < steps[0])
    def queries():
        q_scr[...] += mm(beside(dq, 1), x_ref[...], 0, 0)

    @pl.when(i == steps[2] - 1)
    def finish():
        d = pos_ref.shape[1]
        lane = lax.broadcasted_iota(jnp.int32, (128, d), 1)
        for p in range(count):
            at = 512 * p
            rows = slice(128 * p, 128 * p + 128)
            out_ref[:, at : at + 128] = q_scr[rows, :].T.astype(BF)
            out_ref[:, at + 128 : at + 384] = kv_scr[256 * p : 256 * p + 256, :].T.astype(BF)
            turned = jnp.where(lane < d // 2, -r_scr[rows, :], r_scr[rows, :])
            out_ref[:, at + 384 : at + 512] = turned.T.astype(BF)
        for ref in extra:
            out_ref[:, 512 * count :] = ref[...]


def proj_grads(x, content, position, parts, extra, after):
    count = len(parts)
    d = x.shape[1]
    size = 512
    steps = [a.shape[0] // size for a in (x, content, position)]
    spec = lambda width, kind: pl.BlockSpec(
        (size, width), lambda i: (jnp.minimum(i, steps[kind] - 1), 0)
    )
    turned = lambda width, kind: pl.BlockSpec(
        (width, size), lambda i: (0, jnp.minimum(i, steps[kind] - 1))
    )
    operands = [x, content, position]
    specs = [spec(d, kind) for kind in range(3)]
    for index, one in enumerate((spec(128, 0), turned(256, 1), turned(128, 2))):
        operands += [b[index] for b in parts]
        specs += [one] * count
    operands += extra
    specs += [pl.BlockSpec(e.shape, lambda i: (0, 0)) for e in extra]
    width = 512 * count + sum(e.shape[1] for e in extra)
    total = len(operands)
    return pl.pallas_call(
        ordered(functools.partial(proj_grad_kernel, count, steps), total, len(after)),
        grid=(steps[2],),
        in_specs=specs + [pl.BlockSpec(memory_space=pl.ANY)] * len(after),
        out_specs=pl.BlockSpec((d, width), lambda i: (0, 0)),
        out_shape=jax.ShapeDtypeStruct((d, width), BF),
        scratch_shapes=[
            pltpu.VMEM((count * 128, d), F32),
            pltpu.VMEM((count * 256, d), F32),
            pltpu.VMEM((count * 128, d), F32),
        ],
        compiler_params=pltpu.CompilerParams(vmem_limit_bytes=VMEM),
        cost_estimate=pl.CostEstimate(flops=10**9, bytes_accessed=10**6, transcendentals=0),
        name="proj_grads",
    )(*operands, *after)


def add_kernel(count, *refs):
    total = refs[0][...].astype(F32)
    for ref in refs[1:count]:
        total += ref[...].astype(F32)
    refs[-1][...] = total.astype(refs[-1].dtype)


def add_up(parts, dtype, after):
    shape = parts[0].shape
    rows = parts[0].size // shape[-1]
    flat = [x.reshape(rows, shape[-1]) for x in parts]
    block = rows // 2 if rows % 32 == 0 else rows
    spec = pl.BlockSpec((block, shape[-1]), lambda i: (i, 0))
    out = pl.pallas_call(
        ordered(functools.partial(add_kernel, len(parts)), len(parts), len(after)),
        grid=(rows // block,),
        in_specs=[spec] * len(parts) + [pl.BlockSpec(memory_space=pl.ANY)] * len(after),
        out_specs=spec,
        out_shape=jax.ShapeDtypeStruct((rows, shape[-1]), dtype),
        compiler_params=pltpu.CompilerParams(vmem_limit_bytes=SMALL),
        cost_estimate=pl.CostEstimate(flops=rows, bytes_accessed=10**6, transcendentals=0),
        name="add_up",
    )(*flat, *after)
    return out.reshape(shape)


def fold_kernel(m, count, at_ref, *refs):
    for step in range(m):
        total = refs[step * count][0, 0].astype(F32)
        for ref in refs[step * count + 1 : (step + 1) * count]:
            total += ref[0, 0].astype(F32)
        refs[m * count + step][0] = total.astype(BF)


def fold(at, arrays, after):
    two, m, rows, width = arrays[0].shape
    count = len(arrays)
    spec = lambda step: pl.BlockSpec(
        (1, 1, rows, width), lambda i, at: (i, jnp.bitwise_xor(at[2], step), 0, 0)
    )
    return pl.pallas_call(
        ordered(functools.partial(fold_kernel, m, count), m * count + 1, len(after)),
        grid_spec=pltpu.PrefetchScalarGridSpec(
            num_scalar_prefetch=1,
            grid=(2,),
            in_specs=[spec(step) for step in range(m) for x in arrays]
            + [pl.BlockSpec(memory_space=pl.ANY)] * len(after),
            out_specs=[pl.BlockSpec((1, rows, width), lambda i, at: (i, 0, 0))] * m,
        ),
        out_shape=[jax.ShapeDtypeStruct((2, rows, width), BF)] * m,
        compiler_params=pltpu.CompilerParams(vmem_limit_bytes=SMALL),
        cost_estimate=pl.CostEstimate(flops=rows, bytes_accessed=10**6, transcendentals=0),
        name="fold",
    )(at, *(list(arrays) * m), *after)


def join_kernel(count, at_ref, *refs):
    for e in range(2):
        total = refs[e * count][0].astype(F32)
        for ref in refs[e * count + 1 : (e + 1) * count]:
            total += ref[0].astype(F32)
        refs[2 * count + e][...] = total.astype(BF)


def join(at, arrays, after):
    two, rows, width = arrays[0].shape
    count = len(arrays)
    spec = lambda e: pl.BlockSpec(
        (1, rows, width), lambda i, at: (jnp.bitwise_xor(at[1], e), 0, 0)
    )
    return pl.pallas_call(
        ordered(functools.partial(join_kernel, count), 2 * count + 1, len(after)),
        grid_spec=pltpu.PrefetchScalarGridSpec(
            num_scalar_prefetch=1,
            grid=(1,),
            in_specs=[spec(e) for e in range(2) for x in arrays]
            + [pl.BlockSpec(memory_space=pl.ANY)] * len(after),
            out_specs=[pl.BlockSpec((rows, width), lambda i, at: (0, 0))] * 2,
        ),
        out_shape=[jax.ShapeDtypeStruct((rows, width), BF)] * 2,
        compiler_params=pltpu.CompilerParams(vmem_limit_bytes=SMALL),
        cost_estimate=pl.CostEstimate(flops=rows, bytes_accessed=10**6, transcendentals=0),
        name="join",
    )(at, *(list(arrays) * 2), *after)


GELU_A = 0.7978845608028654
GELU_B = 0.044715


def gelu_and_slope(v):
    square = v * v
    t = jnp.tanh(GELU_A * (v + GELU_B * (v * square)))
    half = 0.5 + 0.5 * t
    slope = half + 0.5 * v * (1.0 - t * t) * (GELU_A * (1.0 + 3.0 * GELU_B * square))
    return v * half, slope


def norm_forward(x):
    average = jnp.mean(x, axis=1, keepdims=True)
    centred = x - average
    inverse = lax.rsqrt(jnp.mean(centred * centred, axis=1, keepdims=True) + EPSILON)
    return centred * inverse, inverse


def norm_backward(grad, gain, unit, inverse):
    scaled = grad * gain
    pull = jnp.mean(scaled, axis=1, keepdims=True)
    twist = jnp.mean(scaled * unit, axis=1, keepdims=True)
    return inverse * (scaled - pull - unit * twist)


def dense_kernel(m, n, ws, pairs, at_ref, *refs):
    own_mixed, got_mixed = refs[:pairs], refs[pairs : 2 * pairs]
    x_ref, cot_ref = refs[2 * pairs : 2 * pairs + 2]
    pieces = refs[2 * pairs + 2 : 2 * pairs + 2 + 2 * m]
    rest = refs[2 * pairs + 2 + 2 * m :]
    result_ref, gr_ref, gm_own, gm_other, vec_ref, b1_ref = rest[:6]
    early_own, early_other, late_own, late_other = rest[6:10]
    w1, w2, wo, vp, slope, hidden, unit_bf, mixed, early, late, bias, sems, out_sems = rest[10:]
    k, low, c = at_ref[0], at_ref[1], at_ref[2]
    d = x_ref.shape[1]
    ff = w1.shape[1]
    parts = ff // d
    fs = parts * ws
    places = []
    for index, piece in enumerate(pieces):
        h = k if index < m else 1 - k
        for e in range(2):
            s = (2 * h + jnp.bitwise_xor(low, e)) * m + jnp.bitwise_xor(c, index % m)
            places.append((piece.at[e], s))
    kinds = 2 + parts + 1

    def load(i, kind, j=0):
        src, s = places[i]
        to = pl.ds(pl.multiple_of(s * ws, 16), ws)
        if kind == 0:
            pair = (src.at[pl.ds(parts * ws, ws), :], wo.at[to, :])
        elif kind == 1:
            pair = (src.at[pl.ds((2 * parts + 1) * ws, 16), :], vp.at[s])
        elif kind == 2:
            rows = pl.ds(pl.multiple_of(j * ws, 16), ws)
            pair = (src.at[rows, :], w1.at[to, pl.ds(pl.multiple_of(j * d, 128), d)])
        else:
            to = pl.ds(pl.multiple_of(s * fs, 16), fs)
            pair = (src.at[pl.ds((parts + 1) * ws, fs), :], w2.at[to, :])
        at = i * kinds + (kind if kind < 2 else 2 + j if kind == 2 else kinds - 1)
        return pltpu.make_async_copy(*pair, sems.at[at])

    count = len(places)
    for kind in (0, 1):
        for i in range(count):
            load(i, kind).start()
    for j in range(parts):
        for i in range(count):
            load(i, 2, j).start()
    for i in range(count):
        load(i, 3).start()

    for p in range(pairs):
        lanes = slice(128 * p, 128 * p + 128)
        other = slice(d // 2 + 128 * p, d // 2 + 128 * p + 128)

        @pl.when(k == 0)
        def low_core():
            mixed[:, lanes] = own_mixed[p][...]
            mixed[:, other] = got_mixed[p][...]

        @pl.when(k != 0)
        def high_core():
            mixed[:, lanes] = got_mixed[p][...]
            mixed[:, other] = own_mixed[p][...]

    for kind in (0, 1):
        for i in range(count):
            load(i, kind).wait()
    spot = lax.broadcasted_iota(jnp.int32, (128, d), 1)
    down = lax.broadcasted_iota(jnp.int32, (128, d), 0)
    vecs = jnp.zeros((16, d), F32)
    for s in range(n):
        place = jnp.where((spot == s * ws + down) & (down < ws), 1.0, 0.0).astype(BF)
        vecs += mm(vp[s, :, :128], place)
    per = (d // 2) // fs
    spot = lax.broadcasted_iota(jnp.int32, (256, d // 2), 1)
    down = lax.broadcasted_iota(jnp.int32, (256, d // 2), 0)
    place = [
        jnp.where((spot == t * fs + down) & (down < fs), 1.0, 0.0).astype(BF) for t in range(per)
    ]
    for q in range(n // per):
        row = sum(mm(vp[q * per + t, :, :256], place[t]) for t in range(per))
        bias[:, q * (d // 2) : (q + 1) * (d // 2)] = row[:8]
    outer_shift, gain_one, shift_one, gain_two, shift_two = [vecs[i : i + 1] for i in range(5)]

    residual = mm(mixed[...], wo[...]) + x_ref[...].astype(F32)
    unit_one, inverse_one = norm_forward(residual)
    normed = unit_one * gain_one + shift_one
    unit_bf[...] = normed.astype(BF)
    total = normed + outer_shift

    def wait_chunk(j):
        for i in range(count):
            load(i, 2, j).wait()

    for j in range(parts):
        wait_chunk(j)
        cols = slice(j * d, (j + 1) * d)
        value, slant = gelu_and_slope(mm(unit_bf[...], w1[:, cols]) + bias[5:6, cols])
        hidden[:, cols] = value.astype(BF)
        slope[:, cols] = slant
    for i in range(count):
        load(i, 3).wait()
    summed = total + mm(hidden[...], w2[...])
    unit_two, inverse_two = norm_forward(summed)
    result_ref[...] = (unit_two * gain_two + shift_two).astype(BF)
    cot = cot_ref[...].astype(F32)
    grad_summed = norm_backward(cot, gain_two, unit_two, inverse_two)
    row_sum = lambda x: jnp.sum(x, axis=0, keepdims=True)
    vec_ref[0:1, :] = row_sum(grad_summed)
    vec_ref[3:4, :] = row_sum(cot * unit_two)
    vec_ref[4:5, :] = row_sum(cot)
    grad_bf = grad_summed.astype(BF)
    grad_normed = grad_summed
    copies = []
    deep = early.shape[0] // 2
    split = ff // 2 // d

    def send(half, src, own, other):
        sem = out_sems.at[len(copies)]
        copies.append(pltpu.make_async_copy(src, own, sem))

        @pl.when(k == half)
        def keep():
            pltpu.make_async_copy(src, own, sem).start()

        @pl.when(k != half)
        def give():
            pltpu.make_async_copy(src, other, sem).start()

    def send_early(cols):
        for half in range(2):
            src = early.at[half * deep : (half + 1) * deep, cols]
            send(half, src, early_own.at[:, cols], early_other.at[:, cols])

    for j in range(parts):
        cols = slice(j * d, (j + 1) * d)
        grad_inner = mm(grad_bf, w2[cols, :], 1, 1) * slope[:, cols]
        b1_ref[0:1, cols] = row_sum(grad_inner)
        inner_bf = grad_inner.astype(BF)
        late[cols, :] = mm(hidden[:, cols], grad_bf, 0, 0).astype(BF)
        to = pl.ds((j % split) * d, d)
        send(j // split, late.at[cols, :], late_own.at[to, :], late_other.at[to, :])
        early[:, cols] = mm(unit_bf[...], inner_bf, 0, 0).astype(BF)
        send_early(cols)
        grad_normed += mm(inner_bf, w1[:, cols], 1, 1)
    vec_ref[1:2, :] = row_sum(grad_normed * unit_one)
    vec_ref[2:3, :] = row_sum(grad_normed)
    grad_residual = norm_backward(grad_normed, gain_one, unit_one, inverse_one)
    gr_ref[...] = grad_residual
    residual_bf = grad_residual.astype(BF)
    early[:, ff:] = mm(mixed[...], residual_bf, 0, 0).astype(BF)
    send_early(slice(ff, ff + d))
    grad_mixed = mm(residual_bf, wo[...], 1, 1).astype(BF)
    for half in range(2):
        part = grad_mixed[:, half * (d // 2) : (half + 1) * (d // 2)]

        @pl.when(k == half)
        def keep(part=part):
            gm_own[...] = part

        @pl.when(k != half)
        def give(part=part):
            gm_other[...] = part

    for copy in copies:
        copy.wait()


def dense(at, own_mixed, got_mixed, inputs, cots, mine, theirs, ws, ff):
    m = len(mine)
    pairs = len(own_mixed)
    rows, d = cots.shape
    n = d // ws
    parts = ff // d
    anywhere = pl.BlockSpec(memory_space=pl.ANY)
    half = lambda width: pl.BlockSpec((rows, width), lambda i, at: (at[0], 0))
    fixed = lambda *shape: pl.BlockSpec(shape, lambda i, at: (0,) * len(shape))
    return pl.pallas_call(
        functools.partial(dense_kernel, m, n, ws, pairs),
        grid_spec=pltpu.PrefetchScalarGridSpec(
            num_scalar_prefetch=1,
            grid=(1,),
            in_specs=[half(128)] * pairs
            + [fixed(rows, 128)] * pairs
            + [half(d), fixed(rows, d)]
            + [anywhere] * (2 * m),
            out_specs=[
                fixed(rows, d),
                fixed(rows, d),
                fixed(rows, d // 2),
                fixed(rows, d // 2),
                fixed(8, d),
                fixed(8, ff),
            ]
            + [anywhere] * 4,
            scratch_shapes=[
                pltpu.VMEM((d, ff), BF),
                pltpu.VMEM((ff, d), BF),
                pltpu.VMEM((d, d), BF),
                pltpu.VMEM((n, 16, d), BF),
                pltpu.VMEM((rows, ff), F32),
                pltpu.VMEM((rows, ff), BF),
                pltpu.VMEM((rows, d), BF),
                pltpu.VMEM((rows, d), BF),
                pltpu.VMEM((d, ff + d), BF),
                pltpu.VMEM((ff, d), BF),
                pltpu.VMEM((8, ff), F32),
                pltpu.SemaphoreType.DMA((4 * m * (3 + parts),)),
                pltpu.SemaphoreType.DMA((3 * parts + 2,)),
            ],
        ),
        out_shape=[
            jax.ShapeDtypeStruct((rows, d), BF),
            jax.ShapeDtypeStruct((rows, d), F32),
            jax.ShapeDtypeStruct((rows, d // 2), BF),
            jax.ShapeDtypeStruct((rows, d // 2), BF),
            jax.ShapeDtypeStruct((8, d), F32),
            jax.ShapeDtypeStruct((8, ff), F32),
            jax.ShapeDtypeStruct((d // 2, ff + d), BF),
            jax.ShapeDtypeStruct((d // 2, ff + d), BF),
            jax.ShapeDtypeStruct((ff // 2, d), BF),
            jax.ShapeDtypeStruct((ff // 2, d), BF),
        ],
        compiler_params=pltpu.CompilerParams(vmem_limit_bytes=VMEM),
        cost_estimate=pl.CostEstimate(flops=10**9, bytes_accessed=10**6, transcendentals=0),
        name="dense",
    )(at, *own_mixed, *got_mixed, inputs, cots, *mine, *theirs)


def dense_plain(at, own_mixed, got_mixed, inputs, cots, mine, theirs, ws, ff):
    rows, d = cots.shape
    n, fs = d // ws, ff * ws // d
    k = at[0]
    mine_half = lambda x: lax.dynamic_slice_in_dim(x, k * rows, rows, 0)
    inner_w, output_w, outer_w, vecs = assemble_late(at, mine, theirs, ws, ff // d)
    inner_w, output_w = inner_w.reshape(d, ff), output_w.reshape(d, d)
    outer_w = outer_w.reshape(ff, d)
    vecs = vecs.reshape(n, 16, d).astype(F32)
    inner_shift = vecs[:, 5, :fs].reshape(ff)
    vecs = vecs[:, :5, :ws].swapaxes(0, 1).reshape(5, d)
    outer_shift, gain_one, shift_one, gain_two, shift_two = [vecs[i] for i in range(5)]
    own = [mine_half(x) for x in own_mixed]
    mixed = jnp.where(
        k == 0,
        jnp.concatenate(own + got_mixed, axis=1),
        jnp.concatenate(got_mixed + own, axis=1),
    )
    residual = mm(mixed, output_w) + mine_half(inputs).astype(F32)
    unit_one, inverse_one = norm_forward(residual)
    normed = unit_one * gain_one + shift_one
    normed_bf = normed.astype(BF)
    value, slope = gelu_and_slope(mm(normed_bf, inner_w) + inner_shift)
    hidden = value.astype(BF)
    summed = mm(hidden, outer_w) + outer_shift + normed
    unit_two, inverse_two = norm_forward(summed)
    result = (unit_two * gain_two + shift_two).astype(BF)
    cot = cots.astype(F32)
    grad_summed = norm_backward(cot, gain_two, unit_two, inverse_two)
    grad_bf = grad_summed.astype(BF)
    grad_inner = mm(grad_bf, outer_w, 1, 1) * slope
    inner_bf = grad_inner.astype(BF)
    grad_normed = mm(inner_bf, inner_w, 1, 1) + grad_summed
    grad_residual = norm_backward(grad_normed, gain_one, unit_one, inverse_one)
    residual_bf = grad_residual.astype(BF)
    grad_mixed = mm(residual_bf, output_w, 1, 1).astype(BF)
    terms = [grad_summed, grad_normed * unit_one, grad_normed, cot * unit_two, cot]
    early = jnp.concatenate([mm(normed_bf, inner_bf, 0, 0), mm(mixed, residual_bf, 0, 0)], axis=1)

    def halves(x, axis):
        size = x.shape[axis] // 2
        return [lax.dynamic_slice_in_dim(x, i * size, size, axis).astype(BF) for i in (k, 1 - k)]

    return (
        result,
        grad_residual,
        *halves(grad_mixed, 1),
        jnp.stack([jnp.sum(x, axis=0) for x in terms]),
        jnp.sum(grad_inner, axis=0)[None],
        *halves(early, 0),
        *halves(mm(hidden, grad_bf, 0, 0), 0),
    )


def body(
    content_in,
    query_in,
    segment_ids,
    parent_ids,
    rank_order,
    query_flags,
    query_weight,
    key_weight,
    value_weight,
    relative_weight,
    output_weight,
    inner_weight,
    outer_weight,
    inner_bias,
    outer_bias,
    attend_gain,
    attend_shift,
    feed_gain,
    feed_shift,
    content_bias,
    position_bias,
    segment_bias,
    segment_table,
    content_cot,
    query_cot,
):
    n = lax.axis_size("shard")
    nr = lax.axis_size("rep")
    trees, r, d = content_in.shape
    groups = 2 * trees
    m = n // groups
    length = r * n
    nkb = length // KB
    ff = inner_weight.shape[1]
    dh = d // 2
    heads = dh // DH
    pairs = heads // 2
    ws = query_weight.shape[0]
    fs = outer_weight.shape[0]
    me = lax.axis_index("shard")
    g, c = me // m, me % m
    low = g % 2
    k = lax.axis_index("rep") % 2
    first = k == 0
    tie = lax.optimization_barrier

    def swap(x):
        return lax.ppermute(x, "rep", [(i, i ^ 1) for i in range(nr)])

    def far(x, step):
        return lax.ppermute(x, "shard", [(i, i ^ (m * step)) for i in range(n)])

    def near(x, step):
        return lax.ppermute(x, "shard", [(i, i ^ step) for i in range(n)])

    def across(x, e):
        moves = []
        for i in range(nr):
            for j in range(n):
                z = j // m
                to = (i - i % 2 + z // 2) * n + (2 * (i % 2) + (z % 2 ^ e)) * m + j % m
                moves.append((i * n + j, to))
        return lax.ppermute(x, ("rep", "shard"), moves)

    def pick(x, index, axis=0):
        return lax.dynamic_index_in_dim(x, index, axis, keepdims=False)

    def put(buffer, x, index, axis=0):
        return lax.dynamic_update_index_in_dim(buffer, x, index, axis)

    def pair_of(mine, other, index, axis=0):
        return put(jnp.stack([mine, mine], axis), other, 1 - index, axis)

    def cross(parts):
        got = [across(pick(parts, low ^ e), e) for e in range(2)]
        return pair_of(got[0], got[1], low)

    def near_gather(x, downward):
        bits = [b for b in range(m.bit_length() - 1)]
        held = {0: x}
        for b in bits[::-1] if downward else bits:
            held.update({o | 1 << b: near(y, 1 << b) for o, y in list(held.items())})
        return jnp.stack([held[o] for o in range(m)])

    def near_parts(x, axis):
        sent = [near(pick(x, c ^ step, axis), step) for step in range(1, m)]
        return [pick(x, c, axis)] + sent

    def far_sum(x):
        total = pick(x, g).astype(F32)
        for step in range(1, groups):
            total = total + far(pick(x, g ^ step), step).astype(F32)
        return total

    weights = [query_weight, key_weight, value_weight, relative_weight]
    low_array = low.astype(jnp.int32).reshape(1)
    vec_rows = [x.reshape(1, ws) for x in (content_bias, position_bias, segment_bias)]
    packed = pack(
        low_array,
        content_in,
        segment_ids,
        rank_order,
        query_flags,
        parent_ids,
        vec_rows + [segment_table],
        weights,
    )
    at = jnp.stack([k, low, c]).astype(jnp.int32)
    got = [across(packed[e], e) for e in range(2)]
    own_query = jnp.stack([across(pick(query_in, low ^ e), e) for e in range(2)])
    near_rows = [near_gather(got[e], e) for e in range(2)]
    their_rows = [swap(x) for x in near_rows]
    late_pack = pack_late(
        inner_weight,
        output_weight,
        outer_weight,
        [x.reshape(1, ws) for x in (outer_bias, attend_gain, attend_shift, feed_gain, feed_shift)]
        + [inner_bias.reshape(1, fs)],
    )
    late_pack, unused = tie((late_pack, got[1]))
    late = [across(late_pack, e) for e in range(2)]
    content_full, codes, wq, kv_weight, wr, inputs = assemble(
        at, near_rows, their_rows, own_query, swap(own_query), r, ws, []
    )
    content_full = content_full.reshape(length, d)
    wq, kv_weight, wr = wq.reshape(d, dh), kv_weight.reshape(d, d), wr.reshape(d, dh)
    inputs = inputs.reshape(groups * 2 * r, d)
    codes = codes.reshape(n, 16, d)
    key_ranks, hot, info, reach, live = masks(
        c.astype(jnp.int32).reshape(1), codes.reshape(n * 16, d), m, r
    )
    base = jnp.stack([c, m]).astype(jnp.int32)
    vectors = codes[:, 1:6, :ws].astype(F32).swapaxes(0, 1).reshape(5, 2, dh)
    head_vecs = jnp.where(first, vectors[:, 0], vectors[:, 1])


    content_cot, query_cot, unused = tie((content_cot, query_cot, content_full))
    cots = cross(jnp.stack([content_cot, query_cot], axis=1))

    position_bf, rel, rel_turned = relative(wr, length)
    queries = mm(inputs, wq)
    kv = mm(content_full, kv_weight).astype(BF)
    vec8 = jnp.pad(head_vecs, ((0, 3), (0, 0)))
    table = head_vecs[3:5].reshape(2, heads, DH).transpose(1, 2, 0)[..., None]
    table = jnp.where(jnp.arange(128) < 2 * NS, table, 0.0).astype(BF)
    table = jnp.tile(table.reshape(heads, DH, 256), (1, 2, 1))
    late = hold(late[0], late[1], [rel])
    late_near = [late] + [near(late, step) for step in range(1, m)]
    forward = []
    got_mixed = []
    for pair in range(pairs):
        after = [[late], [cots], late_near[1:]][min(pair, 2)]
        if pair == 2:
            *held, unused = tie((*late_near, forward[1][1]))
            late_theirs = [swap(x) for x in held]
        after = after + [f[1] for f in forward[-1:]]
        forward.append(
            attend_forward(
                pair,
                after,
                base,
                live,
                queries,
                vec8,
                table,
                info,
                reach,
                kv,
                hot,
                rel,
                key_ranks,
            )
        )
        got_mixed.append(swap(pick(forward[-1][3].reshape(2, groups * r, 128), 1 - k)))

    (
        result,
        grad_residual,
        mine_grad,
        other_grad,
        row_vecs,
        inner_vecs,
        early_mine,
        early_other,
        late_mine,
        late_other,
    ) = (dense if ws % 16 == 0 else dense_plain)(
        at,
        [f[3] for f in forward],
        got_mixed,
        inputs,
        cots.reshape(groups * r, d),
        late_near,
        late_theirs,
        ws,
        ff,
    )
    grad_heads = pair_of(mine_grad, swap(other_grad), k).reshape(groups * 2 * r, dh)

    backward = []

    def back(pair, after):
        f = forward[pair]
        after = after + [b[0] for b in backward[-1:]]
        backward.append(
            attend_backward(
                pair,
                after,
                base,
                live,
                f[0],
                queries,
                grad_heads,
                f[1],
                f[2],
                vec8,
                info,
                kv,
                hot,
                rel_turned,
            )
        )

    def near_fold(arrays, rows, after):
        parts = fold(at, [x.reshape(2, m, rows, x.shape[-1]) for x in arrays], after)
        return [parts[0]] + [near(parts[step], step) for step in range(1, m)]

    def cross_join(parts, after):
        return [across(x, e) for e, x in enumerate(join(at, parts, after))]

    def proj_some(some, extra, after):
        return proj_grads(
            inputs, content_full, position_bf, [backward[p] for p in some], extra, after
        ).reshape(groups, m, ws, -1)

    result = result.reshape(2, 2, r, d)
    outs_got = [across(pick(result, low ^ e), e) for e in range(2)]
    back(0, [])
    after = [backward[0][0]]
    late_parts = near_fold([late_mine, swap(late_other)], fs, after + outs_got)
    early_parts = near_fold([early_mine, swap(early_other)], ws, after)
    back(1, [early_parts[0], late_parts[0]])
    some_grads = proj_some(range(pairs - 1), [], [])
    some_parts = near_parts(some_grads, 1)
    late_cross = cross_join(late_parts, [some_grads])
    early_cross = cross_join(early_parts, [some_grads])
    back(2, [some_grads])

    small = jnp.concatenate([b[3][:5] for b in backward], axis=1)
    small = jnp.where(
        first,
        jnp.concatenate([small, jnp.zeros_like(small)], axis=1),
        jnp.concatenate([jnp.zeros_like(small), small], axis=1),
    )
    inner_vecs = inner_vecs[0].reshape(n, fs // ws, ws).swapaxes(1, 2).reshape(d, fs // ws)
    small = jnp.concatenate([small.T, row_vecs[:5].T, inner_vecs], axis=1)
    small = jnp.pad(small, ((0, 0), (0, 128 - small.shape[1]))).astype(BF)
    last_grads = proj_some([pairs - 1], [small], some_parts[1:] + late_cross + early_cross)
    early_sum = add_up(early_cross, BF, [last_grads])
    late_sum = add_up(late_cross, BF, [last_grads])
    early_got, late_got = swap(early_sum), swap(late_sum)
    *outs_got, unused = tie((*outs_got, last_grads))
    outs = pair_of(outs_got[0], outs_got[1], low)
    last_parts = near_parts(last_grads, 1)
    which = [jnp.asarray(x, jnp.int32).reshape(1) for x in (k, 1 - k)]
    dkv_parts = [b[1] for b in backward]
    dq_parts = [b[0] for b in backward]
    got_kv = swap(input_grad(which[1], dkv_parts, kv_weight, BF, [last_grads], True))
    got_q = swap(input_grad(which[1], dq_parts, wq, BF, [last_grads]))
    own_kv = input_grad(which[0], dkv_parts, kv_weight, F32, [last_grads], True)
    own_q = input_grad(which[0], dq_parts, wq, F32, [last_grads])
    content_parts = near_fold([own_kv, got_kv], r, [own_q, early_got, late_got] + last_parts[1:])
    q_sum = own_q + got_q.astype(F32) + grad_residual
    q_sum = q_sum.reshape(2, 2, r, d)
    query_rows, unused = tie((q_sum[:, 1].astype(BF), content_parts[1]))
    query_grads = cross(query_rows)
    late_total = late_sum.astype(F32) + late_got.astype(F32)
    content_sum = sum([x.astype(F32) for x in content_parts]) + q_sum[:, 0]
    content_grads = cross(content_sum.astype(BF))
    some_near, last_near = [
        add_up(parts, BF, content_parts[:1]) for parts in (some_parts, last_parts)
    ]
    proj_sum = far_sum(jnp.concatenate([some_near, last_near], axis=2))

    early_total = early_sum.astype(F32) + early_got.astype(F32)
    bit = 2
    while bit < nr:
        turn = [(i, i ^ bit) for i in range(nr)]
        early_total = early_total + lax.ppermute(early_total, "rep", turn)
        late_total = late_total + lax.ppermute(late_total, "rep", turn)
        proj_sum = proj_sum + lax.ppermute(proj_sum, "rep", turn)
        bit *= 2
    proj_other = swap(proj_sum)
    halves = jnp.where(first, proj_sum, proj_other), jnp.where(first, proj_other, proj_sum)

    def columns(index):
        return jnp.concatenate(
            [
                x[:, 512 * p + 128 * index : 512 * p + 128 * index + 128]
                for x in halves
                for p in range(pairs)
            ],
            axis=1,
        )

    head_cols = (proj_sum + proj_other)[:, 512 * pairs :]
    vec_cols = head_cols[:, 5:]
    return (
        outs[:, 0],
        outs[:, 1],
        content_grads,
        query_grads,
        columns(0),
        columns(1),
        columns(2),
        columns(3),
        early_total[:, ff : ff + d],
        early_total[:, :ff],
        late_total,
        vec_cols[:, 5 : 5 + fs // ws].T.reshape(fs),
        vec_cols[:, 0],
        vec_cols[:, 1],
        vec_cols[:, 2],
        vec_cols[:, 3],
        vec_cols[:, 4],
        head_cols[:, 0],
        head_cols[:, 1],
        head_cols[:, 2],
        head_cols[:, 3:5].T,
    )


def solution(mesh):
    in_specs = (
        P("rep", "shard", None),
        P("rep", "shard", None),
        P("rep", "shard"),
        P("rep", None),
        P("rep", "shard"),
        P("rep", "shard"),
        P("shard", None),
        P("shard", None),
        P("shard", None),
        P("shard", None),
        P("shard", None),
        P("shard", None),
        P("shard", None),
        P("shard"),
        P("shard"),
        P("shard"),
        P("shard"),
        P("shard"),
        P("shard"),
        P("shard"),
        P("shard"),
        P("shard"),
        P(None, "shard"),
        P("rep", "shard", None),
        P("rep", "shard", None),
    )
    out_specs = (
        P("rep", "shard", None),
        P("rep", "shard", None),
        P("rep", "shard", None),
        P("rep", "shard", None),
        P("shard", None),
        P("shard", None),
        P("shard", None),
        P("shard", None),
        P("shard", None),
        P("shard", None),
        P("shard", None),
        P("shard"),
        P("shard"),
        P("shard"),
        P("shard"),
        P("shard"),
        P("shard"),
        P("shard"),
        P("shard"),
        P("shard"),
        P(None, "shard"),
    )
    return jax.shard_map(body, mesh=mesh, in_specs=in_specs, out_specs=out_specs, check_vma=False)
```

```python
import functools
import math

import jax
import jax.numpy as jnp
from jax import lax
from jax.experimental import pallas as pl
from jax.experimental.pallas import tpu as pltpu
from jax.sharding import PartitionSpec as P

DH = 64
NS = 13
EPSILON = 1e-05
NEG = -1e30
F32 = jnp.float32
BF = jnp.bfloat16
HIGHEST = lax.Precision.HIGHEST

R = 128
KB = 256
W = R + KB
SCALE = DH**-0.5
LOG2E = 1.4426950408889634
LN2 = 0.6931471805599453
VMEM = 60 * 2**20
SMALL = 32 * 2**20
ONES = 32


def mm(a, b, ca=1, cb=0, precision=None):
    return lax.dot_general(
        a, b, (((ca,), (cb,)), ((), ())), preferred_element_type=F32, precision=precision
    )


def row_features(seg_col):
    lane = lax.broadcasted_iota(jnp.int32, (2 * R, 128), 1)
    folded = jnp.where(lane < NS, lane, lane - NS).astype(F32)
    return jnp.where((lane < 2 * NS) & (folded == seg_col), 1.0, 0.0)


def live_list(live_ref, list_ref, row, nkb):
    per = KB // R

    def step(kb, count):
        list_ref[count] = kb
        live = live_ref[row, kb * per]
        for i in range(1, per):
            live = jnp.maximum(live, live_ref[row, kb * per + i])
        return count + live

    return lax.fori_loop(0, nkb, step, 0)


def ordered(kernel, count, extra):
    def run(*refs):
        kernel(*refs[:count], *refs[count + extra :])

    return run


def reversal():
    down = lax.broadcasted_iota(jnp.int32, (KB, KB), 0)
    across = lax.broadcasted_iota(jnp.int32, (KB, KB), 1)
    return jnp.where(down + across == KB - 1, 1.0, 0.0).astype(BF)


def by_two(count, work):
    def step(i, carry):
        work([2 * i, 2 * i + 1])
        return carry

    lax.fori_loop(0, count // 2, step, 0)

    @pl.when(count % 2 == 1)
    def last():
        work([count - 1])


def forward_kernel(
    nkb,
    base_ref,
    live_ref,
    q_ref,
    vec_ref,
    table_ref,
    info_ref,
    reach_ref,
    kv_ref,
    hot_ref,
    rel_ref,
    rank_ref,
    p_ref,
    o_ref,
    inv_ref,
    ob_ref,
    qq_scr,
    qr_scr,
    s_scr,
    m_scr,
    acc_scr,
    flip_scr,
    list_scr,
):
    block = pl.program_id(0)

    @pl.when(block == 0)
    def start():
        flip_scr[...] = reversal()

    row = base_ref[0] + base_ref[1] * block
    base = nkb * KB - R - R * row
    count = live_list(live_ref, list_scr, row, nkb)
    seg_col = info_ref[:, 0:1]
    limit = info_ref[:, 1:2]
    hot_row = row_features(seg_col)
    lane = lax.broadcasted_iota(jnp.int32, (2 * R, 128), 1)
    reach = mm(jnp.where(lane < NS, hot_row, 0.0).astype(BF), reach_ref[...])
    outside = jnp.where((lane < 2 * NS) & (reach < 0.5), NEG, 0.0)
    zero = jnp.zeros((2 * R, DH), BF)
    for h in range(2):
        half = slice(DH * h, DH * h + DH)
        q = q_ref[:, half]
        plain = ((q + vec_ref[0:1, half]) * (SCALE * LOG2E)).astype(BF)
        place = ((q + vec_ref[1:2, half]) * (SCALE * LOG2E)).astype(BF)
        label = q + vec_ref[2:3, half]
        top_part = label.astype(BF)
        rest = (label - top_part.astype(F32)).astype(BF)
        both = mm(jnp.concatenate([top_part, rest], axis=1), table_ref[h])
        same, other = both[:, :128], both[:, 128:]
        term = jnp.where(hot_row > 0.5, same, other) * (SCALE * LOG2E) + outside
        high = term.astype(BF).astype(F32)
        extra = jnp.where(lane < NS, high, jnp.where(lane < 2 * NS, term - high, 0.0))
        side = lambda x: [x, zero] if h == 0 else [zero, x]
        qq_scr[h] = jnp.concatenate(side(plain) + [extra.astype(BF)], axis=1)
        qr_scr[h] = jnp.concatenate(side(place), axis=1)
    m_scr[...] = jnp.full(m_scr.shape, -jnp.inf, F32)
    acc_scr[...] = jnp.zeros(acc_scr.shape, F32)

    def score(blocks):
        highest = [m_scr[h] for h in range(2)]
        for n in blocks:
            k0 = pl.multiple_of(list_scr[n] * KB, KB)
            ok = rank_ref[:, pl.ds(k0, KB)] <= limit
            window = rel_ref[pl.ds(pl.multiple_of(base + k0, 128), W), :]
            keys = jnp.concatenate(
                [kv_ref[pl.ds(k0, KB), :128], hot_ref[pl.ds(k0, KB), :]], axis=1
            )
            for h in range(2):
                s = mm(qq_scr[h], keys, 1, 1)
                full = mm(qr_scr[h], window, 1, 1)
                shifted = [
                    pltpu.roll(
                        full[i * R : i * R + R], W - (R - 1), 1, stride=1, stride_axis=0
                    )[:, :KB]
                    for i in range(2)
                ]
                s = jnp.where(ok, s + jnp.concatenate(shifted, axis=0), NEG)
                s_scr[h, n] = s
                highest[h] = jnp.maximum(highest[h], jnp.maximum(s[:, :128], s[:, 128:]))
        for h in range(2):
            m_scr[h] = highest[h]

    by_two(count, score)
    top = [jnp.max(m_scr[h], axis=1, keepdims=True) for h in range(2)]

    def mix(blocks):
        totals = [0.0, 0.0]
        for n in blocks:
            k0 = pl.multiple_of(list_scr[n] * KB, KB)
            values = jnp.concatenate(
                [kv_ref[pl.ds(k0, KB), 128:], hot_ref[pl.ds(k0, KB), :]], axis=1
            )
            for h in range(2):
                p = jnp.exp2(s_scr[h, n] - top[h]).astype(BF)
                p_ref[0, h, n] = mm(p, flip_scr[...]).astype(BF)
                totals[h] += mm(p, values)
        for h in range(2):
            acc_scr[h] += totals[h]

    by_two(count, mix)
    for h in range(2):
        half = slice(DH * h, DH * h + DH)
        acc = acc_scr[h]
        inverse = 1.0 / acc[:, 128 + ONES : 129 + ONES]
        mixed = acc[:, half] * inverse
        o_ref[:, half] = mixed
        ob_ref[:, half] = mixed.astype(BF)
        inv_ref[:, half] = jnp.broadcast_to(inverse, (2 * R, DH))


def attend_forward(pair, after, base, live, q, vec, table, info, reach, kv, hot, rel, rank):
    nb = q.shape[0] // (2 * R)
    length = kv.shape[0]
    nkb = length // KB
    whole = lambda *shape: pl.BlockSpec(shape, lambda b, *_: (0,) * len(shape))
    return pl.pallas_call(
        ordered(functools.partial(forward_kernel, nkb), 11, len(after)),
        grid_spec=pltpu.PrefetchScalarGridSpec(
            num_scalar_prefetch=2,
            grid=(nb,),
            in_specs=[
                pl.BlockSpec((2 * R, 128), lambda b, *_: (b, pair)),
                pl.BlockSpec((8, 128), lambda b, *_: (0, pair)),
                pl.BlockSpec((2, 2 * DH, 256), lambda b, *_: (pair, 0, 0)),
                pl.BlockSpec((2 * R, 128), lambda b, *_: (b, 0)),
                whole(128, 128),
                pl.BlockSpec((length, 256), lambda b, *_: (0, pair)),
                whole(length, 128),
                pl.BlockSpec((2 * length, 128), lambda b, *_: (0, pair)),
                whole(1, length),
            ]
            + [pl.BlockSpec(memory_space=pl.ANY)] * len(after),
            out_specs=[
                pl.BlockSpec((1, 2, nkb, 2 * R, KB), lambda b, *_: (b, 0, 0, 0, 0)),
                pl.BlockSpec((2 * R, 128), lambda b, *_: (b, 0)),
                pl.BlockSpec((2 * R, 128), lambda b, *_: (b, 0)),
                pl.BlockSpec((2 * R, 128), lambda b, *_: (b, 0)),
            ],
            scratch_shapes=[
                pltpu.VMEM((2, 2 * R, 256), BF),
                pltpu.VMEM((2, 2 * R, 128), BF),
                pltpu.VMEM((2, nkb, 2 * R, KB), F32),
                pltpu.VMEM((2, 2 * R, 128), F32),
                pltpu.VMEM((2, 2 * R, 256), F32),
                pltpu.VMEM((KB, KB), BF),
                pltpu.SMEM((nkb + 1,), jnp.int32),
            ],
        ),
        out_shape=[
            jax.ShapeDtypeStruct((nb, 2, nkb, 2 * R, KB), BF),
            jax.ShapeDtypeStruct((q.shape[0], 128), F32),
            jax.ShapeDtypeStruct((q.shape[0], 128), F32),
            jax.ShapeDtypeStruct((q.shape[0], 128), BF),
        ],
        compiler_params=pltpu.CompilerParams(
            dimension_semantics=("arbitrary",), vmem_limit_bytes=VMEM
        ),
        cost_estimate=pl.CostEstimate(
            flops=10**8, bytes_accessed=10**6, transcendentals=0
        ),
        name="attend_forward",
    )(base, live, q, vec, table, info, reach, kv, hot, rel, rank, *after)


def backward_kernel(
    nkb,
    nb,
    base_ref,
    live_ref,
    p_ref,
    q_ref,
    g_ref,
    o_ref,
    inv_ref,
    vec_ref,
    info_ref,
    kv_ref,
    hot_ref,
    rel_ref,
    dq_ref,
    dkv_ref,
    drel_ref,
    small_ref,
    turn_scr,
    dd_scr,
    acc_scr,
    accr_scr,
    dkv_scr,
    drel_scr,
    keys_scr,
    flip_scr,
    list_scr,
):
    block = pl.program_id(0)
    length = nkb * KB
    row = base_ref[0] + base_ref[1] * block
    base = nkb * KB - R - R * row
    count = live_list(live_ref, list_scr, row, nkb)

    @pl.when(block == 0)
    def start():
        dkv_scr[...] = jnp.zeros(dkv_scr.shape, F32)
        drel_scr[...] = jnp.zeros(drel_scr.shape, F32)
        small_ref[...] = jnp.zeros(small_ref.shape, F32)
        flip = reversal()
        flip_scr[...] = flip
        for kb in range(nkb):
            rows = slice(kb * KB, (kb + 1) * KB)
            keys_scr[rows, :256] = mm(flip, kv_ref[rows, :]).astype(BF)
            keys_scr[rows, 256:] = mm(flip, hot_ref[rows, :]).astype(BF)

    lane = lax.broadcasted_iota(jnp.int32, (2 * R, 128), 1)
    zero = jnp.zeros((2 * R, DH), BF)
    for h in range(2):
        half = slice(DH * h, DH * h + DH)
        q = q_ref[:, half]
        plain = (q + vec_ref[0:1, half]) * (SCALE * LOG2E)
        place = (q + vec_ref[1:2, half]) * (SCALE * LOG2E)
        g = g_ref[:, half].astype(F32)
        inverse = inv_ref[:, DH * h : DH * h + 1]
        delta = -jnp.sum(g * o_ref[:, half], axis=1, keepdims=True) * inverse
        high = delta.astype(BF).astype(F32)
        extra = jnp.where(lane == ONES, high, jnp.where(lane == ONES + 1, delta - high, 0.0))
        side = lambda x: [x, zero] if h == 0 else [zero, x]
        scaled = g * inverse
        dd_scr[h] = jnp.concatenate(side(scaled.astype(BF)) + [extra.astype(BF)], axis=1)
        for i, x in enumerate((plain, scaled, place)):
            turn_scr[h, i] = x.T.astype(BF)
    acc_scr[...] = jnp.zeros(acc_scr.shape, F32)
    accr_scr[...] = jnp.zeros(accr_scr.shape, F32)

    def step(blocks):
        pad = jnp.zeros((R, W - KB), F32)
        d_query = [0.0, 0.0]
        d_place = [0.0, 0.0]
        for n in blocks:
            k0 = pl.multiple_of(list_scr[n] * KB, KB)
            r0 = pl.multiple_of(2 * length - base - k0 - W, 128)
            window = rel_ref[pl.ds(r0, W), :]
            keys = jnp.concatenate(
                [keys_scr[pl.ds(k0, KB), :128], keys_scr[pl.ds(k0, KB), 256:]], axis=1
            )
            values = keys_scr[pl.ds(k0, KB), 128:]
            for h in range(2):
                p = p_ref[0, h, n]
                wide = p.astype(F32) * mm(dd_scr[h], values, 1, 1)
                ds = wide.astype(BF)
                d_query[h] += mm(ds, keys)
                full = [
                    pltpu.roll(
                        jnp.concatenate([wide[i * R : i * R + R], pad], axis=1),
                        0,
                        1,
                        stride=1,
                        stride_axis=0,
                    )
                    for i in range(2)
                ]
                full = jnp.concatenate(full, axis=0).astype(BF)
                d_place[h] += mm(full, window)
                low, high = DH * h, DH * h + DH
                dkv_scr[low:high, pl.ds(k0, KB)] += mm(turn_scr[h, 0], ds)
                dkv_scr[128 + low : 128 + high, pl.ds(k0, KB)] += mm(turn_scr[h, 1], p)
                drel_scr[low:high, pl.ds(r0, W)] += mm(turn_scr[h, 2], full)
        for h in range(2):
            acc_scr[h] += d_query[h]
            accr_scr[h] += d_place[h]

    by_two(count, step)
    hot_row = row_features(info_ref[:, 0:1])
    for h in range(2):
        half = slice(DH * h, DH * h + DH)
        acc = acc_scr[h]
        d_plain = acc[:, half] * SCALE
        d_place = accr_scr[h][:, half] * SCALE
        sums = jnp.where(lane < NS, acc[:, 128:], 0.0) * SCALE
        same = jnp.sum(sums * hot_row, axis=1, keepdims=True)
        other = jnp.sum(sums, axis=1, keepdims=True) - same
        d_label = same * vec_ref[3:4, half] + other * vec_ref[4:5, half]
        label = q_ref[:, half] + vec_ref[2:3, half]
        dq_ref[:, half] = (d_plain + d_place + d_label).astype(BF)
        terms = [d_plain, d_place, d_label, same * label, other * label]
        for row, term in enumerate(terms):
            small_ref[row : row + 1, half] += jnp.sum(term, axis=0, keepdims=True)

    @pl.when(block == nb - 1)
    def finish():
        down = lax.broadcasted_iota(jnp.int32, (256, KB), 0)
        factor = jnp.where(down < 128, LN2, 1.0)
        for kb in range(nkb):
            cols = slice(kb * KB, (kb + 1) * KB)
            dkv_ref[:, cols] = mm((dkv_scr[:, cols] * factor).astype(BF), flip_scr[...]).astype(BF)
        drel_ref[...] = (drel_scr[...] * LN2).astype(BF)


def attend_backward(pair, after, base, live, p, q, g, o, inv, vec, info, kv, hot, rel):
    nb = q.shape[0] // (2 * R)
    length = kv.shape[0]
    nkb = length // KB
    own = pl.BlockSpec((2 * R, 128), lambda b, *_: (b, 0))
    rows = pl.BlockSpec((2 * R, 128), lambda b, *_: (b, pair))
    return pl.pallas_call(
        ordered(functools.partial(backward_kernel, nkb, nb), 12, len(after)),
        grid_spec=pltpu.PrefetchScalarGridSpec(
            num_scalar_prefetch=2,
            grid=(nb,),
            in_specs=[
                pl.BlockSpec((1, 2, nkb, 2 * R, KB), lambda b, *_: (b, 0, 0, 0, 0)),
                rows,
                rows,
                own,
                own,
                pl.BlockSpec((8, 128), lambda b, *_: (0, pair)),
                pl.BlockSpec((2 * R, 128), lambda b, *_: (b, 0)),
                pl.BlockSpec((length, 256), lambda b, *_: (0, pair)),
                pl.BlockSpec((length, 128), lambda b, *_: (0, 0)),
                pl.BlockSpec((2 * length, 128), lambda b, *_: (0, pair)),
            ]
            + [pl.BlockSpec(memory_space=pl.ANY)] * len(after),
            out_specs=[
                own,
                pl.BlockSpec((256, length), lambda b, *_: (0, 0)),
                pl.BlockSpec((128, 2 * length), lambda b, *_: (0, 0)),
                pl.BlockSpec((8, 128), lambda b, *_: (0, 0)),
            ],
            scratch_shapes=[
                pltpu.VMEM((2, 3, DH, 2 * R), BF),
                pltpu.VMEM((2, 2 * R, 256), BF),
                pltpu.VMEM((2, 2 * R, 256), F32),
                pltpu.VMEM((2, 2 * R, 128), F32),
                pltpu.VMEM((256, length), F32),
                pltpu.VMEM((128, 2 * length), F32),
                pltpu.VMEM((length, 384), BF),
                pltpu.VMEM((KB, KB), BF),
                pltpu.SMEM((nkb + 1,), jnp.int32),
            ],
        ),
        out_shape=[
            jax.ShapeDtypeStruct((q.shape[0], 128), BF),
            jax.ShapeDtypeStruct((256, length), BF),
            jax.ShapeDtypeStruct((128, 2 * length), BF),
            jax.ShapeDtypeStruct((8, 128), F32),
        ],
        compiler_params=pltpu.CompilerParams(
            dimension_semantics=("arbitrary",), vmem_limit_bytes=VMEM
        ),
        cost_estimate=pl.CostEstimate(
            flops=10**8, bytes_accessed=10**6, transcendentals=0
        ),
        name="attend_backward",
    )(base, live, p, q, g, o, inv, vec, info, kv, hot, rel, *after)


def whole_block(x):
    return pl.BlockSpec(x.shape, lambda i: (0,) * len(x.shape))


def pack_kernel(r, ws, low_ref, content_ref, seg_ref, rank_ref, flag_ref, parent_ref, *refs):
    vec_refs, weight_refs, (a_ref, b_ref, scr) = refs[:4], refs[4:8], refs[8:]
    low = low_ref[0]
    for e, out in enumerate((a_ref, b_ref)):
        tree = jnp.bitwise_xor(low, e)
        out[:r, :] = content_ref[tree]
        scr[...] = jnp.zeros(scr.shape, F32)
        row = lambda ref: ref[pl.ds(tree, 1), :]
        rank = row(rank_ref)
        scr[0:1, :r] = row(seg_ref).astype(F32)
        scr[0:1, r : 2 * r] = lax.shift_right_logical(rank, 6).astype(F32)
        scr[0:1, 2 * r : 3 * r] = jnp.bitwise_and(rank, 63).astype(F32)
        scr[0:1, 3 * r : 4 * r] = row(flag_ref).astype(F32)
        scr[0:1, 4 * r : 4 * r + NS] = row(parent_ref).astype(F32)
        for i in range(3):
            scr[i + 1 : i + 2, :ws] = vec_refs[i][...].astype(F32)
        scr[4:6, :ws] = vec_refs[3][...].astype(F32)
        out[r : r + 16, :] = scr[...].astype(BF)
        for i in range(4):
            out[r + 16 + i * ws : r + 16 + (i + 1) * ws, :] = weight_refs[i][...]


def pack(low, content, segs, ranks, flags, parents, vecs, weights):
    trees, r, d = content.shape
    ws = weights[0].shape[0]
    shape = jax.ShapeDtypeStruct((r + 16 + 4 * ws, d), BF)
    return pl.pallas_call(
        functools.partial(pack_kernel, r, ws),
        grid=(1,),
        in_specs=[pl.BlockSpec(memory_space=pltpu.SMEM), whole_block(content)]
        + [whole_block(x) for x in (segs, ranks, flags, parents, *vecs, *weights)],
        out_specs=[whole_block(shape)] * 2,
        out_shape=[shape, shape],
        scratch_shapes=[pltpu.VMEM((16, d), F32)],
        compiler_params=pltpu.CompilerParams(vmem_limit_bytes=VMEM),
        name="pack",
    )(low, content, segs, ranks, flags, parents, *vecs, *weights)


def assemble_kernel(r, ws, dh, m, at_ref, a0, a1, t0, t1, q_own, q_other, *outs):
    content_ref, codes_ref, wq_ref, wkv_ref, wr_ref, inputs_ref = outs
    k, low, c = at_ref[0], at_ref[1], at_ref[2]
    h, zl = pl.program_id(0), pl.program_id(1)
    column = lambda start: pl.multiple_of(k * dh + start, 128)

    def fill(src, query):
        inputs_ref[0, 0, 0] = src[0, :r, :]
        inputs_ref[0, 0, 1] = query[...]
        for step in range(m):
            to = jnp.bitwise_xor(c, step)
            rows = lambda i: slice(r + 16 + i * ws, r + 16 + (i + 1) * ws)
            content_ref[0, 0, to] = src[step, :r, :]
            codes_ref[0, 0, to] = src[step, r : r + 16, :]
            wq_ref[0, 0, to] = src[step, rows(0), pl.ds(column(0), dh)]
            wr_ref[0, 0, to] = src[step, rows(3), pl.ds(column(0), dh)]
            for p in range(dh // 128):
                for i in range(2):
                    wkv_ref[0, 0, to, :, 256 * p + 128 * i : 256 * p + 128 * i + 128] = src[
                        step, rows(1 + i), pl.ds(column(128 * p), 128)
                    ]

    for mine in (True, False):
        for e in range(2):
            src = ((a0, a1) if mine else (t0, t1))[e]
            query = (q_own if mine else q_other).at[e]

            @pl.when(((h == k) == mine) & (jnp.bitwise_xor(zl, low) == e))
            def case(src=src, query=query):
                fill(src, query)


def assemble(at, near_rows, their_rows, q_own, q_other, r, ws, after):
    m, rows, d = near_rows[0].shape
    dh = d // 2
    sizes = [(m, r, d), (m, 16, d), (m, ws, dh), (m, ws, d), (m, ws, dh), (2, r, d)]
    return pl.pallas_call(
        ordered(functools.partial(assemble_kernel, r, ws, dh, m), 7, len(after)),
        grid=(2, 2),
        in_specs=[pl.BlockSpec(memory_space=pltpu.SMEM)]
        + [pl.BlockSpec((m, rows, d), lambda h, z: (0, 0, 0))] * 4
        + [pl.BlockSpec((2, r, d), lambda h, z: (0, 0, 0))] * 2
        + [pl.BlockSpec(memory_space=pl.ANY)] * len(after),
        out_specs=[pl.BlockSpec((1, 1) + size, lambda h, z: (h, z, 0, 0, 0)) for size in sizes],
        out_shape=[jax.ShapeDtypeStruct((2, 2) + size, BF) for size in sizes],
        compiler_params=pltpu.CompilerParams(vmem_limit_bytes=SMALL),
        name="assemble",
    )(at, *near_rows, *their_rows, q_own, q_other, *after)


def pack_late_kernel(ws, w1_ref, wo_ref, w2_ref, *refs):
    vec_refs, out, scr = refs[:-2], refs[-2], refs[-1]
    d = wo_ref.shape[1]
    parts = w1_ref.shape[1] // d
    for j in range(parts):
        out[j * ws : (j + 1) * ws, :] = w1_ref[:, j * d : (j + 1) * d]
    out[parts * ws : (parts + 1) * ws, :] = wo_ref[...]
    out[(parts + 1) * ws : (2 * parts + 1) * ws, :] = w2_ref[...]
    scr[...] = jnp.zeros(scr.shape, F32)
    row = 0
    for ref in vec_refs:
        scr[row : row + ref.shape[0], : ref.shape[1]] = ref[...].astype(F32)
        row += ref.shape[0]
    out[(2 * parts + 1) * ws :, :] = scr[...].astype(BF)


def pack_late(w1, wo, w2, vecs):
    ws, d = wo.shape
    rows = ws + w1.shape[1] // d * ws + w2.shape[0] + 16
    return pl.pallas_call(
        functools.partial(pack_late_kernel, ws),
        grid=(1,),
        in_specs=[whole_block(x) for x in (w1, wo, w2, *vecs)],
        out_specs=pl.BlockSpec((rows, d), lambda i: (0, 0)),
        out_shape=jax.ShapeDtypeStruct((rows, d), BF),
        scratch_shapes=[pltpu.VMEM((16, d), F32)],
        compiler_params=pltpu.CompilerParams(vmem_limit_bytes=SMALL),
        name="pack_late",
    )(w1, wo, w2, *vecs)


def assemble_late_kernel(ws, m, at_ref, *refs):
    mine_refs, their_refs, (w1_ref, wo_ref, w2_ref, vec_ref) = refs[:m], refs[m : 2 * m], refs[2 * m :]
    k, low, c = at_ref[0], at_ref[1], at_ref[2]
    h, zl = pl.program_id(0), pl.program_id(1)
    d = wo_ref.shape[-1]
    parts = w1_ref.shape[-1] // d
    e = jnp.bitwise_xor(zl, low)

    def fill(refs):
        for step, src in enumerate(refs):
            to = jnp.bitwise_xor(c, step)
            for j in range(parts):
                w1_ref[0, 0, to, :, j * d : (j + 1) * d] = src[e, j * ws : (j + 1) * ws, :]
            wo_ref[0, 0, to] = src[e, parts * ws : (parts + 1) * ws, :]
            w2_ref[0, 0, to] = src[e, (parts + 1) * ws : (2 * parts + 1) * ws, :]
            vec_ref[0, 0, to] = src[e, (2 * parts + 1) * ws :, :]

    @pl.when(h == k)
    def own():
        fill(mine_refs)

    @pl.when(h != k)
    def other():
        fill(their_refs)


def assemble_late(at, mine, theirs, ws, parts):
    m = len(mine)
    two, rows, d = mine[0].shape
    sizes = [(m, ws, parts * d), (m, ws, d), (m, parts * ws, d), (m, 16, d)]
    return pl.pallas_call(
        functools.partial(assemble_late_kernel, ws, m),
        grid=(2, 2),
        in_specs=[pl.BlockSpec(memory_space=pltpu.SMEM)]
        + [pl.BlockSpec((2, rows, d), lambda h, z: (0, 0, 0))] * (2 * m),
        out_specs=[pl.BlockSpec((1, 1) + size, lambda h, z: (h, z, 0, 0, 0)) for size in sizes],
        out_shape=[jax.ShapeDtypeStruct((2, 2) + size, BF) for size in sizes],
        compiler_params=pltpu.CompilerParams(vmem_limit_bytes=SMALL),
        name="assemble_late",
    )(at, *mine, *theirs)


def relative_kernel(sa_ref, ca_ref, sb_ref, cb_ref, w_ref, pos_ref, rel_ref, turned_ref):
    half = sb_ref.shape[1]
    fine = sb_ref.shape[0]
    for i in range(pos_ref.shape[0] // fine):
        rows = slice(i * fine, (i + 1) * fine)
        sa, ca = sa_ref[0, i : i + 1, :], ca_ref[0, i : i + 1, :]
        sine = sa * cb_ref[...] - ca * sb_ref[...]
        cosine = ca * cb_ref[...] + sa * sb_ref[...]
        pos_ref[rows, :half] = sine.astype(BF)
        pos_ref[rows, half:] = cosine.astype(BF)
    from_sine = mm(pos_ref[:, :half], w_ref[:half, :])
    from_cosine = mm(pos_ref[:, half:], w_ref[half:, :])
    rel_ref[...] = (from_cosine + from_sine).astype(BF)
    turned_ref[...] = (from_cosine - from_sine).astype(BF)


def relative(wr, length):
    d, width = wr.shape
    half, fine = d // 2, 64
    powers = jnp.arange(half, dtype=F32) * (2.0 / d)
    inverse_freq = 1.0 / 10000.0**powers
    coarse = (length - 1 - fine * jnp.arange(2 * length // fine, dtype=jnp.int32)).astype(F32)
    a = coarse[:, None] * inverse_freq[None]
    b = jnp.arange(fine, dtype=F32)[:, None] * inverse_freq[None]
    size = 1024
    per = size // fine
    tables = [jnp.sin(a).reshape(-1, per, half), jnp.cos(a).reshape(-1, per, half), jnp.sin(b), jnp.cos(b)]
    rows = lambda w: pl.BlockSpec((size, w), lambda i: (i, 0))
    return pl.pallas_call(
        relative_kernel,
        grid=(2 * length // size,),
        in_specs=[pl.BlockSpec((1, per, half), lambda i: (i, 0, 0))] * 2
        + [pl.BlockSpec((fine, half), lambda i: (0, 0))] * 2
        + [pl.BlockSpec((d, width), lambda i: (0, 0))],
        out_specs=[rows(d), rows(width), rows(width)],
        out_shape=[
            jax.ShapeDtypeStruct((2 * length, d), BF),
            jax.ShapeDtypeStruct((2 * length, width), BF),
            jax.ShapeDtypeStruct((2 * length, width), BF),
        ],
        compiler_params=pltpu.CompilerParams(vmem_limit_bytes=SMALL),
        cost_estimate=pl.CostEstimate(
            flops=4 * length * d * width, bytes_accessed=8 * length * d, transcendentals=0
        ),
        name="relative",
    )(*tables, wr)


def input_grad_kernel(count, turned, at_ref, *refs):
    parts, w_ref, out_ref = refs[:count], refs[count], refs[-1]
    total = 0.0
    start = 0
    for ref in parts:
        width = ref.shape[0 if turned else 1]
        total += mm(ref[...], w_ref[:, start : start + width], 0 if turned else 1, 1)
        start += width
    out_ref[...] = total.astype(out_ref.dtype)


def input_grad(half, parts, w, dtype, after, turned=False):
    rows = parts[0].shape[1 if turned else 0] // 2
    block = math.gcd(rows, 512)
    blocks = rows // block
    d = w.shape[0]
    return pl.pallas_call(
        ordered(
            functools.partial(input_grad_kernel, len(parts), turned), len(parts) + 2, len(after)
        ),
        grid_spec=pltpu.PrefetchScalarGridSpec(
            num_scalar_prefetch=1,
            grid=(rows // block,),
            in_specs=[
                pl.BlockSpec((x.shape[0], block), lambda i, at: (0, at[0] * blocks + i))
                if turned
                else pl.BlockSpec((block, x.shape[1]), lambda i, at: (at[0] * blocks + i, 0))
                for x in parts
            ]
            + [pl.BlockSpec(w.shape, lambda i, at: (0, 0))]
            + [pl.BlockSpec(memory_space=pl.ANY)] * len(after),
            out_specs=pl.BlockSpec((block, d), lambda i, at: (i, 0)),
        ),
        out_shape=jax.ShapeDtypeStruct((rows, d), dtype),
        compiler_params=pltpu.CompilerParams(vmem_limit_bytes=SMALL),
        cost_estimate=pl.CostEstimate(
            flops=2 * rows * d * w.shape[1], bytes_accessed=4 * rows * d, transcendentals=0
        ),
        name="input_grad",
    )(half, *parts, w, *after)


def mask_kernel(n, m, r, c_ref, codes_ref, rank_ref, hot_ref, info_ref, reach_ref, live_ref):
    c = c_ref[0]
    iota = lambda shape, axis: lax.broadcasted_iota(jnp.int32, shape, axis)
    choose = iota((n, 16 * n), 1) == 16 * iota((n, 16 * n), 0)
    rows = mm(choose.astype(F32).astype(BF), codes_ref[...])
    part = lambda i: rows[:, i * r : (i + 1) * r]
    segs = part(0)
    ranks = part(1) * 64.0 + part(2)
    flags = part(3)
    seg_cols, rank_cols, flag_cols = segs.T, ranks.T, flags.T
    parent_col = rows[:, 4 * r : 4 * r + 128].T[:, 0:1]
    lane = iota((128, 128), 1)
    down = iota((128, 128), 0)
    feature = jnp.where(lane < NS, lane, jnp.where(lane < 2 * NS, lane - NS, -1))
    folded = feature.astype(F32)
    ones_lane = (lane == ONES) | (lane == ONES + 1)
    for i in range(n):
        rank_ref[0:1, i * r : (i + 1) * r] = ranks[i : i + 1, :]
        hit = (folded == seg_cols[:, i : i + 1]) | ones_lane
        hot_ref[i * r : (i + 1) * r, :] = jnp.where(hit, 1.0, 0.0).astype(BF)
    mine = iota((r, n), 1)
    for b in range(n // m):
        column = lambda x: jnp.sum(jnp.where(mine == b * m + c, x, 0.0), axis=1, keepdims=True)
        seg, limit = column(seg_cols), column(rank_cols)
        lower = limit - column(flag_cols)
        for i, value in enumerate((limit, lower)):
            start = (2 * b + i) * r
            info_ref[start : start + r, :] = jnp.where(lane == 0, seg, value)
    inside = (down < NS) & (lane < NS)
    link = inside & ((down == lane) | (parent_col == lane.astype(F32)))
    reached = jnp.where(link, 1.0, 0.0)
    for repeat in range(4):
        half = reached.astype(BF)
        reached = jnp.minimum(mm(half, half), 1.0)
    reached = reached.astype(BF)
    twice = jnp.where(down == feature, 1.0, 0.0).astype(BF)
    reach_ref[...] = mm(reached, twice).astype(BF)
    spot = iota((n, 128), 1)
    present = jnp.zeros((n, 128), F32)
    for t in range(NS):
        any_t = jnp.max(jnp.where(segs == t, 1.0, 0.0), axis=1, keepdims=True)
        present = jnp.where(spot == t, any_t, present)
    present = present.astype(BF)
    seen = jnp.minimum(mm(present, reached), 1.0).astype(BF)
    live_ref[...] = jnp.minimum(mm(seen, present, 1, 1), 1.0).astype(jnp.int32)


def masks(c, codes, m, r):
    n, length = codes.shape[0] // 16, codes.shape[0] // 16 * r
    return pl.pallas_call(
        functools.partial(mask_kernel, n, m, r),
        grid=(1,),
        in_specs=[pl.BlockSpec(memory_space=pltpu.SMEM), whole_block(codes)],
        out_specs=[
            pl.BlockSpec(size, lambda i: (0, 0))
            for size in ((1, length), (length, 128), (n // m * 2 * r, 128), (128, 128), (n, n))
        ],
        out_shape=[
            jax.ShapeDtypeStruct((1, length), F32),
            jax.ShapeDtypeStruct((length, 128), BF),
            jax.ShapeDtypeStruct((n // m * 2 * r, 128), F32),
            jax.ShapeDtypeStruct((128, 128), BF),
            jax.ShapeDtypeStruct((n, n), jnp.int32),
        ],
        compiler_params=pltpu.CompilerParams(vmem_limit_bytes=SMALL),
        name="masks",
    )(c, codes)


def hold_kernel(a_ref, b_ref, out_ref):
    out_ref[0] = a_ref[...]
    out_ref[1] = b_ref[...]


def hold(a, b, after):
    spec = pl.BlockSpec(a.shape, lambda i: (0, 0))
    return pl.pallas_call(
        ordered(hold_kernel, 2, len(after)),
        grid=(1,),
        in_specs=[spec, spec] + [pl.BlockSpec(memory_space=pl.ANY)] * len(after),
        out_specs=pl.BlockSpec((2,) + a.shape, lambda i: (0, 0, 0)),
        out_shape=jax.ShapeDtypeStruct((2,) + a.shape, a.dtype),
        compiler_params=pltpu.CompilerParams(vmem_limit_bytes=SMALL),
        name="hold",
    )(a, b, *after)


def proj_grad_kernel(count, steps, x_ref, c_ref, pos_ref, *refs):
    dq, dkv, drel = refs[:count], refs[count : 2 * count], refs[2 * count : 3 * count]
    extra = refs[3 * count : -4]
    out_ref, q_scr, kv_scr, r_scr = refs[-4:]
    i = pl.program_id(0)

    @pl.when(i == 0)
    def start():
        for scr in (q_scr, kv_scr, r_scr):
            scr[...] = jnp.zeros(scr.shape, F32)

    beside = lambda refs, axis: jnp.concatenate([ref[...] for ref in refs], axis=axis)
    r_scr[...] += mm(beside(drel, 0), pos_ref[...])

    @pl.when(i < steps[1])
    def keys():
        kv_scr[...] += mm(beside(dkv, 0), c_ref[...])

    @pl.when(i < steps[0])
    def queries():
        q_scr[...] += mm(beside(dq, 1), x_ref[...], 0, 0)

    @pl.when(i == steps[2] - 1)
    def finish():
        d = pos_ref.shape[1]
        lane = lax.broadcasted_iota(jnp.int32, (128, d), 1)
        for p in range(count):
            at = 512 * p
            rows = slice(128 * p, 128 * p + 128)
            out_ref[:, at : at + 128] = q_scr[rows, :].T.astype(BF)
            out_ref[:, at + 128 : at + 384] = kv_scr[256 * p : 256 * p + 256, :].T.astype(BF)
            turned = jnp.where(lane < d // 2, -r_scr[rows, :], r_scr[rows, :])
            out_ref[:, at + 384 : at + 512] = turned.T.astype(BF)
        for ref in extra:
            out_ref[:, 512 * count :] = ref[...]


def proj_grads(x, content, position, parts, extra, after):
    count = len(parts)
    d = x.shape[1]
    size = 1024
    steps = [a.shape[0] // size for a in (x, content, position)]
    spec = lambda width, kind: pl.BlockSpec(
        (size, width), lambda i: (jnp.minimum(i, steps[kind] - 1), 0)
    )
    turned = lambda width, kind: pl.BlockSpec(
        (width, size), lambda i: (0, jnp.minimum(i, steps[kind] - 1))
    )
    operands = [x, content, position]
    specs = [spec(d, kind) for kind in range(3)]
    for index, one in enumerate((spec(128, 0), turned(256, 1), turned(128, 2))):
        operands += [b[index] for b in parts]
        specs += [one] * count
    operands += extra
    specs += [pl.BlockSpec(e.shape, lambda i: (0, 0)) for e in extra]
    width = 512 * count + sum(e.shape[1] for e in extra)
    total = len(operands)
    return pl.pallas_call(
        ordered(functools.partial(proj_grad_kernel, count, steps), total, len(after)),
        grid=(steps[2],),
        in_specs=specs + [pl.BlockSpec(memory_space=pl.ANY)] * len(after),
        out_specs=pl.BlockSpec((d, width), lambda i: (0, 0)),
        out_shape=jax.ShapeDtypeStruct((d, width), BF),
        scratch_shapes=[
            pltpu.VMEM((count * 128, d), F32),
            pltpu.VMEM((count * 256, d), F32),
            pltpu.VMEM((count * 128, d), F32),
        ],
        compiler_params=pltpu.CompilerParams(vmem_limit_bytes=VMEM),
        cost_estimate=pl.CostEstimate(flops=10**9, bytes_accessed=10**6, transcendentals=0),
        name="proj_grads",
    )(*operands, *after)


def add_kernel(count, *refs):
    total = refs[0][...].astype(F32)
    for ref in refs[1:count]:
        total += ref[...].astype(F32)
    refs[-1][...] = total.astype(refs[-1].dtype)


def add_up(parts, dtype, after):
    shape = parts[0].shape
    rows = parts[0].size // shape[-1]
    flat = [x.reshape(rows, shape[-1]) for x in parts]
    block = rows // 2 if rows % 32 == 0 else rows
    spec = pl.BlockSpec((block, shape[-1]), lambda i: (i, 0))
    out = pl.pallas_call(
        ordered(functools.partial(add_kernel, len(parts)), len(parts), len(after)),
        grid=(rows // block,),
        in_specs=[spec] * len(parts) + [pl.BlockSpec(memory_space=pl.ANY)] * len(after),
        out_specs=spec,
        out_shape=jax.ShapeDtypeStruct((rows, shape[-1]), dtype),
        compiler_params=pltpu.CompilerParams(vmem_limit_bytes=SMALL),
        cost_estimate=pl.CostEstimate(flops=rows, bytes_accessed=10**6, transcendentals=0),
        name="add_up",
    )(*flat, *after)
    return out.reshape(shape)


def fold_kernel(m, count, at_ref, *refs):
    for step in range(m):
        total = refs[step * count][0, 0].astype(F32)
        for ref in refs[step * count + 1 : (step + 1) * count]:
            total += ref[0, 0].astype(F32)
        refs[m * count + step][0] = total.astype(BF)


def fold(at, arrays, after):
    two, m, rows, width = arrays[0].shape
    count = len(arrays)
    spec = lambda step: pl.BlockSpec(
        (1, 1, rows, width), lambda i, at: (i, jnp.bitwise_xor(at[2], step), 0, 0)
    )
    return pl.pallas_call(
        ordered(functools.partial(fold_kernel, m, count), m * count + 1, len(after)),
        grid_spec=pltpu.PrefetchScalarGridSpec(
            num_scalar_prefetch=1,
            grid=(2,),
            in_specs=[spec(step) for step in range(m) for x in arrays]
            + [pl.BlockSpec(memory_space=pl.ANY)] * len(after),
            out_specs=[pl.BlockSpec((1, rows, width), lambda i, at: (i, 0, 0))] * m,
        ),
        out_shape=[jax.ShapeDtypeStruct((2, rows, width), BF)] * m,
        compiler_params=pltpu.CompilerParams(vmem_limit_bytes=SMALL),
        cost_estimate=pl.CostEstimate(flops=rows, bytes_accessed=10**6, transcendentals=0),
        name="fold",
    )(at, *(list(arrays) * m), *after)


def join_kernel(count, at_ref, *refs):
    for e in range(2):
        total = refs[e * count][0].astype(F32)
        for ref in refs[e * count + 1 : (e + 1) * count]:
            total += ref[0].astype(F32)
        refs[2 * count + e][...] = total.astype(BF)


def join(at, arrays, after):
    two, rows, width = arrays[0].shape
    count = len(arrays)
    spec = lambda e: pl.BlockSpec(
        (1, rows, width), lambda i, at: (jnp.bitwise_xor(at[1], e), 0, 0)
    )
    return pl.pallas_call(
        ordered(functools.partial(join_kernel, count), 2 * count + 1, len(after)),
        grid_spec=pltpu.PrefetchScalarGridSpec(
            num_scalar_prefetch=1,
            grid=(1,),
            in_specs=[spec(e) for e in range(2) for x in arrays]
            + [pl.BlockSpec(memory_space=pl.ANY)] * len(after),
            out_specs=[pl.BlockSpec((rows, width), lambda i, at: (0, 0))] * 2,
        ),
        out_shape=[jax.ShapeDtypeStruct((rows, width), BF)] * 2,
        compiler_params=pltpu.CompilerParams(vmem_limit_bytes=SMALL),
        cost_estimate=pl.CostEstimate(flops=rows, bytes_accessed=10**6, transcendentals=0),
        name="join",
    )(at, *(list(arrays) * 2), *after)


GELU_A = 0.7978845608028654
GELU_B = 0.044715


def gelu_and_slope(v):
    square = v * v
    t = jnp.tanh(GELU_A * (v + GELU_B * (v * square)))
    half = 0.5 + 0.5 * t
    slope = half + 0.5 * v * (1.0 - t * t) * (GELU_A * (1.0 + 3.0 * GELU_B * square))
    return v * half, slope


def norm_forward(x):
    average = jnp.mean(x, axis=1, keepdims=True)
    centred = x - average
    inverse = lax.rsqrt(jnp.mean(centred * centred, axis=1, keepdims=True) + EPSILON)
    return centred * inverse, inverse


def norm_backward(grad, gain, unit, inverse):
    scaled = grad * gain
    pull = jnp.mean(scaled, axis=1, keepdims=True)
    twist = jnp.mean(scaled * unit, axis=1, keepdims=True)
    return inverse * (scaled - pull - unit * twist)


def dense_kernel(m, n, ws, pairs, at_ref, *refs):
    own_mixed, got_mixed = refs[:pairs], refs[pairs : 2 * pairs]
    x_ref, cot_ref = refs[2 * pairs : 2 * pairs + 2]
    pieces = refs[2 * pairs + 2 : 2 * pairs + 2 + 2 * m]
    rest = refs[2 * pairs + 2 + 2 * m :]
    result_ref, gr_ref, gm_own, gm_other, vec_ref, b1_ref = rest[:6]
    early_own, early_other, late_own, late_other = rest[6:10]
    w1, w2, wo, vp, slope, hidden, unit_bf, mixed, early, late, bias, sems, out_sems = rest[10:]
    k, low, c = at_ref[0], at_ref[1], at_ref[2]
    d = x_ref.shape[1]
    ff = w1.shape[1]
    parts = ff // d
    fs = parts * ws
    places = []
    for index, piece in enumerate(pieces):
        h = k if index < m else 1 - k
        for e in range(2):
            s = (2 * h + jnp.bitwise_xor(low, e)) * m + jnp.bitwise_xor(c, index % m)
            places.append((piece.at[e], s))
    kinds = 2 + parts + 1

    def load(i, kind, j=0):
        src, s = places[i]
        to = pl.ds(pl.multiple_of(s * ws, 16), ws)
        if kind == 0:
            pair = (src.at[pl.ds(parts * ws, ws), :], wo.at[to, :])
        elif kind == 1:
            pair = (src.at[pl.ds((2 * parts + 1) * ws, 16), :], vp.at[s])
        elif kind == 2:
            rows = pl.ds(pl.multiple_of(j * ws, 16), ws)
            pair = (src.at[rows, :], w1.at[to, pl.ds(pl.multiple_of(j * d, 128), d)])
        else:
            to = pl.ds(pl.multiple_of(s * fs, 16), fs)
            pair = (src.at[pl.ds((parts + 1) * ws, fs), :], w2.at[to, :])
        at = i * kinds + (kind if kind < 2 else 2 + j if kind == 2 else kinds - 1)
        return pltpu.make_async_copy(*pair, sems.at[at])

    count = len(places)
    for kind in (0, 1):
        for i in range(count):
            load(i, kind).start()
    for j in range(parts):
        for i in range(count):
            load(i, 2, j).start()
    for i in range(count):
        load(i, 3).start()

    for p in range(pairs):
        lanes = slice(128 * p, 128 * p + 128)
        other = slice(d // 2 + 128 * p, d // 2 + 128 * p + 128)

        @pl.when(k == 0)
        def low_core():
            mixed[:, lanes] = own_mixed[p][...]
            mixed[:, other] = got_mixed[p][...]

        @pl.when(k != 0)
        def high_core():
            mixed[:, lanes] = got_mixed[p][...]
            mixed[:, other] = own_mixed[p][...]

    for kind in (0, 1):
        for i in range(count):
            load(i, kind).wait()
    spot = lax.broadcasted_iota(jnp.int32, (128, d), 1)
    down = lax.broadcasted_iota(jnp.int32, (128, d), 0)
    vecs = jnp.zeros((16, d), F32)
    for s in range(n):
        place = jnp.where((spot == s * ws + down) & (down < ws), 1.0, 0.0).astype(BF)
        vecs += mm(vp[s, :, :128], place)
    per = (d // 2) // fs
    spot = lax.broadcasted_iota(jnp.int32, (256, d // 2), 1)
    down = lax.broadcasted_iota(jnp.int32, (256, d // 2), 0)
    place = [
        jnp.where((spot == t * fs + down) & (down < fs), 1.0, 0.0).astype(BF) for t in range(per)
    ]
    for q in range(n // per):
        row = sum(mm(vp[q * per + t, :, :256], place[t]) for t in range(per))
        bias[:, q * (d // 2) : (q + 1) * (d // 2)] = row[:8]
    outer_shift, gain_one, shift_one, gain_two, shift_two = [vecs[i : i + 1] for i in range(5)]

    residual = mm(mixed[...], wo[...]) + x_ref[...].astype(F32)
    unit_one, inverse_one = norm_forward(residual)
    normed = unit_one * gain_one + shift_one
    unit_bf[...] = normed.astype(BF)
    total = normed + outer_shift

    def wait_chunk(j):
        for i in range(count):
            load(i, 2, j).wait()

    for j in range(parts):
        wait_chunk(j)
    for j in range(parts):
        cols = slice(j * d, (j + 1) * d)
        value, slant = gelu_and_slope(mm(unit_bf[...], w1[:, cols]) + bias[5:6, cols])
        hidden[:, cols] = value.astype(BF)
        slope[:, cols] = slant
    for i in range(count):
        load(i, 3).wait()
    summed = total + mm(hidden[...], w2[...])
    unit_two, inverse_two = norm_forward(summed)
    result_ref[...] = (unit_two * gain_two + shift_two).astype(BF)
    cot = cot_ref[...].astype(F32)
    grad_summed = norm_backward(cot, gain_two, unit_two, inverse_two)
    row_sum = lambda x: jnp.sum(x, axis=0, keepdims=True)
    vec_ref[0:1, :] = row_sum(grad_summed)
    vec_ref[3:4, :] = row_sum(cot * unit_two)
    vec_ref[4:5, :] = row_sum(cot)
    grad_bf = grad_summed.astype(BF)
    grad_normed = grad_summed
    copies = []
    deep = early.shape[0] // 2
    split = ff // 2 // d

    def send(half, src, own, other):
        sem = out_sems.at[len(copies)]
        copies.append(pltpu.make_async_copy(src, own, sem))

        @pl.when(k == half)
        def keep():
            pltpu.make_async_copy(src, own, sem).start()

        @pl.when(k != half)
        def give():
            pltpu.make_async_copy(src, other, sem).start()

    def send_early(cols):
        for half in range(2):
            src = early.at[half * deep : (half + 1) * deep, cols]
            send(half, src, early_own.at[:, cols], early_other.at[:, cols])

    for j in range(parts):
        cols = slice(j * d, (j + 1) * d)
        grad_inner = mm(grad_bf, w2[cols, :], 1, 1) * slope[:, cols]
        b1_ref[0:1, cols] = row_sum(grad_inner)
        inner_bf = grad_inner.astype(BF)
        late[cols, :] = mm(hidden[:, cols], grad_bf, 0, 0).astype(BF)
        to = pl.ds((j % split) * d, d)
        send(j // split, late.at[cols, :], late_own.at[to, :], late_other.at[to, :])
        early[:, cols] = mm(unit_bf[...], inner_bf, 0, 0).astype(BF)
        send_early(cols)
        grad_normed += mm(inner_bf, w1[:, cols], 1, 1)
    vec_ref[1:2, :] = row_sum(grad_normed * unit_one)
    vec_ref[2:3, :] = row_sum(grad_normed)
    grad_residual = norm_backward(grad_normed, gain_one, unit_one, inverse_one)
    gr_ref[...] = grad_residual
    residual_bf = grad_residual.astype(BF)
    early[:, ff:] = mm(mixed[...], residual_bf, 0, 0).astype(BF)
    send_early(slice(ff, ff + d))
    grad_mixed = mm(residual_bf, wo[...], 1, 1).astype(BF)
    for half in range(2):
        part = grad_mixed[:, half * (d // 2) : (half + 1) * (d // 2)]

        @pl.when(k == half)
        def keep(part=part):
            gm_own[...] = part

        @pl.when(k != half)
        def give(part=part):
            gm_other[...] = part

    for copy in copies:
        copy.wait()


def dense(at, own_mixed, got_mixed, inputs, cots, mine, theirs, ws, ff):
    m = len(mine)
    pairs = len(own_mixed)
    rows, d = cots.shape
    n = d // ws
    parts = ff // d
    anywhere = pl.BlockSpec(memory_space=pl.ANY)
    half = lambda width: pl.BlockSpec((rows, width), lambda i, at: (at[0], 0))
    fixed = lambda *shape: pl.BlockSpec(shape, lambda i, at: (0,) * len(shape))
    return pl.pallas_call(
        functools.partial(dense_kernel, m, n, ws, pairs),
        grid_spec=pltpu.PrefetchScalarGridSpec(
            num_scalar_prefetch=1,
            grid=(1,),
            in_specs=[half(128)] * pairs
            + [fixed(rows, 128)] * pairs
            + [half(d), fixed(rows, d)]
            + [anywhere] * (2 * m),
            out_specs=[
                fixed(rows, d),
                fixed(rows, d),
                fixed(rows, d // 2),
                fixed(rows, d // 2),
                fixed(8, d),
                fixed(8, ff),
            ]
            + [anywhere] * 4,
            scratch_shapes=[
                pltpu.VMEM((d, ff), BF),
                pltpu.VMEM((ff, d), BF),
                pltpu.VMEM((d, d), BF),
                pltpu.VMEM((n, 16, d), BF),
                pltpu.VMEM((rows, ff), F32),
                pltpu.VMEM((rows, ff), BF),
                pltpu.VMEM((rows, d), BF),
                pltpu.VMEM((rows, d), BF),
                pltpu.VMEM((d, ff + d), BF),
                pltpu.VMEM((ff, d), BF),
                pltpu.VMEM((8, ff), F32),
                pltpu.SemaphoreType.DMA((4 * m * (3 + parts),)),
                pltpu.SemaphoreType.DMA((3 * parts + 2,)),
            ],
        ),
        out_shape=[
            jax.ShapeDtypeStruct((rows, d), BF),
            jax.ShapeDtypeStruct((rows, d), F32),
            jax.ShapeDtypeStruct((rows, d // 2), BF),
            jax.ShapeDtypeStruct((rows, d // 2), BF),
            jax.ShapeDtypeStruct((8, d), F32),
            jax.ShapeDtypeStruct((8, ff), F32),
            jax.ShapeDtypeStruct((d // 2, ff + d), BF),
            jax.ShapeDtypeStruct((d // 2, ff + d), BF),
            jax.ShapeDtypeStruct((ff // 2, d), BF),
            jax.ShapeDtypeStruct((ff // 2, d), BF),
        ],
        compiler_params=pltpu.CompilerParams(vmem_limit_bytes=VMEM),
        cost_estimate=pl.CostEstimate(flops=10**9, bytes_accessed=10**6, transcendentals=0),
        name="dense",
    )(at, *own_mixed, *got_mixed, inputs, cots, *mine, *theirs)


def dense_plain(at, own_mixed, got_mixed, inputs, cots, mine, theirs, ws, ff):
    rows, d = cots.shape
    n, fs = d // ws, ff * ws // d
    k = at[0]
    mine_half = lambda x: lax.dynamic_slice_in_dim(x, k * rows, rows, 0)
    inner_w, output_w, outer_w, vecs = assemble_late(at, mine, theirs, ws, ff // d)
    inner_w, output_w = inner_w.reshape(d, ff), output_w.reshape(d, d)
    outer_w = outer_w.reshape(ff, d)
    vecs = vecs.reshape(n, 16, d).astype(F32)
    inner_shift = vecs[:, 5, :fs].reshape(ff)
    vecs = vecs[:, :5, :ws].swapaxes(0, 1).reshape(5, d)
    outer_shift, gain_one, shift_one, gain_two, shift_two = [vecs[i] for i in range(5)]
    own = [mine_half(x) for x in own_mixed]
    mixed = jnp.where(
        k == 0,
        jnp.concatenate(own + got_mixed, axis=1),
        jnp.concatenate(got_mixed + own, axis=1),
    )
    residual = mm(mixed, output_w) + mine_half(inputs).astype(F32)
    unit_one, inverse_one = norm_forward(residual)
    normed = unit_one * gain_one + shift_one
    normed_bf = normed.astype(BF)
    value, slope = gelu_and_slope(mm(normed_bf, inner_w) + inner_shift)
    hidden = value.astype(BF)
    summed = mm(hidden, outer_w) + outer_shift + normed
    unit_two, inverse_two = norm_forward(summed)
    result = (unit_two * gain_two + shift_two).astype(BF)
    cot = cots.astype(F32)
    grad_summed = norm_backward(cot, gain_two, unit_two, inverse_two)
    grad_bf = grad_summed.astype(BF)
    grad_inner = mm(grad_bf, outer_w, 1, 1) * slope
    inner_bf = grad_inner.astype(BF)
    grad_normed = mm(inner_bf, inner_w, 1, 1) + grad_summed
    grad_residual = norm_backward(grad_normed, gain_one, unit_one, inverse_one)
    residual_bf = grad_residual.astype(BF)
    grad_mixed = mm(residual_bf, output_w, 1, 1).astype(BF)
    terms = [grad_summed, grad_normed * unit_one, grad_normed, cot * unit_two, cot]
    early = jnp.concatenate([mm(normed_bf, inner_bf, 0, 0), mm(mixed, residual_bf, 0, 0)], axis=1)

    def halves(x, axis):
        size = x.shape[axis] // 2
        return [lax.dynamic_slice_in_dim(x, i * size, size, axis).astype(BF) for i in (k, 1 - k)]

    return (
        result,
        grad_residual,
        *halves(grad_mixed, 1),
        jnp.stack([jnp.sum(x, axis=0) for x in terms]),
        jnp.sum(grad_inner, axis=0)[None],
        *halves(early, 0),
        *halves(mm(hidden, grad_bf, 0, 0), 0),
    )


def body(
    content_in,
    query_in,
    segment_ids,
    parent_ids,
    rank_order,
    query_flags,
    query_weight,
    key_weight,
    value_weight,
    relative_weight,
    output_weight,
    inner_weight,
    outer_weight,
    inner_bias,
    outer_bias,
    attend_gain,
    attend_shift,
    feed_gain,
    feed_shift,
    content_bias,
    position_bias,
    segment_bias,
    segment_table,
    content_cot,
    query_cot,
):
    n = lax.axis_size("shard")
    nr = lax.axis_size("rep")
    trees, r, d = content_in.shape
    groups = 2 * trees
    m = n // groups
    length = r * n
    nkb = length // KB
    ff = inner_weight.shape[1]
    dh = d // 2
    heads = dh // DH
    pairs = heads // 2
    ws = query_weight.shape[0]
    fs = outer_weight.shape[0]
    me = lax.axis_index("shard")
    g, c = me // m, me % m
    low = g % 2
    k = lax.axis_index("rep") % 2
    first = k == 0
    tie = lax.optimization_barrier

    def swap(x):
        return lax.ppermute(x, "rep", [(i, i ^ 1) for i in range(nr)])

    def far(x, step):
        return lax.ppermute(x, "shard", [(i, i ^ (m * step)) for i in range(n)])

    def near(x, step):
        return lax.ppermute(x, "shard", [(i, i ^ step) for i in range(n)])

    def across(x, e):
        moves = []
        for i in range(nr):
            for j in range(n):
                z = j // m
                to = (i - i % 2 + z // 2) * n + (2 * (i % 2) + (z % 2 ^ e)) * m + j % m
                moves.append((i * n + j, to))
        return lax.ppermute(x, ("rep", "shard"), moves)

    def pick(x, index, axis=0):
        return lax.dynamic_index_in_dim(x, index, axis, keepdims=False)

    def put(buffer, x, index, axis=0):
        return lax.dynamic_update_index_in_dim(buffer, x, index, axis)

    def pair_of(mine, other, index, axis=0):
        return put(jnp.stack([mine, mine], axis), other, 1 - index, axis)

    def cross(parts):
        got = [across(pick(parts, low ^ e), e) for e in range(2)]
        return pair_of(got[0], got[1], low)

    def near_gather(x, downward):
        bits = [b for b in range(m.bit_length() - 1)]
        held = {0: x}
        for b in bits[::-1] if downward else bits:
            held.update({o | 1 << b: near(y, 1 << b) for o, y in list(held.items())})
        return jnp.stack([held[o] for o in range(m)])

    def near_parts(x, axis):
        sent = [near(pick(x, c ^ step, axis), step) for step in range(1, m)]
        return [pick(x, c, axis)] + sent

    def far_sum(x):
        total = pick(x, g).astype(F32)
        for step in range(1, groups):
            total = total + far(pick(x, g ^ step), step).astype(F32)
        return total

    weights = [query_weight, key_weight, value_weight, relative_weight]
    low_array = low.astype(jnp.int32).reshape(1)
    vec_rows = [x.reshape(1, ws) for x in (content_bias, position_bias, segment_bias)]
    packed = pack(
        low_array,
        content_in,
        segment_ids,
        rank_order,
        query_flags,
        parent_ids,
        vec_rows + [segment_table],
        weights,
    )
    at = jnp.stack([k, low, c]).astype(jnp.int32)
    got = [across(packed[e], e) for e in range(2)]
    own_query = jnp.stack([across(pick(query_in, low ^ e), e) for e in range(2)])
    near_rows = [near_gather(got[e], e) for e in range(2)]
    their_rows = [swap(x) for x in near_rows]
    late_pack = pack_late(
        inner_weight,
        output_weight,
        outer_weight,
        [x.reshape(1, ws) for x in (outer_bias, attend_gain, attend_shift, feed_gain, feed_shift)]
        + [inner_bias.reshape(1, fs)],
    )
    late_pack, unused = tie((late_pack, got[1]))
    late = [across(late_pack, e) for e in range(2)]
    content_full, codes, wq, kv_weight, wr, inputs = assemble(
        at, near_rows, their_rows, own_query, swap(own_query), r, ws, []
    )
    content_full = content_full.reshape(length, d)
    wq, kv_weight, wr = wq.reshape(d, dh), kv_weight.reshape(d, d), wr.reshape(d, dh)
    inputs = inputs.reshape(groups * 2 * r, d)
    codes = codes.reshape(n, 16, d)
    key_ranks, hot, info, reach, live = masks(
        c.astype(jnp.int32).reshape(1), codes.reshape(n * 16, d), m, r
    )
    base = jnp.stack([c, m]).astype(jnp.int32)
    vectors = codes[:, 1:6, :ws].astype(F32).swapaxes(0, 1).reshape(5, 2, dh)
    head_vecs = jnp.where(first, vectors[:, 0], vectors[:, 1])


    content_cot, query_cot, unused = tie((content_cot, query_cot, content_full))
    cots = cross(jnp.stack([content_cot, query_cot], axis=1))

    position_bf, rel, rel_turned = relative(wr, length)
    queries = mm(inputs, wq)
    kv = mm(content_full, kv_weight).astype(BF)
    vec8 = jnp.pad(head_vecs, ((0, 3), (0, 0)))
    table = head_vecs[3:5].reshape(2, heads, DH).transpose(1, 2, 0)[..., None]
    table = jnp.where(jnp.arange(128) < 2 * NS, table, 0.0).astype(BF)
    table = jnp.tile(table.reshape(heads, DH, 256), (1, 2, 1))
    late = hold(late[0], late[1], [rel])
    late_near = [late] + [near(late, step) for step in range(1, m)]
    forward = []
    got_mixed = []
    for pair in range(pairs):
        after = [[late], [cots], late_near[1:]][min(pair, 2)]
        if pair == 2:
            *held, unused = tie((*late_near, forward[1][1]))
            late_theirs = [swap(x) for x in held]
        after = after + [f[1] for f in forward[-1:]]
        forward.append(
            attend_forward(
                pair,
                after,
                base,
                live,
                queries,
                vec8,
                table,
                info,
                reach,
                kv,
                hot,
                rel,
                key_ranks,
            )
        )
        got_mixed.append(swap(pick(forward[-1][3].reshape(2, groups * r, 128), 1 - k)))

    (
        result,
        grad_residual,
        mine_grad,
        other_grad,
        row_vecs,
        inner_vecs,
        early_mine,
        early_other,
        late_mine,
        late_other,
    ) = (dense if ws % 16 == 0 else dense_plain)(
        at,
        [f[3] for f in forward],
        got_mixed,
        inputs,
        cots.reshape(groups * r, d),
        late_near,
        late_theirs,
        ws,
        ff,
    )
    grad_heads = pair_of(mine_grad, swap(other_grad), k).reshape(groups * 2 * r, dh)

    backward = []

    def back(pair, after):
        f = forward[pair]
        after = after + [b[0] for b in backward[-1:]]
        backward.append(
            attend_backward(
                pair,
                after,
                base,
                live,
                f[0],
                queries,
                grad_heads,
                f[1],
                f[2],
                vec8,
                info,
                kv,
                hot,
                rel_turned,
            )
        )

    def near_fold(arrays, rows, after):
        parts = fold(at, [x.reshape(2, m, rows, x.shape[-1]) for x in arrays], after)
        return [parts[0]] + [near(parts[step], step) for step in range(1, m)]

    def cross_join(parts, after):
        return [across(x, e) for e, x in enumerate(join(at, parts, after))]

    def proj_some(some, extra, after):
        return proj_grads(
            inputs, content_full, position_bf, [backward[p] for p in some], extra, after
        ).reshape(groups, m, ws, -1)

    result = result.reshape(2, 2, r, d)
    outs_got = [across(pick(result, low ^ e), e) for e in range(2)]
    back(0, [])
    after = [backward[0][0]]
    late_parts = near_fold([late_mine, swap(late_other)], fs, after + outs_got)
    early_parts = near_fold([early_mine, swap(early_other)], ws, after)
    back(1, [early_parts[0], late_parts[0]])
    some_grads = proj_some(range(pairs - 1), [], [])
    some_parts = near_parts(some_grads, 1)
    late_cross = cross_join(late_parts, [some_grads])
    early_cross = cross_join(early_parts, [some_grads])
    back(2, [some_grads])

    small = jnp.concatenate([b[3][:5] for b in backward], axis=1)
    small = jnp.where(
        first,
        jnp.concatenate([small, jnp.zeros_like(small)], axis=1),
        jnp.concatenate([jnp.zeros_like(small), small], axis=1),
    )
    inner_vecs = inner_vecs[0].reshape(n, fs // ws, ws).swapaxes(1, 2).reshape(d, fs // ws)
    small = jnp.concatenate([small.T, row_vecs[:5].T, inner_vecs], axis=1)
    small = jnp.pad(small, ((0, 0), (0, 128 - small.shape[1]))).astype(BF)
    last_grads = proj_some([pairs - 1], [small], some_parts[1:] + late_cross + early_cross)
    early_sum = add_up(early_cross, BF, [last_grads])
    late_sum = add_up(late_cross, BF, [last_grads])
    early_got, late_got = swap(early_sum), swap(late_sum)
    *outs_got, unused = tie((*outs_got, last_grads))
    outs = pair_of(outs_got[0], outs_got[1], low)
    last_parts = near_parts(last_grads, 1)
    which = [jnp.asarray(x, jnp.int32).reshape(1) for x in (k, 1 - k)]
    dkv_parts = [b[1] for b in backward]
    dq_parts = [b[0] for b in backward]
    got_kv = swap(input_grad(which[1], dkv_parts, kv_weight, BF, [last_grads], True))
    got_q = swap(input_grad(which[1], dq_parts, wq, BF, [last_grads]))
    own_kv = input_grad(which[0], dkv_parts, kv_weight, F32, [last_grads], True)
    own_q = input_grad(which[0], dq_parts, wq, F32, [last_grads])
    content_parts = near_fold([own_kv, got_kv], r, [own_q, early_got, late_got] + last_parts[1:])
    q_sum = own_q + got_q.astype(F32) + grad_residual
    q_sum = q_sum.reshape(2, 2, r, d)
    query_rows, unused = tie((q_sum[:, 1].astype(BF), content_parts[1]))
    query_grads = cross(query_rows)
    late_total = late_sum.astype(F32) + late_got.astype(F32)
    content_sum = sum([x.astype(F32) for x in content_parts]) + q_sum[:, 0]
    content_grads = cross(content_sum.astype(BF))
    some_near, last_near = [
        add_up(parts, BF, content_parts[:1]) for parts in (some_parts, last_parts)
    ]
    proj_sum = far_sum(jnp.concatenate([some_near, last_near], axis=2))

    early_total = early_sum.astype(F32) + early_got.astype(F32)
    bit = 2
    while bit < nr:
        turn = [(i, i ^ bit) for i in range(nr)]
        early_total = early_total + lax.ppermute(early_total, "rep", turn)
        late_total = late_total + lax.ppermute(late_total, "rep", turn)
        proj_sum = proj_sum + lax.ppermute(proj_sum, "rep", turn)
        bit *= 2
    proj_other = swap(proj_sum)
    halves = jnp.where(first, proj_sum, proj_other), jnp.where(first, proj_other, proj_sum)

    def columns(index):
        return jnp.concatenate(
            [
                x[:, 512 * p + 128 * index : 512 * p + 128 * index + 128]
                for x in halves
                for p in range(pairs)
            ],
            axis=1,
        )

    head_cols = (proj_sum + proj_other)[:, 512 * pairs :]
    vec_cols = head_cols[:, 5:]
    return (
        outs[:, 0],
        outs[:, 1],
        content_grads,
        query_grads,
        columns(0),
        columns(1),
        columns(2),
        columns(3),
        early_total[:, ff : ff + d],
        early_total[:, :ff],
        late_total,
        vec_cols[:, 5 : 5 + fs // ws].T.reshape(fs),
        vec_cols[:, 0],
        vec_cols[:, 1],
        vec_cols[:, 2],
        vec_cols[:, 3],
        vec_cols[:, 4],
        head_cols[:, 0],
        head_cols[:, 1],
        head_cols[:, 2],
        head_cols[:, 3:5].T,
    )


def solution(mesh):
    in_specs = (
        P("rep", "shard", None),
        P("rep", "shard", None),
        P("rep", "shard"),
        P("rep", None),
        P("rep", "shard"),
        P("rep", "shard"),
        P("shard", None),
        P("shard", None),
        P("shard", None),
        P("shard", None),
        P("shard", None),
        P("shard", None),
        P("shard", None),
        P("shard"),
        P("shard"),
        P("shard"),
        P("shard"),
        P("shard"),
        P("shard"),
        P("shard"),
        P("shard"),
        P("shard"),
        P(None, "shard"),
        P("rep", "shard", None),
        P("rep", "shard", None),
    )
    out_specs = (
        P("rep", "shard", None),
        P("rep", "shard", None),
        P("rep", "shard", None),
        P("rep", "shard", None),
        P("shard", None),
        P("shard", None),
        P("shard", None),
        P("shard", None),
        P("shard", None),
        P("shard", None),
        P("shard", None),
        P("shard"),
        P("shard"),
        P("shard"),
        P("shard"),
        P("shard"),
        P("shard"),
        P("shard"),
        P("shard"),
        P("shard"),
        P(None, "shard"),
    )
    return jax.shard_map(body, mesh=mesh, in_specs=in_specs, out_specs=out_specs, check_vma=False)
```

```python
import functools
import math

import jax
import jax.numpy as jnp
from jax import lax
from jax.experimental import pallas as pl
from jax.experimental.pallas import tpu as pltpu
from jax.sharding import PartitionSpec as P

DH = 64
NS = 13
EPSILON = 1e-05
NEG = -1e30
F32 = jnp.float32
BF = jnp.bfloat16
HIGHEST = lax.Precision.HIGHEST

R = 128
KB = 256
W = R + KB
SCALE = DH**-0.5
LOG2E = 1.4426950408889634
LN2 = 0.6931471805599453
VMEM = 60 * 2**20
SMALL = 32 * 2**20
ONES = 32


def mm(a, b, ca=1, cb=0, precision=None):
    return lax.dot_general(
        a, b, (((ca,), (cb,)), ((), ())), preferred_element_type=F32, precision=precision
    )


def row_features(seg_col):
    lane = lax.broadcasted_iota(jnp.int32, (2 * R, 128), 1)
    folded = jnp.where(lane < NS, lane, lane - NS).astype(F32)
    return jnp.where((lane < 2 * NS) & (folded == seg_col), 1.0, 0.0)


def live_list(live_ref, list_ref, row, nkb):
    per = KB // R

    def step(kb, count):
        list_ref[count] = kb
        live = live_ref[row, kb * per]
        for i in range(1, per):
            live = jnp.maximum(live, live_ref[row, kb * per + i])
        return count + live

    return lax.fori_loop(0, nkb, step, 0)


def ordered(kernel, count, extra):
    def run(*refs):
        kernel(*refs[:count], *refs[count + extra :])

    return run


def reversal():
    down = lax.broadcasted_iota(jnp.int32, (KB, KB), 0)
    across = lax.broadcasted_iota(jnp.int32, (KB, KB), 1)
    return jnp.where(down + across == KB - 1, 1.0, 0.0).astype(BF)


def by_four(count, work):
    def step(i, carry):
        work([4 * i, 4 * i + 1, 4 * i + 2, 4 * i + 3])
        return carry

    lax.fori_loop(0, count // 4, step, 0)
    rest = count // 4 * 4

    @pl.when(count % 4 >= 2)
    def pair():
        work([rest, rest + 1])

    @pl.when(count % 2 == 1)
    def last():
        work([count - 1])


def by_two(count, work):
    def step(i, carry):
        work([2 * i, 2 * i + 1])
        return carry

    lax.fori_loop(0, count // 2, step, 0)

    @pl.when(count % 2 == 1)
    def last():
        work([count - 1])


def forward_kernel(
    nkb,
    base_ref,
    live_ref,
    q_ref,
    vec_ref,
    table_ref,
    info_ref,
    reach_ref,
    kv_ref,
    hot_ref,
    rel_ref,
    rank_ref,
    p_ref,
    o_ref,
    inv_ref,
    ob_ref,
    qq_scr,
    qr_scr,
    s_scr,
    m_scr,
    acc_scr,
    flip_scr,
    list_scr,
):
    block = pl.program_id(0)

    @pl.when(block == 0)
    def start():
        flip_scr[...] = reversal()

    row = base_ref[0] + base_ref[1] * block
    base = nkb * KB - R - R * row
    count = live_list(live_ref, list_scr, row, nkb)
    seg_col = info_ref[:, 0:1]
    limit = info_ref[:, 1:2]
    hot_row = row_features(seg_col)
    lane = lax.broadcasted_iota(jnp.int32, (2 * R, 128), 1)
    reach = mm(jnp.where(lane < NS, hot_row, 0.0).astype(BF), reach_ref[...])
    outside = jnp.where((lane < 2 * NS) & (reach < 0.5), NEG, 0.0)
    zero = jnp.zeros((2 * R, DH), BF)
    for h in range(2):
        half = slice(DH * h, DH * h + DH)
        q = q_ref[:, half]
        plain = ((q + vec_ref[0:1, half]) * (SCALE * LOG2E)).astype(BF)
        place = ((q + vec_ref[1:2, half]) * (SCALE * LOG2E)).astype(BF)
        label = q + vec_ref[2:3, half]
        top_part = label.astype(BF)
        rest = (label - top_part.astype(F32)).astype(BF)
        both = mm(jnp.concatenate([top_part, rest], axis=1), table_ref[h])
        same, other = both[:, :128], both[:, 128:]
        term = jnp.where(hot_row > 0.5, same, other) * (SCALE * LOG2E) + outside
        high = term.astype(BF).astype(F32)
        extra = jnp.where(lane < NS, high, jnp.where(lane < 2 * NS, term - high, 0.0))
        side = lambda x: [x, zero] if h == 0 else [zero, x]
        qq_scr[h] = jnp.concatenate(side(plain) + [extra.astype(BF)], axis=1)
        qr_scr[h] = jnp.concatenate(side(place), axis=1)
    m_scr[...] = jnp.full(m_scr.shape, -jnp.inf, F32)
    acc_scr[...] = jnp.zeros(acc_scr.shape, F32)

    def score(blocks):
        highest = [m_scr[h] for h in range(2)]
        for n in blocks:
            k0 = pl.multiple_of(list_scr[n] * KB, KB)
            ok = rank_ref[:, pl.ds(k0, KB)] <= limit
            window = rel_ref[pl.ds(pl.multiple_of(base + k0, 128), W), :]
            keys = jnp.concatenate(
                [kv_ref[pl.ds(k0, KB), :128], hot_ref[pl.ds(k0, KB), :]], axis=1
            )
            for h in range(2):
                s = mm(qq_scr[h], keys, 1, 1)
                full = mm(qr_scr[h], window, 1, 1)
                shifted = [
                    pltpu.roll(
                        full[i * R : i * R + R], W - (R - 1), 1, stride=1, stride_axis=0
                    )[:, :KB]
                    for i in range(2)
                ]
                s = jnp.where(ok, s + jnp.concatenate(shifted, axis=0), NEG)
                s_scr[h, n] = s
                highest[h] = jnp.maximum(highest[h], jnp.maximum(s[:, :128], s[:, 128:]))
        for h in range(2):
            m_scr[h] = highest[h]

    by_four(count, score)
    top = [jnp.max(m_scr[h], axis=1, keepdims=True) for h in range(2)]

    def mix(blocks):
        totals = [0.0, 0.0]
        for n in blocks:
            k0 = pl.multiple_of(list_scr[n] * KB, KB)
            values = jnp.concatenate(
                [kv_ref[pl.ds(k0, KB), 128:], hot_ref[pl.ds(k0, KB), :]], axis=1
            )
            for h in range(2):
                p = jnp.exp2(s_scr[h, n] - top[h]).astype(BF)
                p_ref[0, h, n] = mm(p, flip_scr[...]).astype(BF)
                totals[h] += mm(p, values)
        for h in range(2):
            acc_scr[h] += totals[h]

    by_four(count, mix)
    for h in range(2):
        half = slice(DH * h, DH * h + DH)
        acc = acc_scr[h]
        inverse = 1.0 / acc[:, 128 + ONES : 129 + ONES]
        mixed = acc[:, half] * inverse
        o_ref[:, half] = mixed
        ob_ref[:, half] = mixed.astype(BF)
        inv_ref[:, half] = jnp.broadcast_to(inverse, (2 * R, DH))


def attend_forward(pair, after, base, live, q, vec, table, info, reach, kv, hot, rel, rank):
    nb = q.shape[0] // (2 * R)
    length = kv.shape[0]
    nkb = length // KB
    whole = lambda *shape: pl.BlockSpec(shape, lambda b, *_: (0,) * len(shape))
    return pl.pallas_call(
        ordered(functools.partial(forward_kernel, nkb), 11, len(after)),
        grid_spec=pltpu.PrefetchScalarGridSpec(
            num_scalar_prefetch=2,
            grid=(nb,),
            in_specs=[
                pl.BlockSpec((2 * R, 128), lambda b, *_: (b, pair)),
                pl.BlockSpec((8, 128), lambda b, *_: (0, pair)),
                pl.BlockSpec((2, 2 * DH, 256), lambda b, *_: (pair, 0, 0)),
                pl.BlockSpec((2 * R, 128), lambda b, *_: (b, 0)),
                whole(128, 128),
                pl.BlockSpec((length, 256), lambda b, *_: (0, pair)),
                whole(length, 128),
                pl.BlockSpec((2 * length, 128), lambda b, *_: (0, pair)),
                whole(1, length),
            ]
            + [pl.BlockSpec(memory_space=pl.ANY)] * len(after),
            out_specs=[
                pl.BlockSpec((1, 2, nkb, 2 * R, KB), lambda b, *_: (b, 0, 0, 0, 0)),
                pl.BlockSpec((2 * R, 128), lambda b, *_: (b, 0)),
                pl.BlockSpec((2 * R, 128), lambda b, *_: (b, 0)),
                pl.BlockSpec((2 * R, 128), lambda b, *_: (b, 0)),
            ],
            scratch_shapes=[
                pltpu.VMEM((2, 2 * R, 256), BF),
                pltpu.VMEM((2, 2 * R, 128), BF),
                pltpu.VMEM((2, nkb, 2 * R, KB), F32),
                pltpu.VMEM((2, 2 * R, 128), F32),
                pltpu.VMEM((2, 2 * R, 256), F32),
                pltpu.VMEM((KB, KB), BF),
                pltpu.SMEM((nkb + 1,), jnp.int32),
            ],
        ),
        out_shape=[
            jax.ShapeDtypeStruct((nb, 2, nkb, 2 * R, KB), BF),
            jax.ShapeDtypeStruct((q.shape[0], 128), F32),
            jax.ShapeDtypeStruct((q.shape[0], 128), F32),
            jax.ShapeDtypeStruct((q.shape[0], 128), BF),
        ],
        compiler_params=pltpu.CompilerParams(
            dimension_semantics=("arbitrary",), vmem_limit_bytes=VMEM
        ),
        cost_estimate=pl.CostEstimate(
            flops=10**8, bytes_accessed=10**6, transcendentals=0
        ),
        name="attend_forward",
    )(base, live, q, vec, table, info, reach, kv, hot, rel, rank, *after)


def backward_kernel(
    nkb,
    nb,
    base_ref,
    live_ref,
    p_ref,
    q_ref,
    g_ref,
    o_ref,
    inv_ref,
    vec_ref,
    info_ref,
    kv_ref,
    hot_ref,
    rel_ref,
    dq_ref,
    dkv_ref,
    drel_ref,
    small_ref,
    turn_scr,
    dd_scr,
    acc_scr,
    accr_scr,
    dkv_scr,
    drel_scr,
    keys_scr,
    flip_scr,
    list_scr,
):
    block = pl.program_id(0)
    length = nkb * KB
    row = base_ref[0] + base_ref[1] * block
    base = nkb * KB - R - R * row
    count = live_list(live_ref, list_scr, row, nkb)

    @pl.when(block == 0)
    def start():
        dkv_scr[...] = jnp.zeros(dkv_scr.shape, F32)
        drel_scr[...] = jnp.zeros(drel_scr.shape, F32)
        small_ref[...] = jnp.zeros(small_ref.shape, F32)
        flip = reversal()
        flip_scr[...] = flip
        for kb in range(nkb):
            rows = slice(kb * KB, (kb + 1) * KB)
            keys_scr[rows, :256] = mm(flip, kv_ref[rows, :]).astype(BF)
            keys_scr[rows, 256:] = mm(flip, hot_ref[rows, :]).astype(BF)

    lane = lax.broadcasted_iota(jnp.int32, (2 * R, 128), 1)
    zero = jnp.zeros((2 * R, DH), BF)
    for h in range(2):
        half = slice(DH * h, DH * h + DH)
        q = q_ref[:, half]
        plain = (q + vec_ref[0:1, half]) * (SCALE * LOG2E)
        place = (q + vec_ref[1:2, half]) * (SCALE * LOG2E)
        g = g_ref[:, half].astype(F32)
        inverse = inv_ref[:, DH * h : DH * h + 1]
        delta = -jnp.sum(g * o_ref[:, half], axis=1, keepdims=True) * inverse
        high = delta.astype(BF).astype(F32)
        extra = jnp.where(lane == ONES, high, jnp.where(lane == ONES + 1, delta - high, 0.0))
        side = lambda x: [x, zero] if h == 0 else [zero, x]
        scaled = g * inverse
        dd_scr[h] = jnp.concatenate(side(scaled.astype(BF)) + [extra.astype(BF)], axis=1)
        for i, x in enumerate((plain, scaled, place)):
            turn_scr[h, i] = x.T.astype(BF)
    acc_scr[...] = jnp.zeros(acc_scr.shape, F32)
    accr_scr[...] = jnp.zeros(accr_scr.shape, F32)

    def step(blocks):
        pad = jnp.zeros((R, W - KB), F32)
        d_query = [0.0, 0.0]
        d_place = [0.0, 0.0]
        for n in blocks:
            k0 = pl.multiple_of(list_scr[n] * KB, KB)
            r0 = pl.multiple_of(2 * length - base - k0 - W, 128)
            window = rel_ref[pl.ds(r0, W), :]
            keys = jnp.concatenate(
                [keys_scr[pl.ds(k0, KB), :128], keys_scr[pl.ds(k0, KB), 256:]], axis=1
            )
            values = keys_scr[pl.ds(k0, KB), 128:]
            for h in range(2):
                p = p_ref[0, h, n]
                wide = p.astype(F32) * mm(dd_scr[h], values, 1, 1)
                ds = wide.astype(BF)
                d_query[h] += mm(ds, keys)
                full = [
                    pltpu.roll(
                        jnp.concatenate([wide[i * R : i * R + R], pad], axis=1),
                        0,
                        1,
                        stride=1,
                        stride_axis=0,
                    )
                    for i in range(2)
                ]
                full = jnp.concatenate(full, axis=0).astype(BF)
                d_place[h] += mm(full, window)
                low, high = DH * h, DH * h + DH
                dkv_scr[low:high, pl.ds(k0, KB)] += mm(turn_scr[h, 0], ds)
                dkv_scr[128 + low : 128 + high, pl.ds(k0, KB)] += mm(turn_scr[h, 1], p)
                drel_scr[low:high, pl.ds(r0, W)] += mm(turn_scr[h, 2], full)
        for h in range(2):
            acc_scr[h] += d_query[h]
            accr_scr[h] += d_place[h]

    by_two(count, step)
    hot_row = row_features(info_ref[:, 0:1])
    for h in range(2):
        half = slice(DH * h, DH * h + DH)
        acc = acc_scr[h]
        d_plain = acc[:, half] * SCALE
        d_place = accr_scr[h][:, half] * SCALE
        sums = jnp.where(lane < NS, acc[:, 128:], 0.0) * SCALE
        same = jnp.sum(sums * hot_row, axis=1, keepdims=True)
        other = jnp.sum(sums, axis=1, keepdims=True) - same
        d_label = same * vec_ref[3:4, half] + other * vec_ref[4:5, half]
        label = q_ref[:, half] + vec_ref[2:3, half]
        dq_ref[:, half] = (d_plain + d_place + d_label).astype(BF)
        terms = [d_plain, d_place, d_label, same * label, other * label]
        for row, term in enumerate(terms):
            small_ref[row : row + 1, half] += jnp.sum(term, axis=0, keepdims=True)

    @pl.when(block == nb - 1)
    def finish():
        down = lax.broadcasted_iota(jnp.int32, (256, KB), 0)
        factor = jnp.where(down < 128, LN2, 1.0)
        for kb in range(nkb):
            cols = slice(kb * KB, (kb + 1) * KB)
            dkv_ref[:, cols] = mm((dkv_scr[:, cols] * factor).astype(BF), flip_scr[...]).astype(BF)
        drel_ref[...] = (drel_scr[...] * LN2).astype(BF)


def attend_backward(pair, after, base, live, p, q, g, o, inv, vec, info, kv, hot, rel):
    nb = q.shape[0] // (2 * R)
    length = kv.shape[0]
    nkb = length // KB
    own = pl.BlockSpec((2 * R, 128), lambda b, *_: (b, 0))
    rows = pl.BlockSpec((2 * R, 128), lambda b, *_: (b, pair))
    return pl.pallas_call(
        ordered(functools.partial(backward_kernel, nkb, nb), 12, len(after)),
        grid_spec=pltpu.PrefetchScalarGridSpec(
            num_scalar_prefetch=2,
            grid=(nb,),
            in_specs=[
                pl.BlockSpec((1, 2, nkb, 2 * R, KB), lambda b, *_: (b, 0, 0, 0, 0)),
                rows,
                rows,
                own,
                own,
                pl.BlockSpec((8, 128), lambda b, *_: (0, pair)),
                pl.BlockSpec((2 * R, 128), lambda b, *_: (b, 0)),
                pl.BlockSpec((length, 256), lambda b, *_: (0, pair)),
                pl.BlockSpec((length, 128), lambda b, *_: (0, 0)),
                pl.BlockSpec((2 * length, 128), lambda b, *_: (0, pair)),
            ]
            + [pl.BlockSpec(memory_space=pl.ANY)] * len(after),
            out_specs=[
                own,
                pl.BlockSpec((256, length), lambda b, *_: (0, 0)),
                pl.BlockSpec((128, 2 * length), lambda b, *_: (0, 0)),
                pl.BlockSpec((8, 128), lambda b, *_: (0, 0)),
            ],
            scratch_shapes=[
                pltpu.VMEM((2, 3, DH, 2 * R), BF),
                pltpu.VMEM((2, 2 * R, 256), BF),
                pltpu.VMEM((2, 2 * R, 256), F32),
                pltpu.VMEM((2, 2 * R, 128), F32),
                pltpu.VMEM((256, length), F32),
                pltpu.VMEM((128, 2 * length), F32),
                pltpu.VMEM((length, 384), BF),
                pltpu.VMEM((KB, KB), BF),
                pltpu.SMEM((nkb + 1,), jnp.int32),
            ],
        ),
        out_shape=[
            jax.ShapeDtypeStruct((q.shape[0], 128), BF),
            jax.ShapeDtypeStruct((256, length), BF),
            jax.ShapeDtypeStruct((128, 2 * length), BF),
            jax.ShapeDtypeStruct((8, 128), F32),
        ],
        compiler_params=pltpu.CompilerParams(
            dimension_semantics=("arbitrary",), vmem_limit_bytes=VMEM
        ),
        cost_estimate=pl.CostEstimate(
            flops=10**8, bytes_accessed=10**6, transcendentals=0
        ),
        name="attend_backward",
    )(base, live, p, q, g, o, inv, vec, info, kv, hot, rel, *after)


def whole_block(x):
    return pl.BlockSpec(x.shape, lambda i: (0,) * len(x.shape))


def pack_kernel(r, ws, low_ref, content_ref, seg_ref, rank_ref, flag_ref, parent_ref, *refs):
    vec_refs, weight_refs, (a_ref, b_ref, scr) = refs[:4], refs[4:8], refs[8:]
    low = low_ref[0]
    for e, out in enumerate((a_ref, b_ref)):
        tree = jnp.bitwise_xor(low, e)
        out[:r, :] = content_ref[tree]
        scr[...] = jnp.zeros(scr.shape, F32)
        row = lambda ref: ref[pl.ds(tree, 1), :]
        rank = row(rank_ref)
        scr[0:1, :r] = row(seg_ref).astype(F32)
        scr[0:1, r : 2 * r] = lax.shift_right_logical(rank, 6).astype(F32)
        scr[0:1, 2 * r : 3 * r] = jnp.bitwise_and(rank, 63).astype(F32)
        scr[0:1, 3 * r : 4 * r] = row(flag_ref).astype(F32)
        scr[0:1, 4 * r : 4 * r + NS] = row(parent_ref).astype(F32)
        for i in range(3):
            scr[i + 1 : i + 2, :ws] = vec_refs[i][...].astype(F32)
        scr[4:6, :ws] = vec_refs[3][...].astype(F32)
        out[r : r + 16, :] = scr[...].astype(BF)
        for i in range(4):
            out[r + 16 + i * ws : r + 16 + (i + 1) * ws, :] = weight_refs[i][...]


def pack(low, content, segs, ranks, flags, parents, vecs, weights):
    trees, r, d = content.shape
    ws = weights[0].shape[0]
    shape = jax.ShapeDtypeStruct((r + 16 + 4 * ws, d), BF)
    return pl.pallas_call(
        functools.partial(pack_kernel, r, ws),
        grid=(1,),
        in_specs=[pl.BlockSpec(memory_space=pltpu.SMEM), whole_block(content)]
        + [whole_block(x) for x in (segs, ranks, flags, parents, *vecs, *weights)],
        out_specs=[whole_block(shape)] * 2,
        out_shape=[shape, shape],
        scratch_shapes=[pltpu.VMEM((16, d), F32)],
        compiler_params=pltpu.CompilerParams(vmem_limit_bytes=VMEM),
        name="pack",
    )(low, content, segs, ranks, flags, parents, *vecs, *weights)


def assemble_kernel(r, ws, dh, m, at_ref, a0, a1, t0, t1, q_own, q_other, *outs):
    content_ref, codes_ref, wq_ref, wkv_ref, wr_ref, inputs_ref = outs
    k, low, c = at_ref[0], at_ref[1], at_ref[2]
    h, zl = pl.program_id(0), pl.program_id(1)
    column = lambda start: pl.multiple_of(k * dh + start, 128)

    def fill(src, query):
        inputs_ref[0, 0, 0] = src[0, :r, :]
        inputs_ref[0, 0, 1] = query[...]
        for step in range(m):
            to = jnp.bitwise_xor(c, step)
            rows = lambda i: slice(r + 16 + i * ws, r + 16 + (i + 1) * ws)
            content_ref[0, 0, to] = src[step, :r, :]
            codes_ref[0, 0, to] = src[step, r : r + 16, :]
            wq_ref[0, 0, to] = src[step, rows(0), pl.ds(column(0), dh)]
            wr_ref[0, 0, to] = src[step, rows(3), pl.ds(column(0), dh)]
            for p in range(dh // 128):
                for i in range(2):
                    wkv_ref[0, 0, to, :, 256 * p + 128 * i : 256 * p + 128 * i + 128] = src[
                        step, rows(1 + i), pl.ds(column(128 * p), 128)
                    ]

    for mine in (True, False):
        for e in range(2):
            src = ((a0, a1) if mine else (t0, t1))[e]
            query = (q_own if mine else q_other).at[e]

            @pl.when(((h == k) == mine) & (jnp.bitwise_xor(zl, low) == e))
            def case(src=src, query=query):
                fill(src, query)


def assemble(at, near_rows, their_rows, q_own, q_other, r, ws, after):
    m, rows, d = near_rows[0].shape
    dh = d // 2
    sizes = [(m, r, d), (m, 16, d), (m, ws, dh), (m, ws, d), (m, ws, dh), (2, r, d)]
    return pl.pallas_call(
        ordered(functools.partial(assemble_kernel, r, ws, dh, m), 7, len(after)),
        grid=(2, 2),
        in_specs=[pl.BlockSpec(memory_space=pltpu.SMEM)]
        + [pl.BlockSpec((m, rows, d), lambda h, z: (0, 0, 0))] * 4
        + [pl.BlockSpec((2, r, d), lambda h, z: (0, 0, 0))] * 2
        + [pl.BlockSpec(memory_space=pl.ANY)] * len(after),
        out_specs=[pl.BlockSpec((1, 1) + size, lambda h, z: (h, z, 0, 0, 0)) for size in sizes],
        out_shape=[jax.ShapeDtypeStruct((2, 2) + size, BF) for size in sizes],
        compiler_params=pltpu.CompilerParams(vmem_limit_bytes=SMALL),
        name="assemble",
    )(at, *near_rows, *their_rows, q_own, q_other, *after)


def pack_late_kernel(ws, w1_ref, wo_ref, w2_ref, *refs):
    vec_refs, out, scr = refs[:-2], refs[-2], refs[-1]
    d = wo_ref.shape[1]
    parts = w1_ref.shape[1] // d
    for j in range(parts):
        out[j * ws : (j + 1) * ws, :] = w1_ref[:, j * d : (j + 1) * d]
    out[parts * ws : (parts + 1) * ws, :] = wo_ref[...]
    out[(parts + 1) * ws : (2 * parts + 1) * ws, :] = w2_ref[...]
    scr[...] = jnp.zeros(scr.shape, F32)
    row = 0
    for ref in vec_refs:
        scr[row : row + ref.shape[0], : ref.shape[1]] = ref[...].astype(F32)
        row += ref.shape[0]
    out[(2 * parts + 1) * ws :, :] = scr[...].astype(BF)


def pack_late(w1, wo, w2, vecs):
    ws, d = wo.shape
    rows = ws + w1.shape[1] // d * ws + w2.shape[0] + 16
    return pl.pallas_call(
        functools.partial(pack_late_kernel, ws),
        grid=(1,),
        in_specs=[whole_block(x) for x in (w1, wo, w2, *vecs)],
        out_specs=pl.BlockSpec((rows, d), lambda i: (0, 0)),
        out_shape=jax.ShapeDtypeStruct((rows, d), BF),
        scratch_shapes=[pltpu.VMEM((16, d), F32)],
        compiler_params=pltpu.CompilerParams(vmem_limit_bytes=SMALL),
        name="pack_late",
    )(w1, wo, w2, *vecs)


def assemble_late_kernel(ws, m, at_ref, *refs):
    mine_refs, their_refs, (w1_ref, wo_ref, w2_ref, vec_ref) = refs[:m], refs[m : 2 * m], refs[2 * m :]
    k, low, c = at_ref[0], at_ref[1], at_ref[2]
    h, zl = pl.program_id(0), pl.program_id(1)
    d = wo_ref.shape[-1]
    parts = w1_ref.shape[-1] // d
    e = jnp.bitwise_xor(zl, low)

    def fill(refs):
        for step, src in enumerate(refs):
            to = jnp.bitwise_xor(c, step)
            for j in range(parts):
                w1_ref[0, 0, to, :, j * d : (j + 1) * d] = src[e, j * ws : (j + 1) * ws, :]
            wo_ref[0, 0, to] = src[e, parts * ws : (parts + 1) * ws, :]
            w2_ref[0, 0, to] = src[e, (parts + 1) * ws : (2 * parts + 1) * ws, :]
            vec_ref[0, 0, to] = src[e, (2 * parts + 1) * ws :, :]

    @pl.when(h == k)
    def own():
        fill(mine_refs)

    @pl.when(h != k)
    def other():
        fill(their_refs)


def assemble_late(at, mine, theirs, ws, parts):
    m = len(mine)
    two, rows, d = mine[0].shape
    sizes = [(m, ws, parts * d), (m, ws, d), (m, parts * ws, d), (m, 16, d)]
    return pl.pallas_call(
        functools.partial(assemble_late_kernel, ws, m),
        grid=(2, 2),
        in_specs=[pl.BlockSpec(memory_space=pltpu.SMEM)]
        + [pl.BlockSpec((2, rows, d), lambda h, z: (0, 0, 0))] * (2 * m),
        out_specs=[pl.BlockSpec((1, 1) + size, lambda h, z: (h, z, 0, 0, 0)) for size in sizes],
        out_shape=[jax.ShapeDtypeStruct((2, 2) + size, BF) for size in sizes],
        compiler_params=pltpu.CompilerParams(vmem_limit_bytes=SMALL),
        name="assemble_late",
    )(at, *mine, *theirs)


def relative_kernel(sa_ref, ca_ref, sb_ref, cb_ref, w_ref, pos_ref, rel_ref, turned_ref):
    half = sb_ref.shape[1]
    fine = sb_ref.shape[0]
    for i in range(pos_ref.shape[0] // fine):
        rows = slice(i * fine, (i + 1) * fine)
        sa, ca = sa_ref[0, i : i + 1, :], ca_ref[0, i : i + 1, :]
        sine = sa * cb_ref[...] - ca * sb_ref[...]
        cosine = ca * cb_ref[...] + sa * sb_ref[...]
        pos_ref[rows, :half] = sine.astype(BF)
        pos_ref[rows, half:] = cosine.astype(BF)
    from_sine = mm(pos_ref[:, :half], w_ref[:half, :])
    from_cosine = mm(pos_ref[:, half:], w_ref[half:, :])
    rel_ref[...] = (from_cosine + from_sine).astype(BF)
    turned_ref[...] = (from_cosine - from_sine).astype(BF)


def relative(wr, length):
    d, width = wr.shape
    half, fine = d // 2, 64
    powers = jnp.arange(half, dtype=F32) * (2.0 / d)
    inverse_freq = 1.0 / 10000.0**powers
    coarse = (length - 1 - fine * jnp.arange(2 * length // fine, dtype=jnp.int32)).astype(F32)
    a = coarse[:, None] * inverse_freq[None]
    b = jnp.arange(fine, dtype=F32)[:, None] * inverse_freq[None]
    size = 1024
    per = size // fine
    tables = [jnp.sin(a).reshape(-1, per, half), jnp.cos(a).reshape(-1, per, half), jnp.sin(b), jnp.cos(b)]
    rows = lambda w: pl.BlockSpec((size, w), lambda i: (i, 0))
    return pl.pallas_call(
        relative_kernel,
        grid=(2 * length // size,),
        in_specs=[pl.BlockSpec((1, per, half), lambda i: (i, 0, 0))] * 2
        + [pl.BlockSpec((fine, half), lambda i: (0, 0))] * 2
        + [pl.BlockSpec((d, width), lambda i: (0, 0))],
        out_specs=[rows(d), rows(width), rows(width)],
        out_shape=[
            jax.ShapeDtypeStruct((2 * length, d), BF),
            jax.ShapeDtypeStruct((2 * length, width), BF),
            jax.ShapeDtypeStruct((2 * length, width), BF),
        ],
        compiler_params=pltpu.CompilerParams(vmem_limit_bytes=SMALL),
        cost_estimate=pl.CostEstimate(
            flops=4 * length * d * width, bytes_accessed=8 * length * d, transcendentals=0
        ),
        name="relative",
    )(*tables, wr)


def input_grad_kernel(count, turned, at_ref, *refs):
    parts, w_ref, out_ref = refs[:count], refs[count], refs[-1]
    total = 0.0
    start = 0
    for ref in parts:
        width = ref.shape[0 if turned else 1]
        total += mm(ref[...], w_ref[:, start : start + width], 0 if turned else 1, 1)
        start += width
    out_ref[...] = total.astype(out_ref.dtype)


def input_grad(half, parts, w, dtype, after, turned=False):
    rows = parts[0].shape[1 if turned else 0] // 2
    block = math.gcd(rows, 512)
    blocks = rows // block
    d = w.shape[0]
    return pl.pallas_call(
        ordered(
            functools.partial(input_grad_kernel, len(parts), turned), len(parts) + 2, len(after)
        ),
        grid_spec=pltpu.PrefetchScalarGridSpec(
            num_scalar_prefetch=1,
            grid=(rows // block,),
            in_specs=[
                pl.BlockSpec((x.shape[0], block), lambda i, at: (0, at[0] * blocks + i))
                if turned
                else pl.BlockSpec((block, x.shape[1]), lambda i, at: (at[0] * blocks + i, 0))
                for x in parts
            ]
            + [pl.BlockSpec(w.shape, lambda i, at: (0, 0))]
            + [pl.BlockSpec(memory_space=pl.ANY)] * len(after),
            out_specs=pl.BlockSpec((block, d), lambda i, at: (i, 0)),
        ),
        out_shape=jax.ShapeDtypeStruct((rows, d), dtype),
        compiler_params=pltpu.CompilerParams(vmem_limit_bytes=SMALL),
        cost_estimate=pl.CostEstimate(
            flops=2 * rows * d * w.shape[1], bytes_accessed=4 * rows * d, transcendentals=0
        ),
        name="input_grad",
    )(half, *parts, w, *after)


def mask_kernel(n, m, r, c_ref, codes_ref, rank_ref, hot_ref, info_ref, reach_ref, live_ref):
    c = c_ref[0]
    iota = lambda shape, axis: lax.broadcasted_iota(jnp.int32, shape, axis)
    choose = iota((n, 16 * n), 1) == 16 * iota((n, 16 * n), 0)
    rows = mm(choose.astype(F32).astype(BF), codes_ref[...])
    part = lambda i: rows[:, i * r : (i + 1) * r]
    segs = part(0)
    ranks = part(1) * 64.0 + part(2)
    flags = part(3)
    seg_cols, rank_cols, flag_cols = segs.T, ranks.T, flags.T
    parent_col = rows[:, 4 * r : 4 * r + 128].T[:, 0:1]
    lane = iota((128, 128), 1)
    down = iota((128, 128), 0)
    feature = jnp.where(lane < NS, lane, jnp.where(lane < 2 * NS, lane - NS, -1))
    folded = feature.astype(F32)
    ones_lane = (lane == ONES) | (lane == ONES + 1)
    for i in range(n):
        rank_ref[0:1, i * r : (i + 1) * r] = ranks[i : i + 1, :]
        hit = (folded == seg_cols[:, i : i + 1]) | ones_lane
        hot_ref[i * r : (i + 1) * r, :] = jnp.where(hit, 1.0, 0.0).astype(BF)
    mine = iota((r, n), 1)
    for b in range(n // m):
        column = lambda x: jnp.sum(jnp.where(mine == b * m + c, x, 0.0), axis=1, keepdims=True)
        seg, limit = column(seg_cols), column(rank_cols)
        lower = limit - column(flag_cols)
        for i, value in enumerate((limit, lower)):
            start = (2 * b + i) * r
            info_ref[start : start + r, :] = jnp.where(lane == 0, seg, value)
    inside = (down < NS) & (lane < NS)
    link = inside & ((down == lane) | (parent_col == lane.astype(F32)))
    reached = jnp.where(link, 1.0, 0.0)
    for repeat in range(4):
        half = reached.astype(BF)
        reached = jnp.minimum(mm(half, half), 1.0)
    reached = reached.astype(BF)
    twice = jnp.where(down == feature, 1.0, 0.0).astype(BF)
    reach_ref[...] = mm(reached, twice).astype(BF)
    spot = iota((n, 128), 1)
    present = jnp.zeros((n, 128), F32)
    for t in range(NS):
        any_t = jnp.max(jnp.where(segs == t, 1.0, 0.0), axis=1, keepdims=True)
        present = jnp.where(spot == t, any_t, present)
    present = present.astype(BF)
    seen = jnp.minimum(mm(present, reached), 1.0).astype(BF)
    live_ref[...] = jnp.minimum(mm(seen, present, 1, 1), 1.0).astype(jnp.int32)


def masks(c, codes, m, r):
    n, length = codes.shape[0] // 16, codes.shape[0] // 16 * r
    return pl.pallas_call(
        functools.partial(mask_kernel, n, m, r),
        grid=(1,),
        in_specs=[pl.BlockSpec(memory_space=pltpu.SMEM), whole_block(codes)],
        out_specs=[
            pl.BlockSpec(size, lambda i: (0, 0))
            for size in ((1, length), (length, 128), (n // m * 2 * r, 128), (128, 128), (n, n))
        ],
        out_shape=[
            jax.ShapeDtypeStruct((1, length), F32),
            jax.ShapeDtypeStruct((length, 128), BF),
            jax.ShapeDtypeStruct((n // m * 2 * r, 128), F32),
            jax.ShapeDtypeStruct((128, 128), BF),
            jax.ShapeDtypeStruct((n, n), jnp.int32),
        ],
        compiler_params=pltpu.CompilerParams(vmem_limit_bytes=SMALL),
        name="masks",
    )(c, codes)


def hold_kernel(a_ref, b_ref, out_ref):
    out_ref[0] = a_ref[...]
    out_ref[1] = b_ref[...]


def hold(a, b, after):
    spec = pl.BlockSpec(a.shape, lambda i: (0, 0))
    return pl.pallas_call(
        ordered(hold_kernel, 2, len(after)),
        grid=(1,),
        in_specs=[spec, spec] + [pl.BlockSpec(memory_space=pl.ANY)] * len(after),
        out_specs=pl.BlockSpec((2,) + a.shape, lambda i: (0, 0, 0)),
        out_shape=jax.ShapeDtypeStruct((2,) + a.shape, a.dtype),
        compiler_params=pltpu.CompilerParams(vmem_limit_bytes=SMALL),
        name="hold",
    )(a, b, *after)


def proj_grad_kernel(count, steps, x_ref, c_ref, pos_ref, *refs):
    dq, dkv, drel = refs[:count], refs[count : 2 * count], refs[2 * count : 3 * count]
    extra = refs[3 * count : -4]
    out_ref, q_scr, kv_scr, r_scr = refs[-4:]
    i = pl.program_id(0)

    @pl.when(i == 0)
    def start():
        for scr in (q_scr, kv_scr, r_scr):
            scr[...] = jnp.zeros(scr.shape, F32)

    beside = lambda refs, axis: jnp.concatenate([ref[...] for ref in refs], axis=axis)
    r_scr[...] += mm(beside(drel, 0), pos_ref[...])

    @pl.when(i < steps[1])
    def keys():
        kv_scr[...] += mm(beside(dkv, 0), c_ref[...])

    @pl.when(i < steps[0])
    def queries():
        q_scr[...] += mm(beside(dq, 1), x_ref[...], 0, 0)

    @pl.when(i == steps[2] - 1)
    def finish():
        d = pos_ref.shape[1]
        lane = lax.broadcasted_iota(jnp.int32, (128, d), 1)
        for p in range(count):
            at = 512 * p
            rows = slice(128 * p, 128 * p + 128)
            out_ref[:, at : at + 128] = q_scr[rows, :].T.astype(BF)
            out_ref[:, at + 128 : at + 384] = kv_scr[256 * p : 256 * p + 256, :].T.astype(BF)
            turned = jnp.where(lane < d // 2, -r_scr[rows, :], r_scr[rows, :])
            out_ref[:, at + 384 : at + 512] = turned.T.astype(BF)
        for ref in extra:
            out_ref[:, 512 * count :] = ref[...]


def proj_grads(x, content, position, parts, extra, after):
    count = len(parts)
    d = x.shape[1]
    size = 1024
    steps = [a.shape[0] // size for a in (x, content, position)]
    spec = lambda width, kind: pl.BlockSpec(
        (size, width), lambda i: (jnp.minimum(i, steps[kind] - 1), 0)
    )
    turned = lambda width, kind: pl.BlockSpec(
        (width, size), lambda i: (0, jnp.minimum(i, steps[kind] - 1))
    )
    operands = [x, content, position]
    specs = [spec(d, kind) for kind in range(3)]
    for index, one in enumerate((spec(128, 0), turned(256, 1), turned(128, 2))):
        operands += [b[index] for b in parts]
        specs += [one] * count
    operands += extra
    specs += [pl.BlockSpec(e.shape, lambda i: (0, 0)) for e in extra]
    width = 512 * count + sum(e.shape[1] for e in extra)
    total = len(operands)
    return pl.pallas_call(
        ordered(functools.partial(proj_grad_kernel, count, steps), total, len(after)),
        grid=(steps[2],),
        in_specs=specs + [pl.BlockSpec(memory_space=pl.ANY)] * len(after),
        out_specs=pl.BlockSpec((d, width), lambda i: (0, 0)),
        out_shape=jax.ShapeDtypeStruct((d, width), BF),
        scratch_shapes=[
            pltpu.VMEM((count * 128, d), F32),
            pltpu.VMEM((count * 256, d), F32),
            pltpu.VMEM((count * 128, d), F32),
        ],
        compiler_params=pltpu.CompilerParams(vmem_limit_bytes=VMEM),
        cost_estimate=pl.CostEstimate(flops=10**9, bytes_accessed=10**6, transcendentals=0),
        name="proj_grads",
    )(*operands, *after)


def add_kernel(count, *refs):
    total = refs[0][...].astype(F32)
    for ref in refs[1:count]:
        total += ref[...].astype(F32)
    refs[-1][...] = total.astype(refs[-1].dtype)


def add_up(parts, dtype, after):
    shape = parts[0].shape
    rows = parts[0].size // shape[-1]
    flat = [x.reshape(rows, shape[-1]) for x in parts]
    block = rows // 2 if rows % 32 == 0 else rows
    spec = pl.BlockSpec((block, shape[-1]), lambda i: (i, 0))
    out = pl.pallas_call(
        ordered(functools.partial(add_kernel, len(parts)), len(parts), len(after)),
        grid=(rows // block,),
        in_specs=[spec] * len(parts) + [pl.BlockSpec(memory_space=pl.ANY)] * len(after),
        out_specs=spec,
        out_shape=jax.ShapeDtypeStruct((rows, shape[-1]), dtype),
        compiler_params=pltpu.CompilerParams(vmem_limit_bytes=SMALL),
        cost_estimate=pl.CostEstimate(flops=rows, bytes_accessed=10**6, transcendentals=0),
        name="add_up",
    )(*flat, *after)
    return out.reshape(shape)


def fold_kernel(m, count, at_ref, *refs):
    for step in range(m):
        total = refs[step * count][0, 0].astype(F32)
        for ref in refs[step * count + 1 : (step + 1) * count]:
            total += ref[0, 0].astype(F32)
        refs[m * count + step][0] = total.astype(BF)


def fold(at, arrays, after):
    two, m, rows, width = arrays[0].shape
    count = len(arrays)
    spec = lambda step: pl.BlockSpec(
        (1, 1, rows, width), lambda i, at: (i, jnp.bitwise_xor(at[2], step), 0, 0)
    )
    return pl.pallas_call(
        ordered(functools.partial(fold_kernel, m, count), m * count + 1, len(after)),
        grid_spec=pltpu.PrefetchScalarGridSpec(
            num_scalar_prefetch=1,
            grid=(2,),
            in_specs=[spec(step) for step in range(m) for x in arrays]
            + [pl.BlockSpec(memory_space=pl.ANY)] * len(after),
            out_specs=[pl.BlockSpec((1, rows, width), lambda i, at: (i, 0, 0))] * m,
        ),
        out_shape=[jax.ShapeDtypeStruct((2, rows, width), BF)] * m,
        compiler_params=pltpu.CompilerParams(vmem_limit_bytes=SMALL),
        cost_estimate=pl.CostEstimate(flops=rows, bytes_accessed=10**6, transcendentals=0),
        name="fold",
    )(at, *(list(arrays) * m), *after)


def join_kernel(count, at_ref, *refs):
    for e in range(2):
        total = refs[e * count][0].astype(F32)
        for ref in refs[e * count + 1 : (e + 1) * count]:
            total += ref[0].astype(F32)
        refs[2 * count + e][...] = total.astype(BF)


def join(at, arrays, after):
    two, rows, width = arrays[0].shape
    count = len(arrays)
    spec = lambda e: pl.BlockSpec(
        (1, rows, width), lambda i, at: (jnp.bitwise_xor(at[1], e), 0, 0)
    )
    return pl.pallas_call(
        ordered(functools.partial(join_kernel, count), 2 * count + 1, len(after)),
        grid_spec=pltpu.PrefetchScalarGridSpec(
            num_scalar_prefetch=1,
            grid=(1,),
            in_specs=[spec(e) for e in range(2) for x in arrays]
            + [pl.BlockSpec(memory_space=pl.ANY)] * len(after),
            out_specs=[pl.BlockSpec((rows, width), lambda i, at: (0, 0))] * 2,
        ),
        out_shape=[jax.ShapeDtypeStruct((rows, width), BF)] * 2,
        compiler_params=pltpu.CompilerParams(vmem_limit_bytes=SMALL),
        cost_estimate=pl.CostEstimate(flops=rows, bytes_accessed=10**6, transcendentals=0),
        name="join",
    )(at, *(list(arrays) * 2), *after)


GELU_A = 0.7978845608028654
GELU_B = 0.044715


def gelu_and_slope(v):
    square = v * v
    t = jnp.tanh(GELU_A * (v + GELU_B * (v * square)))
    half = 0.5 + 0.5 * t
    slope = half + 0.5 * v * (1.0 - t * t) * (GELU_A * (1.0 + 3.0 * GELU_B * square))
    return v * half, slope


def norm_forward(x):
    average = jnp.mean(x, axis=1, keepdims=True)
    centred = x - average
    inverse = lax.rsqrt(jnp.mean(centred * centred, axis=1, keepdims=True) + EPSILON)
    return centred * inverse, inverse


def norm_backward(grad, gain, unit, inverse):
    scaled = grad * gain
    pull = jnp.mean(scaled, axis=1, keepdims=True)
    twist = jnp.mean(scaled * unit, axis=1, keepdims=True)
    return inverse * (scaled - pull - unit * twist)


def dense_kernel(m, n, ws, pairs, at_ref, *refs):
    own_mixed, got_mixed = refs[:pairs], refs[pairs : 2 * pairs]
    x_ref, cot_ref = refs[2 * pairs : 2 * pairs + 2]
    pieces = refs[2 * pairs + 2 : 2 * pairs + 2 + 2 * m]
    rest = refs[2 * pairs + 2 + 2 * m :]
    result_ref, gr_ref, gm_own, gm_other, vec_ref, b1_ref = rest[:6]
    early_own, early_other, late_own, late_other = rest[6:10]
    w1, w2, wo, vp, slope, hidden, unit_bf, mixed, early, late, bias, sems, out_sems = rest[10:]
    k, low, c = at_ref[0], at_ref[1], at_ref[2]
    d = x_ref.shape[1]
    ff = w1.shape[1]
    parts = ff // d
    fs = parts * ws
    places = []
    for index, piece in enumerate(pieces):
        h = k if index < m else 1 - k
        for e in range(2):
            s = (2 * h + jnp.bitwise_xor(low, e)) * m + jnp.bitwise_xor(c, index % m)
            places.append((piece.at[e], s))
    kinds = 2 + parts + 1

    def load(i, kind, j=0):
        src, s = places[i]
        to = pl.ds(pl.multiple_of(s * ws, 16), ws)
        if kind == 0:
            pair = (src.at[pl.ds(parts * ws, ws), :], wo.at[to, :])
        elif kind == 1:
            pair = (src.at[pl.ds((2 * parts + 1) * ws, 16), :], vp.at[s])
        elif kind == 2:
            rows = pl.ds(pl.multiple_of(j * ws, 16), ws)
            pair = (src.at[rows, :], w1.at[to, pl.ds(pl.multiple_of(j * d, 128), d)])
        else:
            to = pl.ds(pl.multiple_of(s * fs, 16), fs)
            pair = (src.at[pl.ds((parts + 1) * ws, fs), :], w2.at[to, :])
        at = i * kinds + (kind if kind < 2 else 2 + j if kind == 2 else kinds - 1)
        return pltpu.make_async_copy(*pair, sems.at[at])

    count = len(places)
    for kind in (0, 1):
        for i in range(count):
            load(i, kind).start()
    for j in range(parts):
        for i in range(count):
            load(i, 2, j).start()
    for i in range(count):
        load(i, 3).start()

    for p in range(pairs):
        lanes = slice(128 * p, 128 * p + 128)
        other = slice(d // 2 + 128 * p, d // 2 + 128 * p + 128)

        @pl.when(k == 0)
        def low_core():
            mixed[:, lanes] = own_mixed[p][...]
            mixed[:, other] = got_mixed[p][...]

        @pl.when(k != 0)
        def high_core():
            mixed[:, lanes] = got_mixed[p][...]
            mixed[:, other] = own_mixed[p][...]

    for kind in (0, 1):
        for i in range(count):
            load(i, kind).wait()
    spot = lax.broadcasted_iota(jnp.int32, (128, d), 1)
    down = lax.broadcasted_iota(jnp.int32, (128, d), 0)
    vecs = jnp.zeros((16, d), F32)
    for s in range(n):
        place = jnp.where((spot == s * ws + down) & (down < ws), 1.0, 0.0).astype(BF)
        vecs += mm(vp[s, :, :128], place)
    per = (d // 2) // fs
    spot = lax.broadcasted_iota(jnp.int32, (256, d // 2), 1)
    down = lax.broadcasted_iota(jnp.int32, (256, d // 2), 0)
    place = [
        jnp.where((spot == t * fs + down) & (down < fs), 1.0, 0.0).astype(BF) for t in range(per)
    ]
    for q in range(n // per):
        row = sum(mm(vp[q * per + t, :, :256], place[t]) for t in range(per))
        bias[:, q * (d // 2) : (q + 1) * (d // 2)] = row[:8]
    outer_shift, gain_one, shift_one, gain_two, shift_two = [vecs[i : i + 1] for i in range(5)]

    residual = mm(mixed[...], wo[...]) + x_ref[...].astype(F32)
    unit_one, inverse_one = norm_forward(residual)
    normed = unit_one * gain_one + shift_one
    unit_bf[...] = normed.astype(BF)
    total = normed + outer_shift

    def wait_chunk(j):
        for i in range(count):
            load(i, 2, j).wait()

    for j in range(parts):
        wait_chunk(j)
    for j in range(parts):
        cols = slice(j * d, (j + 1) * d)
        value, slant = gelu_and_slope(mm(unit_bf[...], w1[:, cols]) + bias[5:6, cols])
        hidden[:, cols] = value.astype(BF)
        slope[:, cols] = slant
    for i in range(count):
        load(i, 3).wait()
    summed = total + mm(hidden[...], w2[...])
    unit_two, inverse_two = norm_forward(summed)
    result_ref[...] = (unit_two * gain_two + shift_two).astype(BF)
    cot = cot_ref[...].astype(F32)
    grad_summed = norm_backward(cot, gain_two, unit_two, inverse_two)
    row_sum = lambda x: jnp.sum(x, axis=0, keepdims=True)
    vec_ref[0:1, :] = row_sum(grad_summed)
    vec_ref[3:4, :] = row_sum(cot * unit_two)
    vec_ref[4:5, :] = row_sum(cot)
    grad_bf = grad_summed.astype(BF)
    grad_normed = grad_summed
    copies = []
    deep = early.shape[0] // 2
    split = ff // 2 // d

    def send(half, src, own, other):
        sem = out_sems.at[len(copies)]
        copies.append(pltpu.make_async_copy(src, own, sem))

        @pl.when(k == half)
        def keep():
            pltpu.make_async_copy(src, own, sem).start()

        @pl.when(k != half)
        def give():
            pltpu.make_async_copy(src, other, sem).start()

    def send_early(cols):
        for half in range(2):
            src = early.at[half * deep : (half + 1) * deep, cols]
            send(half, src, early_own.at[:, cols], early_other.at[:, cols])

    for j in range(parts):
        cols = slice(j * d, (j + 1) * d)
        grad_inner = mm(grad_bf, w2[cols, :], 1, 1) * slope[:, cols]
        b1_ref[0:1, cols] = row_sum(grad_inner)
        inner_bf = grad_inner.astype(BF)
        late[cols, :] = mm(hidden[:, cols], grad_bf, 0, 0).astype(BF)
        to = pl.ds((j % split) * d, d)
        send(j // split, late.at[cols, :], late_own.at[to, :], late_other.at[to, :])
        early[:, cols] = mm(unit_bf[...], inner_bf, 0, 0).astype(BF)
        send_early(cols)
        grad_normed += mm(inner_bf, w1[:, cols], 1, 1)
    vec_ref[1:2, :] = row_sum(grad_normed * unit_one)
    vec_ref[2:3, :] = row_sum(grad_normed)
    grad_residual = norm_backward(grad_normed, gain_one, unit_one, inverse_one)
    gr_ref[...] = grad_residual
    residual_bf = grad_residual.astype(BF)
    early[:, ff:] = mm(mixed[...], residual_bf, 0, 0).astype(BF)
    send_early(slice(ff, ff + d))
    grad_mixed = mm(residual_bf, wo[...], 1, 1).astype(BF)
    for half in range(2):
        part = grad_mixed[:, half * (d // 2) : (half + 1) * (d // 2)]

        @pl.when(k == half)
        def keep(part=part):
            gm_own[...] = part

        @pl.when(k != half)
        def give(part=part):
            gm_other[...] = part

    for copy in copies:
        copy.wait()


def dense(at, own_mixed, got_mixed, inputs, cots, mine, theirs, ws, ff):
    m = len(mine)
    pairs = len(own_mixed)
    rows, d = cots.shape
    n = d // ws
    parts = ff // d
    anywhere = pl.BlockSpec(memory_space=pl.ANY)
    half = lambda width: pl.BlockSpec((rows, width), lambda i, at: (at[0], 0))
    fixed = lambda *shape: pl.BlockSpec(shape, lambda i, at: (0,) * len(shape))
    return pl.pallas_call(
        functools.partial(dense_kernel, m, n, ws, pairs),
        grid_spec=pltpu.PrefetchScalarGridSpec(
            num_scalar_prefetch=1,
            grid=(1,),
            in_specs=[half(128)] * pairs
            + [fixed(rows, 128)] * pairs
            + [half(d), fixed(rows, d)]
            + [anywhere] * (2 * m),
            out_specs=[
                fixed(rows, d),
                fixed(rows, d),
                fixed(rows, d // 2),
                fixed(rows, d // 2),
                fixed(8, d),
                fixed(8, ff),
            ]
            + [anywhere] * 4,
            scratch_shapes=[
                pltpu.VMEM((d, ff), BF),
                pltpu.VMEM((ff, d), BF),
                pltpu.VMEM((d, d), BF),
                pltpu.VMEM((n, 16, d), BF),
                pltpu.VMEM((rows, ff), F32),
                pltpu.VMEM((rows, ff), BF),
                pltpu.VMEM((rows, d), BF),
                pltpu.VMEM((rows, d), BF),
                pltpu.VMEM((d, ff + d), BF),
                pltpu.VMEM((ff, d), BF),
                pltpu.VMEM((8, ff), F32),
                pltpu.SemaphoreType.DMA((4 * m * (3 + parts),)),
                pltpu.SemaphoreType.DMA((3 * parts + 2,)),
            ],
        ),
        out_shape=[
            jax.ShapeDtypeStruct((rows, d), BF),
            jax.ShapeDtypeStruct((rows, d), F32),
            jax.ShapeDtypeStruct((rows, d // 2), BF),
            jax.ShapeDtypeStruct((rows, d // 2), BF),
            jax.ShapeDtypeStruct((8, d), F32),
            jax.ShapeDtypeStruct((8, ff), F32),
            jax.ShapeDtypeStruct((d // 2, ff + d), BF),
            jax.ShapeDtypeStruct((d // 2, ff + d), BF),
            jax.ShapeDtypeStruct((ff // 2, d), BF),
            jax.ShapeDtypeStruct((ff // 2, d), BF),
        ],
        compiler_params=pltpu.CompilerParams(vmem_limit_bytes=VMEM),
        cost_estimate=pl.CostEstimate(flops=10**9, bytes_accessed=10**6, transcendentals=0),
        name="dense",
    )(at, *own_mixed, *got_mixed, inputs, cots, *mine, *theirs)


def dense_plain(at, own_mixed, got_mixed, inputs, cots, mine, theirs, ws, ff):
    rows, d = cots.shape
    n, fs = d // ws, ff * ws // d
    k = at[0]
    mine_half = lambda x: lax.dynamic_slice_in_dim(x, k * rows, rows, 0)
    inner_w, output_w, outer_w, vecs = assemble_late(at, mine, theirs, ws, ff // d)
    inner_w, output_w = inner_w.reshape(d, ff), output_w.reshape(d, d)
    outer_w = outer_w.reshape(ff, d)
    vecs = vecs.reshape(n, 16, d).astype(F32)
    inner_shift = vecs[:, 5, :fs].reshape(ff)
    vecs = vecs[:, :5, :ws].swapaxes(0, 1).reshape(5, d)
    outer_shift, gain_one, shift_one, gain_two, shift_two = [vecs[i] for i in range(5)]
    own = [mine_half(x) for x in own_mixed]
    mixed = jnp.where(
        k == 0,
        jnp.concatenate(own + got_mixed, axis=1),
        jnp.concatenate(got_mixed + own, axis=1),
    )
    residual = mm(mixed, output_w) + mine_half(inputs).astype(F32)
    unit_one, inverse_one = norm_forward(residual)
    normed = unit_one * gain_one + shift_one
    normed_bf = normed.astype(BF)
    value, slope = gelu_and_slope(mm(normed_bf, inner_w) + inner_shift)
    hidden = value.astype(BF)
    summed = mm(hidden, outer_w) + outer_shift + normed
    unit_two, inverse_two = norm_forward(summed)
    result = (unit_two * gain_two + shift_two).astype(BF)
    cot = cots.astype(F32)
    grad_summed = norm_backward(cot, gain_two, unit_two, inverse_two)
    grad_bf = grad_summed.astype(BF)
    grad_inner = mm(grad_bf, outer_w, 1, 1) * slope
    inner_bf = grad_inner.astype(BF)
    grad_normed = mm(inner_bf, inner_w, 1, 1) + grad_summed
    grad_residual = norm_backward(grad_normed, gain_one, unit_one, inverse_one)
    residual_bf = grad_residual.astype(BF)
    grad_mixed = mm(residual_bf, output_w, 1, 1).astype(BF)
    terms = [grad_summed, grad_normed * unit_one, grad_normed, cot * unit_two, cot]
    early = jnp.concatenate([mm(normed_bf, inner_bf, 0, 0), mm(mixed, residual_bf, 0, 0)], axis=1)

    def halves(x, axis):
        size = x.shape[axis] // 2
        return [lax.dynamic_slice_in_dim(x, i * size, size, axis).astype(BF) for i in (k, 1 - k)]

    return (
        result,
        grad_residual,
        *halves(grad_mixed, 1),
        jnp.stack([jnp.sum(x, axis=0) for x in terms]),
        jnp.sum(grad_inner, axis=0)[None],
        *halves(early, 0),
        *halves(mm(hidden, grad_bf, 0, 0), 0),
    )


def body(
    content_in,
    query_in,
    segment_ids,
    parent_ids,
    rank_order,
    query_flags,
    query_weight,
    key_weight,
    value_weight,
    relative_weight,
    output_weight,
    inner_weight,
    outer_weight,
    inner_bias,
    outer_bias,
    attend_gain,
    attend_shift,
    feed_gain,
    feed_shift,
    content_bias,
    position_bias,
    segment_bias,
    segment_table,
    content_cot,
    query_cot,
):
    n = lax.axis_size("shard")
    nr = lax.axis_size("rep")
    trees, r, d = content_in.shape
    groups = 2 * trees
    m = n // groups
    length = r * n
    nkb = length // KB
    ff = inner_weight.shape[1]
    dh = d // 2
    heads = dh // DH
    pairs = heads // 2
    ws = query_weight.shape[0]
    fs = outer_weight.shape[0]
    me = lax.axis_index("shard")
    g, c = me // m, me % m
    low = g % 2
    k = lax.axis_index("rep") % 2
    first = k == 0
    tie = lax.optimization_barrier

    def swap(x):
        return lax.ppermute(x, "rep", [(i, i ^ 1) for i in range(nr)])

    def far(x, step):
        return lax.ppermute(x, "shard", [(i, i ^ (m * step)) for i in range(n)])

    def near(x, step):
        return lax.ppermute(x, "shard", [(i, i ^ step) for i in range(n)])

    def across(x, e):
        moves = []
        for i in range(nr):
            for j in range(n):
                z = j // m
                to = (i - i % 2 + z // 2) * n + (2 * (i % 2) + (z % 2 ^ e)) * m + j % m
                moves.append((i * n + j, to))
        return lax.ppermute(x, ("rep", "shard"), moves)

    def pick(x, index, axis=0):
        return lax.dynamic_index_in_dim(x, index, axis, keepdims=False)

    def put(buffer, x, index, axis=0):
        return lax.dynamic_update_index_in_dim(buffer, x, index, axis)

    def pair_of(mine, other, index, axis=0):
        return put(jnp.stack([mine, mine], axis), other, 1 - index, axis)

    def cross(parts):
        got = [across(pick(parts, low ^ e), e) for e in range(2)]
        return pair_of(got[0], got[1], low)

    def near_gather(x, downward):
        bits = [b for b in range(m.bit_length() - 1)]
        held = {0: x}
        for b in bits[::-1] if downward else bits:
            held.update({o | 1 << b: near(y, 1 << b) for o, y in list(held.items())})
        return jnp.stack([held[o] for o in range(m)])

    def near_parts(x, axis):
        sent = [near(pick(x, c ^ step, axis), step) for step in range(1, m)]
        return [pick(x, c, axis)] + sent

    def far_sum(x):
        total = pick(x, g).astype(F32)
        for step in range(1, groups):
            total = total + far(pick(x, g ^ step), step).astype(F32)
        return total

    weights = [query_weight, key_weight, value_weight, relative_weight]
    low_array = low.astype(jnp.int32).reshape(1)
    vec_rows = [x.reshape(1, ws) for x in (content_bias, position_bias, segment_bias)]
    packed = pack(
        low_array,
        content_in,
        segment_ids,
        rank_order,
        query_flags,
        parent_ids,
        vec_rows + [segment_table],
        weights,
    )
    at = jnp.stack([k, low, c]).astype(jnp.int32)
    got = [across(packed[e], e) for e in range(2)]
    own_query = jnp.stack([across(pick(query_in, low ^ e), e) for e in range(2)])
    near_rows = [near_gather(got[e], e) for e in range(2)]
    their_rows = [swap(x) for x in near_rows]
    late_pack = pack_late(
        inner_weight,
        output_weight,
        outer_weight,
        [x.reshape(1, ws) for x in (outer_bias, attend_gain, attend_shift, feed_gain, feed_shift)]
        + [inner_bias.reshape(1, fs)],
    )
    late_pack, unused = tie((late_pack, got[1]))
    late = [across(late_pack, e) for e in range(2)]
    content_full, codes, wq, kv_weight, wr, inputs = assemble(
        at, near_rows, their_rows, own_query, swap(own_query), r, ws, []
    )
    content_full = content_full.reshape(length, d)
    wq, kv_weight, wr = wq.reshape(d, dh), kv_weight.reshape(d, d), wr.reshape(d, dh)
    inputs = inputs.reshape(groups * 2 * r, d)
    codes = codes.reshape(n, 16, d)
    key_ranks, hot, info, reach, live = masks(
        c.astype(jnp.int32).reshape(1), codes.reshape(n * 16, d), m, r
    )
    base = jnp.stack([c, m]).astype(jnp.int32)
    vectors = codes[:, 1:6, :ws].astype(F32).swapaxes(0, 1).reshape(5, 2, dh)
    head_vecs = jnp.where(first, vectors[:, 0], vectors[:, 1])


    content_cot, query_cot, unused = tie((content_cot, query_cot, content_full))
    cots = cross(jnp.stack([content_cot, query_cot], axis=1))

    position_bf, rel, rel_turned = relative(wr, length)
    queries = mm(inputs, wq)
    kv = mm(content_full, kv_weight).astype(BF)
    vec8 = jnp.pad(head_vecs, ((0, 3), (0, 0)))
    table = head_vecs[3:5].reshape(2, heads, DH).transpose(1, 2, 0)[..., None]
    table = jnp.where(jnp.arange(128) < 2 * NS, table, 0.0).astype(BF)
    table = jnp.tile(table.reshape(heads, DH, 256), (1, 2, 1))
    late = hold(late[0], late[1], [rel])
    late_near = [late] + [near(late, step) for step in range(1, m)]
    forward = []
    got_mixed = []
    for pair in range(pairs):
        after = [[late], [cots], late_near[1:]][min(pair, 2)]
        if pair == 2:
            *held, unused = tie((*late_near, forward[1][1]))
            late_theirs = [swap(x) for x in held]
        after = after + [f[1] for f in forward[-1:]]
        forward.append(
            attend_forward(
                pair,
                after,
                base,
                live,
                queries,
                vec8,
                table,
                info,
                reach,
                kv,
                hot,
                rel,
                key_ranks,
            )
        )
        got_mixed.append(swap(pick(forward[-1][3].reshape(2, groups * r, 128), 1 - k)))

    (
        result,
        grad_residual,
        mine_grad,
        other_grad,
        row_vecs,
        inner_vecs,
        early_mine,
        early_other,
        late_mine,
        late_other,
    ) = (dense if ws % 16 == 0 else dense_plain)(
        at,
        [f[3] for f in forward],
        got_mixed,
        inputs,
        cots.reshape(groups * r, d),
        late_near,
        late_theirs,
        ws,
        ff,
    )
    grad_heads = pair_of(mine_grad, swap(other_grad), k).reshape(groups * 2 * r, dh)

    backward = []

    def back(pair, after):
        f = forward[pair]
        after = after + [b[0] for b in backward[-1:]]
        backward.append(
            attend_backward(
                pair,
                after,
                base,
                live,
                f[0],
                queries,
                grad_heads,
                f[1],
                f[2],
                vec8,
                info,
                kv,
                hot,
                rel_turned,
            )
        )

    def near_fold(arrays, rows, after):
        parts = fold(at, [x.reshape(2, m, rows, x.shape[-1]) for x in arrays], after)
        return [parts[0]] + [near(parts[step], step) for step in range(1, m)]

    def cross_join(parts, after):
        return [across(x, e) for e, x in enumerate(join(at, parts, after))]

    def proj_some(some, extra, after):
        return proj_grads(
            inputs, content_full, position_bf, [backward[p] for p in some], extra, after
        ).reshape(groups, m, ws, -1)

    result = result.reshape(2, 2, r, d)
    outs_got = [across(pick(result, low ^ e), e) for e in range(2)]
    back(0, [])
    after = [backward[0][0]]
    late_parts = near_fold([late_mine, swap(late_other)], fs, after + outs_got)
    early_parts = near_fold([early_mine, swap(early_other)], ws, after)
    back(1, [early_parts[0], late_parts[0]])
    some_grads = proj_some(range(pairs - 1), [], [])
    some_parts = near_parts(some_grads, 1)
    late_cross = cross_join(late_parts, [some_grads])
    early_cross = cross_join(early_parts, [some_grads])
    back(2, [some_grads])

    small = jnp.concatenate([b[3][:5] for b in backward], axis=1)
    small = jnp.where(
        first,
        jnp.concatenate([small, jnp.zeros_like(small)], axis=1),
        jnp.concatenate([jnp.zeros_like(small), small], axis=1),
    )
    inner_vecs = inner_vecs[0].reshape(n, fs // ws, ws).swapaxes(1, 2).reshape(d, fs // ws)
    small = jnp.concatenate([small.T, row_vecs[:5].T, inner_vecs], axis=1)
    small = jnp.pad(small, ((0, 0), (0, 128 - small.shape[1]))).astype(BF)
    last_grads = proj_some([pairs - 1], [small], some_parts[1:] + late_cross + early_cross)
    early_sum = add_up(early_cross, BF, [last_grads])
    late_sum = add_up(late_cross, BF, [last_grads])
    early_got, late_got = swap(early_sum), swap(late_sum)
    *outs_got, unused = tie((*outs_got, last_grads))
    outs = pair_of(outs_got[0], outs_got[1], low)
    last_parts = near_parts(last_grads, 1)
    which = [jnp.asarray(x, jnp.int32).reshape(1) for x in (k, 1 - k)]
    dkv_parts = [b[1] for b in backward]
    dq_parts = [b[0] for b in backward]
    got_kv = swap(input_grad(which[1], dkv_parts, kv_weight, BF, [last_grads], True))
    got_q = swap(input_grad(which[1], dq_parts, wq, BF, [last_grads]))
    own_kv = input_grad(which[0], dkv_parts, kv_weight, F32, [last_grads], True)
    own_q = input_grad(which[0], dq_parts, wq, F32, [last_grads])
    content_parts = near_fold([own_kv, got_kv], r, [own_q, early_got, late_got] + last_parts[1:])
    q_sum = own_q + got_q.astype(F32) + grad_residual
    q_sum = q_sum.reshape(2, 2, r, d)
    query_rows, unused = tie((q_sum[:, 1].astype(BF), content_parts[1]))
    query_grads = cross(query_rows)
    late_total = late_sum.astype(F32) + late_got.astype(F32)
    content_sum = sum([x.astype(F32) for x in content_parts]) + q_sum[:, 0]
    content_grads = cross(content_sum.astype(BF))
    some_near, last_near = [
        add_up(parts, BF, content_parts[:1]) for parts in (some_parts, last_parts)
    ]
    proj_sum = far_sum(jnp.concatenate([some_near, last_near], axis=2))

    early_total = early_sum.astype(F32) + early_got.astype(F32)
    bit = 2
    while bit < nr:
        turn = [(i, i ^ bit) for i in range(nr)]
        early_total = early_total + lax.ppermute(early_total, "rep", turn)
        late_total = late_total + lax.ppermute(late_total, "rep", turn)
        proj_sum = proj_sum + lax.ppermute(proj_sum, "rep", turn)
        bit *= 2
    proj_other = swap(proj_sum)
    halves = jnp.where(first, proj_sum, proj_other), jnp.where(first, proj_other, proj_sum)

    def columns(index):
        return jnp.concatenate(
            [
                x[:, 512 * p + 128 * index : 512 * p + 128 * index + 128]
                for x in halves
                for p in range(pairs)
            ],
            axis=1,
        )

    head_cols = (proj_sum + proj_other)[:, 512 * pairs :]
    vec_cols = head_cols[:, 5:]
    return (
        outs[:, 0],
        outs[:, 1],
        content_grads,
        query_grads,
        columns(0),
        columns(1),
        columns(2),
        columns(3),
        early_total[:, ff : ff + d],
        early_total[:, :ff],
        late_total,
        vec_cols[:, 5 : 5 + fs // ws].T.reshape(fs),
        vec_cols[:, 0],
        vec_cols[:, 1],
        vec_cols[:, 2],
        vec_cols[:, 3],
        vec_cols[:, 4],
        head_cols[:, 0],
        head_cols[:, 1],
        head_cols[:, 2],
        head_cols[:, 3:5].T,
    )


def solution(mesh):
    in_specs = (
        P("rep", "shard", None),
        P("rep", "shard", None),
        P("rep", "shard"),
        P("rep", None),
        P("rep", "shard"),
        P("rep", "shard"),
        P("shard", None),
        P("shard", None),
        P("shard", None),
        P("shard", None),
        P("shard", None),
        P("shard", None),
        P("shard", None),
        P("shard"),
        P("shard"),
        P("shard"),
        P("shard"),
        P("shard"),
        P("shard"),
        P("shard"),
        P("shard"),
        P("shard"),
        P(None, "shard"),
        P("rep", "shard", None),
        P("rep", "shard", None),
    )
    out_specs = (
        P("rep", "shard", None),
        P("rep", "shard", None),
        P("rep", "shard", None),
        P("rep", "shard", None),
        P("shard", None),
        P("shard", None),
        P("shard", None),
        P("shard", None),
        P("shard", None),
        P("shard", None),
        P("shard", None),
        P("shard"),
        P("shard"),
        P("shard"),
        P("shard"),
        P("shard"),
        P("shard"),
        P("shard"),
        P("shard"),
        P("shard"),
        P(None, "shard"),
    )
    return jax.shard_map(body, mesh=mesh, in_specs=in_specs, out_specs=out_specs, check_vma=False)
```
